32 devices in a mesh: pipe: 8 (over z, core), seq: 4 (over y, x).
Axes of the slice: x: 2, y: 2, z: 4, core: 2. Of those that a mesh axis runs over, the one named last changes fastest.
Arguments:
- x_fwd: float32 [8, 512, 2048], P('pipe', 'seq'), may hold values from -12 to 12
- x_bwd: float32 [8, 512, 2048], P('pipe', 'seq'), may hold values from -12 to 12
- grad_in: float32 [8, 512, 2048], P('pipe', 'seq'), may hold values from -6 to 6
- gain: float32 [8, 2048], P('pipe'), may hold values from 0.25 to 1.75
- w_query: bfloat16 [8, 2048, 2048], P('pipe', None, 'seq'), may hold values from -2 to 2
- w_key: bfloat16 [8, 2048, 2048], P('pipe', None, 'seq'), may hold values from -2 to 2
- w_value: bfloat16 [8, 2048, 2048], P('pipe', None, 'seq'), may hold values from -0.125 to 0.125
- w_out: bfloat16 [8, 2048, 2048], P('pipe', None, 'seq'), may hold values from -0.125 to 0.125
Outputs:
- act_next: float32 [8, 512, 2048], P('pipe', 'seq')
- grad_prev: float32 [8, 512, 2048], P('pipe', 'seq')
The draws below stay inside these ranges and needn't reach their ends.
All inputs are finite; a program needn't handle non-finite values.
Results may differ from the reference program's by a relative error of at most 0.012.
The reference program's roundings to bfloat16 on the way count: a program that leaves them out, or rounds other values in their place, can miss the bound.
Values may be sent and summed in bfloat16 or wider, within the bound.
No kernel may reach another device: no remote copies, remote signals or barrier semaphores. Data moves between devices by JAX's collectives and lax.ppermute only.
A program may use at most 192 MiB of HBM per device.

```python
import math
import jax
import jax.numpy as jnp
from jax import lax

D = 2048
H = 16
HD = 128
HH = 2048
L = 512
SECTIONS = 8


def query_base(key):
    base = jax.random.normal(jax.random.fold_in(key, 101), (SECTIONS, D, HH), jnp.float32)
    return jnp.clip(base, -6.0, 6.0) / math.sqrt(D)


def draw_w_query(key, part):
    return jnp.clip(3.0 * query_base(key), -2.0, 2.0).astype(jnp.bfloat16)


def draw_w_key(key, part):
    noise = jnp.clip(jax.random.normal(jax.random.fold_in(key, 102), (SECTIONS, D, HH), jnp.float32), -6.0, 6.0) / math.sqrt(D)
    values = noise
    return jnp.clip(values, -2.0, 2.0).astype(jnp.bfloat16)


def activation_draw(key, salt):
    source = jax.random.fold_in(key, salt)
    values = 0.5 * jnp.clip(jax.random.normal(jax.random.fold_in(source, 5), (SECTIONS, L, D), jnp.float32), -6.0, 6.0)
    return jnp.clip(values, -12.0, 12.0)


def draw_x_fwd(key, part):
    return activation_draw(key, 21)


def draw_x_bwd(key, part):
    return activation_draw(key, 22)


def shard_levels(stream_key, dims, split, low, top_value):
    factor_of = 1.0
    for dim, blocks in split:
        heights = jax.random.uniform(jax.random.fold_in(jax.random.fold_in(stream_key, 6), dim), (blocks,), jnp.float32, low / len(split), top_value / len(split))
        factor_of = factor_of * jnp.repeat(jnp.exp(heights), dims[dim] // blocks).reshape((-1,) + (1,) * (len(dims) - 1 - dim))
    return factor_of


def bell_draw(own_key, dims, spread, reach, shards=(), dtype=jnp.bfloat16):
    result = spread * jax.random.normal(own_key, dims, jnp.float32)
    if shards:
        result = result * shard_levels(own_key, dims, shards, -0.22, 0.18)
    return jnp.clip(result, -reach, reach).astype(dtype)


def setup_inputs(seed: int = 0) -> dict:
    seeds = jax.random.split(jax.random.key(seed), 9)
    x_fwd = draw_x_fwd(jax.random.fold_in(seeds[8], 71), 0)
    x_bwd = draw_x_bwd(jax.random.fold_in(seeds[8], 71), 0)
    grad_in = bell_draw(seeds[2], (SECTIONS, L, D), 1.0, 6.0, ((0, 8), (1, 4)), jnp.float32)
    gain = jnp.clip(1.0 + 0.15 * jax.random.normal(seeds[3], (SECTIONS, D), jnp.float32), 0.25, 1.75)
    w_query = draw_w_query(jax.random.fold_in(seeds[8], 71), 0)
    w_key = draw_w_key(jax.random.fold_in(seeds[8], 71), 0)
    w_value = bell_draw(seeds[6], (SECTIONS, D, HH), D ** -0.5, 0.125, ((0, 8), (2, 4)))
    w_out = bell_draw(seeds[7], (SECTIONS, D, HH), HH ** -0.5, 0.125, ((0, 8), (2, 4)))
    return {"x_fwd": x_fwd, "x_bwd": x_bwd, "grad_in": grad_in, "gain": gain, "w_query": w_query, "w_key": w_key, "w_value": w_value, "w_out": w_out}


def rope_tables(positions):
    half_dim = HD // 2
    inverse = 10000.0 ** (-(jnp.arange(half_dim).astype(jnp.float32) * 2.0 / HD))
    angles = positions.astype(jnp.float32)[:, None] * inverse[None, :]
    return (jnp.cos(angles)[:, None, :], jnp.sin(angles)[:, None, :])

def rotate(values, cosine, sine_table):
    shaped = values.reshape(values.shape[0], -1, HD)
    first_half = shaped[..., :HD // 2]
    second_half = shaped[..., HD // 2:]
    output = jnp.concatenate([first_half * cosine - second_half * sine_table, second_half * cosine + first_half * sine_table], -1)
    return output.reshape(values.shape)

def rotate_back(values, cosine, sine_table):
    shaped = values.reshape(values.shape[0], -1, HD)
    first_half = shaped[..., :HD // 2]
    second_half = shaped[..., HD // 2:]
    output = jnp.concatenate([first_half * cosine + second_half * sine_table, second_half * cosine - first_half * sine_table], -1)
    return output.reshape(values.shape)

def normalize(inputs, gain_row):
    inv_rms = lax.rsqrt(lax.optimization_barrier(jnp.mean(inputs * inputs, -1, keepdims=True)) + 1e-05)
    return ((inputs * inv_rms * gain_row).astype(jnp.bfloat16), inv_rms)

def times_t(left, right):
    return lax.dot_general(left, right, (((1,), (1,)), ((), ())), preferred_element_type=jnp.float32)

def per_head(values):
    return values.reshape(values.shape[0], H, HD).transpose(1, 0, 2)

def join_heads(values):
    return values.transpose(1, 0, 2).reshape(values.shape[1], H * HD)

def attend(query, key_rows, value_rows):
    score_scale = HD ** (-0.5)

    def one_head(operands):
        query_h, key_h, value_h = operands
        scores = jnp.dot(query_h, key_h.T, preferred_element_type=jnp.float32) * score_scale
        probs = jax.nn.softmax(scores, axis=-1)
        return jnp.dot(probs.astype(jnp.bfloat16), value_h, preferred_element_type=jnp.float32).astype(jnp.bfloat16)
    return join_heads(lax.map(one_head, (per_head(query), per_head(key_rows), per_head(value_rows))))

def attend_back(query, key_rows, value_rows, grad_out):
    score_scale = HD ** (-0.5)

    def one_head(operands):
        query_h, key_h, value_h, grad_h = operands
        scores = jnp.dot(query_h, key_h.T, preferred_element_type=jnp.float32) * score_scale
        probs = jax.nn.softmax(scores, axis=-1)
        value_grad = jnp.dot(probs.astype(jnp.bfloat16).T, grad_h, preferred_element_type=jnp.float32).astype(jnp.bfloat16)
        prob_grad = jnp.dot(grad_h, value_h.T, preferred_element_type=jnp.float32)
        row_delta = lax.optimization_barrier(jnp.sum(probs * prob_grad, -1, keepdims=True))
        score_grad = (probs * (prob_grad - row_delta) * score_scale).astype(jnp.bfloat16)
        query_grad = jnp.dot(score_grad, key_h, preferred_element_type=jnp.float32)
        key_grad = jnp.dot(score_grad.T, query_h, preferred_element_type=jnp.float32)
        return (query_grad, key_grad, value_grad)
    query_grad, key_grad, value_grad = lax.map(one_head, (per_head(query), per_head(key_rows), per_head(value_rows), per_head(grad_out)))
    return (join_heads(query_grad), join_heads(key_grad), join_heads(value_grad))

def section(operands):
    act_in, saved_in, grad, gain_row, query_w, key_w, value_w, out_w = operands
    length = act_in.shape[0]
    cosine, sine_table = rope_tables(jnp.arange(length).astype(jnp.int32))

    def project(normed):
        query = rotate(jnp.dot(normed, query_w, preferred_element_type=jnp.float32), cosine, sine_table).astype(jnp.bfloat16)
        key_rows = rotate(jnp.dot(normed, key_w, preferred_element_type=jnp.float32), cosine, sine_table).astype(jnp.bfloat16)
        value_rows = jnp.dot(normed, value_w, preferred_element_type=jnp.float32).astype(jnp.bfloat16)
        return (query, key_rows, value_rows)
    normed_fwd, inv_fwd = normalize(act_in, gain_row)
    normed_bwd, inv_bwd = normalize(saved_in, gain_row)
    attn = attend(*project(normed_fwd))
    act_out = act_in + times_t(attn, out_w)
    d_attn = jnp.dot(grad.astype(jnp.bfloat16), out_w, preferred_element_type=jnp.float32).astype(jnp.bfloat16)
    query_b, key_b, value_b = project(normed_bwd)
    query_grad, key_grad, value_grad = attend_back(query_b, key_b, value_b, d_attn)
    query_grad = rotate_back(query_grad, cosine, sine_table).astype(jnp.bfloat16)
    key_grad = rotate_back(key_grad, cosine, sine_table).astype(jnp.bfloat16)
    d_normed = times_t(query_grad, query_w) + times_t(key_grad, key_w) + times_t(value_grad, value_w)
    gain_grad = d_normed * gain_row
    d_input = inv_bwd * gain_grad - saved_in * inv_bwd * inv_bwd * inv_bwd * lax.optimization_barrier(jnp.mean(saved_in * gain_grad, -1, keepdims=True))
    return (act_out, grad + d_input)

def reference(x_fwd, x_bwd, grad_in, gain, w_query, w_key, w_value, w_out):
    act_out, d_input = lax.map(section, (x_fwd, x_bwd, grad_in, gain, w_query, w_key, w_value, w_out))
    return (jnp.roll(act_out, 1, axis=0), jnp.roll(d_input, -1, axis=0))
```

```python
import jax
import jax.numpy as jnp
from jax import lax
from jax.sharding import PartitionSpec as P

HD = 128


def bits_of(number):
    return [bit for bit in range(number.bit_length()) if (number >> bit) & 1]


def by_distance(count):
    return sorted(range(1, count), key=lambda rel: (len(bits_of(rel)), rel))


def across(value, bit):
    count = lax.axis_size("seq")
    return lax.ppermute(value, "seq", [(i, i ^ (1 << bit)) for i in range(count)])


def column_part(value, part, parts):
    unit = 128
    tiles = value.shape[-1] // unit
    low = tiles * part // parts * unit
    high = tiles * (part + 1) // parts * unit
    return value[:, low:high]


def gather_blocks(own):
    blocks = {0: own}
    for rel in by_distance(lax.axis_size("seq")):
        bits = bits_of(rel)
        parts = [
            across(column_part(blocks[rel ^ (1 << bit)], i, len(bits)), bit)
            for i, bit in enumerate(bits)
        ]
        blocks[rel] = parts[0] if len(parts) == 1 else jnp.concatenate(parts, 1)
    return jnp.concatenate([blocks[rel] for rel in range(len(blocks))], 0)


def scatter_blocks(term_fn):
    count = lax.axis_size("seq")
    arrived = {rel: [] for rel in range(count)}

    def total_of(rel):
        total = term_fn(rel)
        for pieces in arrived[rel]:
            total = total + pieces
        return total

    for rel in reversed(by_distance(count)):
        bits = bits_of(rel)
        sent = total_of(rel).astype(jnp.bfloat16)
        for i, bit in enumerate(bits):
            piece = across(column_part(sent, i, len(bits)), bit).astype(jnp.float32)
            width = sent.shape[-1]
            before = sum(column_part(sent, j, len(bits)).shape[-1] for j in range(i))
            after = width - before - piece.shape[-1]
            arrived[rel ^ (1 << bit)].append(jnp.pad(piece, ((0, 0), (before, after))))
    return total_of(0)


def passed_along(value, axis, steps):
    count = lax.axis_size(axis)
    pairs = [(source, (source + steps) % count) for source in range(count)]
    return lax.ppermute(value, axis, pairs)


def rope_tables(positions):
    half_dim = HD // 2
    inverse = 10000.0 ** (-(jnp.arange(half_dim).astype(jnp.float32) * 2.0 / HD))
    angles = positions.astype(jnp.float32)[:, None] * inverse[None, :]
    return (jnp.cos(angles)[:, None, :], jnp.sin(angles)[:, None, :])


def rotate(values, cosine, sine_table):
    shaped = values.reshape(values.shape[0], -1, HD)
    first_half = shaped[..., : HD // 2]
    second_half = shaped[..., HD // 2 :]
    output = jnp.concatenate(
        [
            first_half * cosine - second_half * sine_table,
            second_half * cosine + first_half * sine_table,
        ],
        -1,
    )
    return output.reshape(values.shape)


def normalize(inputs, gain_row):
    inv_rms = lax.rsqrt(jnp.mean(inputs * inputs, -1, keepdims=True) + 1e-05)
    return ((inputs * inv_rms * gain_row).astype(jnp.bfloat16), inv_rms)


def times_t(left, right):
    return lax.dot_general(
        left, right, (((1,), (1,)), ((), ())), preferred_element_type=jnp.float32
    )


def split_heads(values):
    return values.reshape(values.shape[0], -1, HD)


def softmax_of(query_heads, key_heads):
    scores = (
        jnp.einsum("qhd,khd->hqk", query_heads, key_heads, preferred_element_type=jnp.float32)
        * HD ** (-0.5)
    )
    return jax.nn.softmax(scores, axis=-1)


def attend(query, key_rows, value_rows):
    probs = softmax_of(split_heads(query), split_heads(key_rows))
    output = jnp.einsum(
        "hqk,khd->qhd",
        probs.astype(jnp.bfloat16),
        split_heads(value_rows),
        preferred_element_type=jnp.float32,
    )
    return output.astype(jnp.bfloat16).reshape(query.shape)


def attend_back(query, key_rows, value_rows, grad_out, cosine, sine_table):
    query_heads, key_heads = split_heads(query), split_heads(key_rows)
    value_heads, grad_heads = split_heads(value_rows), split_heads(grad_out)
    probs = softmax_of(query_heads, key_heads)
    value_grad = jnp.einsum(
        "hqk,qhd->khd", probs.astype(jnp.bfloat16), grad_heads, preferred_element_type=jnp.float32
    )
    prob_grad = jnp.einsum(
        "qhd,khd->hqk", grad_heads, value_heads, preferred_element_type=jnp.float32
    )
    row_delta = jnp.sum(probs * prob_grad, -1, keepdims=True)
    score_grad = (probs * (prob_grad - row_delta) * HD ** (-0.5)).astype(jnp.bfloat16)
    query_grad = jnp.einsum(
        "hqk,khd->qhd", score_grad, key_heads, preferred_element_type=jnp.float32
    )
    key_grad = jnp.einsum(
        "hqk,qhd->khd", score_grad, query_heads, preferred_element_type=jnp.float32
    )
    return (
        rotate(query_grad.reshape(query.shape), cosine, -sine_table).astype(jnp.bfloat16),
        rotate(key_grad.reshape(query.shape), cosine, -sine_table).astype(jnp.bfloat16),
        value_grad.reshape(query.shape).astype(jnp.bfloat16),
    )


def shards(x_fwd, x_bwd, grad_in, gain, w_query, w_key, w_value, w_out):
    act_in = x_fwd[0]
    saved_in = x_bwd[0]
    grad = grad_in[0]
    gain_row = gain[0]
    local_rows = act_in.shape[0]
    count = lax.axis_size("seq")
    own_query, own_key, own_value, own_out = w_query[0], w_key[0], w_value[0], w_out[0]

    normed_bwd, inv_bwd = normalize(saved_in, gain_row)
    all_bwd = gather_blocks(normed_bwd)
    all_grad = gather_blocks(grad.astype(jnp.bfloat16))
    normed_fwd, _ = normalize(act_in, gain_row)
    all_fwd = gather_blocks(normed_fwd)

    block_of = lax.axis_index("seq") ^ jnp.arange(count)
    positions = (block_of[:, None] * local_rows + jnp.arange(local_rows)[None, :]).reshape(-1)
    cosine, sine_table = rope_tables(positions)

    def project(rows):
        query = rotate(
            jnp.dot(rows, own_query, preferred_element_type=jnp.float32), cosine, sine_table
        ).astype(jnp.bfloat16)
        key_rows = rotate(
            jnp.dot(rows, own_key, preferred_element_type=jnp.float32), cosine, sine_table
        ).astype(jnp.bfloat16)
        value_rows = jnp.dot(rows, own_value, preferred_element_type=jnp.float32).astype(
            jnp.bfloat16
        )
        return query, key_rows, value_rows

    def rows_of(values, rel):
        return values[rel * local_rows : (rel + 1) * local_rows]

    query_b, key_b, value_b = project(all_bwd)
    attn_grad = jnp.dot(all_grad, own_out, preferred_element_type=jnp.float32).astype(jnp.bfloat16)
    query_grad, key_grad, value_grad = attend_back(
        query_b, key_b, value_b, attn_grad, cosine, sine_table
    )

    def grad_term(rel):
        total = times_t(rows_of(query_grad, rel), own_query)
        total = total + times_t(rows_of(key_grad, rel), own_key)
        return total + times_t(rows_of(value_grad, rel), own_value)

    d_normed = scatter_blocks(grad_term)

    attn = attend(*project(all_fwd))
    branch = scatter_blocks(lambda rel: times_t(rows_of(attn, rel), own_out))

    gain_grad = d_normed * gain_row
    d_input = inv_bwd * gain_grad - saved_in * inv_bwd * inv_bwd * inv_bwd * jnp.mean(
        saved_in * gain_grad, -1, keepdims=True
    )
    sent_backward = passed_along((grad + d_input).astype(jnp.bfloat16), "pipe", -1).astype(
        jnp.float32
    )
    act_out = act_in + branch
    sent_forward = passed_along(act_out.astype(jnp.bfloat16), "pipe", 1).astype(act_out.dtype)
    return (sent_forward[None], sent_backward[None])


def solution(mesh):
    placed = (
        P("pipe", "seq", None),
        P("pipe", "seq", None),
        P("pipe", "seq", None),
        P("pipe", None),
        P("pipe", None, "seq"),
        P("pipe", None, "seq"),
        P("pipe", None, "seq"),
        P("pipe", None, "seq"),
    )
    return jax.shard_map(
        shards,
        mesh=mesh,
        in_specs=placed,
        out_specs=(P("pipe", "seq", None), P("pipe", "seq", None)),
        check_vma=False,
    )
```

```python
import functools
import math

import jax
import jax.numpy as jnp
from jax import lax
from jax.experimental import pallas as pl
from jax.experimental.pallas import tpu as pltpu
from jax.sharding import PartitionSpec as P

HD = 128
LANES = 128
CHUNK = 256
EXP2_SCALE = HD ** (-0.5) * math.log2(math.e)
NT = (((1,), (1,)), ((), ()))
TN = (((0,), (0,)), ((), ()))
VMEM_LIMIT = 50 * 1024 * 1024


def bits_of(number):
    return [bit for bit in range(number.bit_length()) if (number >> bit) & 1]


def by_distance(count):
    return sorted(range(1, count), key=lambda rel: (len(bits_of(rel)), rel))


def part_bounds(width, count):
    parts = max(count.bit_length() - 1, 1)
    tiles = width // LANES
    return [(tiles * i // parts * LANES, tiles * (i + 1) // parts * LANES) for i in range(parts)]


def last_bit(rel, part):
    bits = bits_of(rel)
    return bits[part % len(bits)]


def across(value, bit):
    count = lax.axis_size("seq")
    return lax.ppermute(value, "seq", [(i, i ^ (1 << bit)) for i in range(count)])


def across_and_on(value, flip):
    count, sections = lax.axis_size("seq"), lax.axis_size("pipe")
    pairs = [
        (p * count + i, (p + 1) % sections * count + (i ^ flip))
        for p in range(sections)
        for i in range(count)
    ]
    return lax.ppermute(value, ("pipe", "seq"), pairs)


def passed_along(value, axis, steps):
    count = lax.axis_size(axis)
    pairs = [(source, (source + steps) % count) for source in range(count)]
    return lax.ppermute(value, axis, pairs)


def gather_blocks(own_parts):
    count = lax.axis_size("seq")
    blocks = {(0, part): value for part, value in enumerate(own_parts)}
    for rel in by_distance(count):
        for part in range(len(own_parts)):
            bit = last_bit(rel, part)
            blocks[rel, part] = across(blocks[rel ^ (1 << bit), part], bit)
    return blocks


def summed_on_the_way(count, parts):
    return {
        (rel ^ (1 << last_bit(rel, part)), part)
        for rel in range(1, count)
        for part in range(parts)
        if len(bits_of(rel)) > 1
    }


def scatter_blocks(terms, send_last):
    count = lax.axis_size("seq")
    arrived, final = {}, {}
    for rel in reversed(by_distance(count)):
        for part in sorted({key[1] for key in terms}):
            total = terms[rel, part]
            for piece in arrived.get((rel, part), []):
                total = total + piece.astype(jnp.float32)
            bit = last_bit(rel, part)
            target = rel ^ (1 << bit)
            if target:
                piece = across(total.astype(jnp.bfloat16), bit)
                arrived.setdefault((target, part), []).append(piece)
            else:
                final[rel, part] = send_last(total.astype(jnp.bfloat16), bit)
    return final


def call(kernel, out_shapes, operands, in_specs, scratch=(), flops=0, name=None):
    moved = sum(math.prod(x.shape) * x.dtype.itemsize for x in list(operands) + list(out_shapes))
    return pl.pallas_call(
        kernel,
        out_shape=out_shapes,
        in_specs=in_specs,
        out_specs=[pl.BlockSpec(memory_space=pltpu.VMEM)] * len(out_shapes),
        scratch_shapes=list(scratch),
        compiler_params=pltpu.CompilerParams(vmem_limit_bytes=VMEM_LIMIT),
        cost_estimate=pl.CostEstimate(flops=int(flops), bytes_accessed=int(moved), transcendentals=0),
        name=name,
    )(*operands)


ANY = pl.BlockSpec(memory_space=pl.ANY)
VMEM = pl.BlockSpec(memory_space=pltpu.VMEM)


def norm_parts(inputs, gain, count, after=()):
    rows, width = inputs.shape
    bounds = part_bounds(width, count)

    def kernel(x_ref, gain_ref, *refs):
        refs = refs[len(after) :]
        x = x_ref[...]
        inv = lax.rsqrt(jnp.mean(x * x, -1, keepdims=True) + 1e-05)
        for ref, (low, high) in zip(refs, bounds):
            ref[...] = (x_ref[:, low:high] * inv * gain_ref[:, low:high]).astype(jnp.bfloat16)
        refs[-1][...] = inv

    outs = [jax.ShapeDtypeStruct((rows, high - low), jnp.bfloat16) for low, high in bounds]
    outs.append(jax.ShapeDtypeStruct((rows, 1), jnp.float32))
    *parts, inv = call(
        kernel, outs, (inputs, gain, *after), [VMEM, VMEM] + [ANY] * len(after), name="norm"
    )
    return parts, inv


def cast_parts(inputs, count, after=()):
    rows, width = inputs.shape
    bounds = part_bounds(width, count)

    def kernel(x_ref, *refs):
        for ref, (low, high) in zip(refs[len(after) :], bounds):
            ref[...] = x_ref[:, low:high].astype(jnp.bfloat16)

    outs = [jax.ShapeDtypeStruct((rows, high - low), jnp.bfloat16) for low, high in bounds]
    return call(kernel, outs, (inputs, *after), [VMEM] + [ANY] * len(after), name="cast")


def block_copies(block_refs, keys, rows, bounds, all_rows, sems):
    return [
        pltpu.make_async_copy(
            ref,
            all_rows.at[pl.ds(rel * rows, rows), pl.ds(bounds[part][0], ref.shape[1])],
            sems.at[i],
        )
        for i, (ref, (rel, part)) in enumerate(zip(block_refs, keys))
    ]


def turned(values, cosine, sine):
    return values * cosine + pltpu.roll(values, HD // 2, 1) * sine


def project_into(rows_ref, weight_ref, out_ref, cos_ref=None, sin_ref=None):
    features = out_ref.shape[1]
    for low in range(0, features, CHUNK):
        high = min(low + CHUNK, features)
        values = jnp.dot(
            rows_ref[...], weight_ref[:, low:high], preferred_element_type=jnp.float32
        )
        for head in range(0, high - low, HD):
            piece = values[:, head : head + HD]
            if cos_ref is not None:
                piece = turned(piece, cos_ref[...], sin_ref[...])
            out_ref[:, low + head : low + head + HD] = piece.astype(jnp.bfloat16)


def project(blocks, weights, cosine, sine, rows, bounds):
    keys = sorted(blocks)
    length, width = cosine.shape[0], bounds[-1][1]
    features = weights[0].shape[1]
    n = len(keys)

    def kernel(*refs):
        block_refs, weight_refs = refs[:n], refs[n : n + 3]
        cos_ref, sin_ref = refs[n + 3 : n + 5]
        outs = refs[n + 5 : n + 8]
        all_rows, held, sems = refs[n + 8 :]
        copies = block_copies(block_refs, keys, rows, bounds, all_rows, sems)
        loads = [
            pltpu.make_async_copy(weight_refs[i], held.at[i], sems.at[n + i]) for i in range(3)
        ]
        for copy in copies + loads:
            copy.start()
        for copy in copies:
            copy.wait()
        for i in range(3):
            loads[i].wait()
            tables = (cos_ref, sin_ref) if i < 2 else ()
            project_into(all_rows, held.at[i], outs[i], *tables)

    return call(
        kernel,
        [jax.ShapeDtypeStruct((length, features), jnp.bfloat16)] * 3,
        [blocks[key] for key in keys] + list(weights) + [cosine, sine],
        [ANY] * (n + 3) + [VMEM, VMEM],
        [
            pltpu.VMEM((length, width), jnp.bfloat16),
            pltpu.VMEM((3, width, features), jnp.bfloat16),
            pltpu.SemaphoreType.DMA((n + 3,)),
        ],
        flops=6 * length * width * features,
        name="project",
    )


def term_outs(rows, bounds, count):
    later = summed_on_the_way(count, len(bounds))
    keys = [(rel, part) for rel in reversed(by_distance(count)) for part in range(len(bounds))]
    shapes = [
        jax.ShapeDtypeStruct(
            (rows, bounds[part][1] - bounds[part][0]),
            jnp.float32 if (rel, part) in later else jnp.bfloat16,
        )
        for rel, part in keys
    ]
    return keys, shapes


def store_terms(values, low, refs, keys, rows, bounds):
    high = low + values.shape[1]
    for ref, (rel, part) in zip(refs, keys):
        first, last = bounds[part]
        start, stop = max(first, low), min(last, high)
        if start < stop:
            piece = values[rel * rows : (rel + 1) * rows, start - low : stop - low]
            ref[:, start - first : stop - first] = piece.astype(ref.dtype)


def backward_terms(blocks, qkv, weights, cosine, sine, rows, bounds, count):
    in_keys = sorted(blocks)
    length, width = cosine.shape[0], bounds[-1][1]
    features = qkv[0].shape[1]
    n = len(in_keys)
    keys, shapes = term_outs(rows, bounds, count)
    step = min(length, 512)

    def kernel(*refs):
        block_refs, weight_refs = refs[:n], refs[n : n + 4]
        q_ref, k_ref, v_ref, cos_ref, sin_ref = refs[n + 4 : n + 9]
        own_ref = refs[n + 9]
        outs = refs[n + 10 : n + 10 + len(keys)]
        all_rows, held, d_attn, d_qkv, sems = refs[n + 10 + len(keys) :]
        copies = block_copies(block_refs, in_keys, rows, bounds, all_rows, sems)
        loads = [
            pltpu.make_async_copy(weight_refs[i], held.at[i], sems.at[n + i]) for i in range(4)
        ]
        for copy in copies + loads:
            copy.start()
        for copy in copies:
            copy.wait()
        loads[0].wait()
        project_into(all_rows, held.at[0], d_attn)

        for head in range(features // HD):
            cols = slice(head * HD, (head + 1) * HD)
            key, value = k_ref[:, cols], v_ref[:, cols]
            d_key, d_value = 0.0, 0.0
            for low in range(0, length, step):
                part = slice(low, low + step)
                query, grad = q_ref[part, cols], d_attn[part, cols]
                scores = lax.dot_general(key, query, NT, preferred_element_type=jnp.float32)
                top = jnp.max(scores, 0, keepdims=True)
                raised = jnp.exp2((scores - top) * EXP2_SCALE)
                probs = raised * (1.0 / jnp.sum(raised, 0, keepdims=True))
                d_value += jnp.dot(
                    probs.astype(jnp.bfloat16), grad, preferred_element_type=jnp.float32
                )
                d_probs = lax.dot_general(value, grad, NT, preferred_element_type=jnp.float32)
                delta = jnp.sum(probs * d_probs, 0, keepdims=True)
                d_scores = (probs * (d_probs - delta) * HD ** (-0.5)).astype(jnp.bfloat16)
                d_key += jnp.dot(d_scores, query, preferred_element_type=jnp.float32)
                d_query = lax.dot_general(
                    key, d_scores, TN, preferred_element_type=jnp.float32
                ).T
                d_qkv[0, part, cols] = turned(
                    d_query, cos_ref[part, :], -sin_ref[part, :]
                ).astype(jnp.bfloat16)
            d_qkv[1, :, cols] = turned(d_key, cos_ref[...], -sin_ref[...]).astype(jnp.bfloat16)
            d_qkv[2, :, cols] = d_value.astype(jnp.bfloat16)

        for i in range(1, 4):
            loads[i].wait()
        for low in range(0, width, CHUNK):
            total = 0.0
            for i in range(3):
                total += lax.dot_general(
                    d_qkv[i],
                    held[i + 1, low : low + CHUNK, :],
                    NT,
                    preferred_element_type=jnp.float32,
                )
            own_ref[:, low : low + CHUNK] = total[:rows]
            store_terms(total, low, outs, keys, rows, bounds)

    own, *terms = call(
        kernel,
        [jax.ShapeDtypeStruct((rows, width), jnp.float32)] + shapes,
        [blocks[key] for key in in_keys] + list(weights) + list(qkv) + [cosine, sine],
        [ANY] * (n + 4) + [VMEM] * 5,
        [
            pltpu.VMEM((length, width), jnp.bfloat16),
            pltpu.VMEM((4, width, features), jnp.bfloat16),
            pltpu.VMEM((length, features), jnp.bfloat16),
            pltpu.VMEM((3, length, features), jnp.bfloat16),
            pltpu.SemaphoreType.DMA((n + 4,)),
        ],
        flops=8 * length * width * features + 10 * length * length * features,
        name="backward",
    )
    return own, dict(zip(keys, terms))


def forward_terms(blocks, act_in, weights, cosine, sine, rows, bounds, count):
    in_keys = sorted(blocks)
    length, width = cosine.shape[0], bounds[-1][1]
    features = weights[0].shape[1]
    n = len(in_keys)
    keys, shapes = term_outs(rows, bounds, count)
    step = min(length, 512)

    def kernel(*refs):
        block_refs, weight_refs = refs[:n], refs[n : n + 4]
        act_ref, cos_ref, sin_ref = refs[n + 4 : n + 7]
        own_ref = refs[n + 7]
        outs = refs[n + 8 : n + 8 + len(keys)]
        all_rows, held, qkv, attn, sems = refs[n + 8 + len(keys) :]
        copies = block_copies(block_refs, in_keys, rows, bounds, all_rows, sems)
        loads = [
            pltpu.make_async_copy(weight_refs[i], held.at[i], sems.at[n + i]) for i in range(4)
        ]
        for copy in copies + loads:
            copy.start()
        for copy in copies:
            copy.wait()
        for i in range(3):
            loads[i].wait()
            tables = (cos_ref, sin_ref) if i < 2 else ()
            project_into(all_rows, held.at[i], qkv.at[i], *tables)

        for head in range(features // HD):
            cols = slice(head * HD, (head + 1) * HD)
            for low in range(0, length, step):
                part = slice(low, low + step)
                scores = lax.dot_general(
                    qkv[0, part, cols], qkv[1, :, cols], NT, preferred_element_type=jnp.float32
                )
                top = jnp.max(scores, 1, keepdims=True)
                raised = jnp.exp2((scores - top) * EXP2_SCALE)
                total = jnp.sum(raised, 1, keepdims=True)
                mixed = jnp.dot(
                    raised.astype(jnp.bfloat16), qkv[2, :, cols], preferred_element_type=jnp.float32
                )
                attn[part, cols] = (mixed * (1.0 / total)).astype(jnp.bfloat16)

        loads[3].wait()
        for low in range(0, width, CHUNK):
            total = lax.dot_general(
                attn[...], held[3, low : low + CHUNK, :], NT, preferred_element_type=jnp.float32
            )
            own = total[:rows] + act_ref[:, low : low + CHUNK]
            own_ref[:, low : low + CHUNK] = own.astype(jnp.bfloat16)
            store_terms(total, low, outs, keys, rows, bounds)

    own, *terms = call(
        kernel,
        [jax.ShapeDtypeStruct((rows, width), jnp.bfloat16)] + shapes,
        [blocks[key] for key in in_keys] + list(weights) + [act_in, cosine, sine],
        [ANY] * (n + 4) + [VMEM] * 3,
        [
            pltpu.VMEM((length, width), jnp.bfloat16),
            pltpu.VMEM((4, width, features), jnp.bfloat16),
            pltpu.VMEM((3, length, features), jnp.bfloat16),
            pltpu.VMEM((length, features), jnp.bfloat16),
            pltpu.SemaphoreType.DMA((n + 4,)),
        ],
        flops=8 * length * width * features + 4 * length * length * features,
        name="forward",
    )
    return own, dict(zip(keys, terms))


def input_grad(own, pieces, saved, grad, inv, gain, bounds):
    keys = sorted(pieces)

    def kernel(own_ref, saved_ref, grad_ref, inv_ref, gain_ref, *refs):
        out_ref, scaled = refs[len(keys) :]
        inv_rows = inv_ref[...]
        product = 0.0
        for part, (low, high) in enumerate(bounds):
            total = own_ref[:, low:high]
            for ref, key in zip(refs, keys):
                if key[1] == part:
                    total = total + ref[...].astype(jnp.float32)
            total = total * gain_ref[:, low:high]
            scaled[:, low:high] = total
            product += jnp.sum(saved_ref[:, low:high] * total, -1, keepdims=True)
        mean = product / own_ref.shape[1]
        factor = inv_rows * inv_rows * inv_rows * mean
        out_ref[...] = (
            grad_ref[...] + inv_rows * scaled[...] - saved_ref[...] * factor
        ).astype(jnp.bfloat16)

    return call(
        kernel,
        [jax.ShapeDtypeStruct(own.shape, jnp.bfloat16)],
        [own, saved, grad, inv, gain] + [pieces[key] for key in keys],
        [VMEM] * (5 + len(keys)),
        [pltpu.VMEM(own.shape, jnp.float32)],
        name="input_grad",
    )[0]


def activation_sum(own, pieces, bounds):
    keys = sorted(pieces)

    def kernel(own_ref, *refs):
        out_ref = refs[len(keys)]
        for part, (low, high) in enumerate(bounds):
            total = own_ref[:, low:high].astype(jnp.float32)
            for ref, key in zip(refs, keys):
                if key[1] == part:
                    total = total + ref[...].astype(jnp.float32)
            out_ref[0, :, low:high] = total

    return call(
        kernel,
        [jax.ShapeDtypeStruct((1, *own.shape), jnp.float32)],
        [own] + [pieces[key] for key in keys],
        [VMEM] * (1 + len(keys)),
        name="activation_sum",
    )[0]


def rope_tables(positions):
    half_dim = HD // 2
    inverse = 10000.0 ** (-(jnp.arange(half_dim).astype(jnp.float32) * 2.0 / HD))
    angles = positions.astype(jnp.float32)[:, None] * inverse[None, :]
    cosine, sine = jnp.cos(angles), jnp.sin(angles)
    return jnp.concatenate([cosine, cosine], 1), jnp.concatenate([-sine, sine], 1)


def shards(x_fwd, x_bwd, grad_in, gain, w_query, w_key, w_value, w_out):
    act_in, saved_in, grad = x_fwd[0], x_bwd[0], grad_in[0]
    rows, width = act_in.shape
    count = lax.axis_size("seq")
    bounds = part_bounds(width, count)
    own_query, own_key, own_value, own_out = w_query[0], w_key[0], w_value[0], w_out[0]

    block_of = lax.axis_index("seq") ^ jnp.arange(count)
    positions = (block_of[:, None] * rows + jnp.arange(rows)[None, :]).reshape(-1)
    cosine, sine = rope_tables(positions)

    def first_arrivals(blocks):
        return [blocks[1 << last_bit(count - 1, part), part] for part in range(len(bounds))]

    parts_bwd, inv_bwd = norm_parts(saved_in, gain, count)
    all_bwd = gather_blocks(parts_bwd)
    all_grad = gather_blocks(cast_parts(grad, count, first_arrivals(all_bwd)))
    parts_fwd, _ = norm_parts(act_in, gain, count, first_arrivals(all_grad))
    all_fwd = gather_blocks(parts_fwd)

    qkv = project(all_bwd, (own_query, own_key, own_value), cosine, sine, rows, bounds)
    d_own, d_terms = backward_terms(
        all_grad, qkv, (own_out, own_query, own_key, own_value), cosine, sine, rows, bounds, count
    )
    d_pieces = scatter_blocks(d_terms, across)

    own, terms = forward_terms(
        all_fwd, act_in, (own_query, own_key, own_value, own_out), cosine, sine, rows, bounds, count
    )
    own = across_and_on(own, 0)
    pieces = scatter_blocks(terms, lambda value, bit: across_and_on(value, 1 << bit))

    d_input = input_grad(d_own, d_pieces, saved_in, grad, inv_bwd, gain, bounds)
    sent_backward = passed_along(d_input, "pipe", -1).astype(jnp.float32)
    return (activation_sum(own, pieces, bounds), sent_backward[None])


def solution(mesh):
    placed = (
        P("pipe", "seq", None),
        P("pipe", "seq", None),
        P("pipe", "seq", None),
        P("pipe", None),
        P("pipe", None, "seq"),
        P("pipe", None, "seq"),
        P("pipe", None, "seq"),
        P("pipe", None, "seq"),
    )
    return jax.shard_map(
        shards,
        mesh=mesh,
        in_specs=placed,
        out_specs=(P("pipe", "seq", None), P("pipe", "seq", None)),
        check_vma=False,
    )
```

```python
import functools
import math

import jax
import jax.numpy as jnp
from jax import lax
from jax.experimental import pallas as pl
from jax.experimental.pallas import tpu as pltpu
from jax.sharding import PartitionSpec as P

HD = 128
LANES = 128
CHUNK = 256
EXP2_SCALE = HD ** (-0.5) * math.log2(math.e)
NT = (((1,), (1,)), ((), ()))
TN = (((0,), (0,)), ((), ()))
HEADS_WEIGHT = 8_000_000_000
TERMS_WEIGHT = 3_000_000_000
INPUT_GRAD_WEIGHT = 8_000_000_000
LAST_SUM_WEIGHT = 8_000_000_000
VMEM_LIMIT = 50 * 1024 * 1024


def bits_of(number):
    return [bit for bit in range(number.bit_length()) if (number >> bit) & 1]


def by_distance(count):
    return sorted(range(1, count), key=lambda rel: (len(bits_of(rel)), rel))


def part_bounds(rows, count):
    parts = 2 if count > 2 else 1
    return [(rows * i // parts, rows * (i + 1) // parts) for i in range(parts)]


def last_bit(rel, part):
    bits = bits_of(rel)
    return bits[part % len(bits)]


def ways_to(rel, bounds):
    ways = {}
    for part, (low, high) in enumerate(bounds):
        bit = last_bit(rel, part)
        ways[bit] = (min(low, ways.get(bit, (low, high))[0]), high)
    return [(bit, low, high) for bit, (low, high) in ways.items()]


def across(value, bit):
    count = lax.axis_size("seq")
    return lax.ppermute(value, "seq", [(i, i ^ (1 << bit)) for i in range(count)])


def across_and_on(value, flip):
    count, sections = lax.axis_size("seq"), lax.axis_size("pipe")
    pairs = [
        (p * count + i, (p + 1) % sections * count + (i ^ flip))
        for p in range(sections)
        for i in range(count)
    ]
    return lax.ppermute(value, ("pipe", "seq"), pairs)


def passed_along(value, axis, steps):
    count = lax.axis_size(axis)
    pairs = [(source, (source + steps) % count) for source in range(count)]
    return lax.ppermute(value, axis, pairs)


def onward_rows(count, bounds):
    return [
        (rel ^ (1 << bit), bit, low, high)
        for rel in by_distance(count)
        for bit, low, high in ways_to(rel, bounds)
    ]


def gather_first(own, what):
    count = lax.axis_size("seq")
    blocks = {(0, 0): own}
    for rel in by_distance(count):
        if len(bits_of(rel)) == 1:
            with jax.named_scope(f"gather_{what}_block{rel}"):
                blocks[rel, 0] = across(own, bits_of(rel)[0])
    return blocks


def second_hops(blocks, rows):
    count = lax.axis_size("seq")
    return [
        (blocks[rel, 0], low, high)
        for rel, bit, low, high in onward_rows(count, part_bounds(rows, count))
        if len(bits_of(rel)) == 1
    ]


def gather_rest(blocks, picked, what):
    count = lax.axis_size("seq")
    rows = blocks[0, 0].shape[0]
    picked = list(picked)
    for rel, bit, low, high in onward_rows(count, part_bounds(rows, count)):
        if rel == 0:
            continue
        value = picked.pop(0) if len(bits_of(rel)) == 1 else blocks[rel, low]
        if value.shape[0] > high - low:
            value = value[: high - low]
        with jax.named_scope(f"gather_{what}_block{rel ^ (1 << bit)}_row{low}"):
            blocks[rel ^ (1 << bit), low] = across(value, bit)
    return blocks


def messages_of(rows, count):
    bounds = part_bounds(rows, count)
    parts = range(len(bounds))
    later = {
        (rel ^ (1 << last_bit(rel, part)), part)
        for rel in range(1, count)
        for part in parts
        if len(bits_of(rel)) > 1
    }
    keys = [(rel, part) for rel in reversed(by_distance(count)) for part in parts]
    groups = {}
    for key in keys:
        if key not in later:
            groups.setdefault(last_bit(*key), []).append(key)
    return list(groups.values()), [key for key in keys if key in later]


def scatter_blocks(own, terms, rows, send_last, what, after=(), close=False):
    count = lax.axis_size("seq")
    bounds = part_bounds(rows, count)
    groups, later = messages_of(rows, count)
    arrived, near, last, sums = {}, {}, {}, []

    def send(value, keys):
        bit = last_bit(*keys[0])
        targets = [(rel ^ (1 << bit), part) for rel, part in keys]
        onward = any(rel for rel, _ in targets)
        with jax.named_scope(f"scatter_{what}_block{keys[0][0]}_part{keys[0][1]}"):
            moved = (across if onward else send_last)(value, bit)
        first = 0
        for key, target in zip(keys, targets):
            if target[0]:
                arrived.setdefault(target, []).append((moved, first))
            else:
                (near if onward else last)[key] = (moved, first)
            first += bounds[key[1]][1] - bounds[key[1]][0]

    for value, keys in zip(terms, groups):
        send(value, keys)
    values = dict(zip(later, terms[len(groups) :]))
    for level in sorted({len(bits_of(rel)) for rel, _ in later}, reverse=True):
        keys = [key for key in later if len(bits_of(key[0])) == level]
        totals = [(values[key], [(0, *piece) for piece in arrived[key]]) for key in keys]
        if close and level == 1:
            totals.append((own, [(bounds[key[1]][0], *near[key]) for key in sorted(near)]))
        results = sum_rows(totals, bounds, after)
        if close and level == 1:
            own = results[-1]
        sums += results[: len(keys)]
        for key, value in zip(keys, results):
            send(value, [key])
    if not close:
        last.update(near)
    elif not later:
        own = own.astype(jnp.bfloat16)
    return own, last, sums


def call(kernel, out_shapes, operands, in_specs, scratch=(), flops=1, name=None):
    return pl.pallas_call(
        kernel,
        out_shape=out_shapes,
        in_specs=in_specs,
        out_specs=[pl.BlockSpec(memory_space=pltpu.VMEM)] * len(out_shapes),
        scratch_shapes=list(scratch),
        compiler_params=pltpu.CompilerParams(vmem_limit_bytes=VMEM_LIMIT),
        cost_estimate=pl.CostEstimate(flops=int(flops), bytes_accessed=1, transcendentals=0),
        name=name,
    )(*operands)


ANY = pl.BlockSpec(memory_space=pl.ANY)
VMEM = pl.BlockSpec(memory_space=pltpu.VMEM)


def picked_shapes(pieces):
    return [
        jax.ShapeDtypeStruct((high - low, value.shape[1]), value.dtype)
        for value, low, high in pieces
    ]


def pick(pieces, in_refs, out_refs):
    for (_, low, high), in_ref, out_ref in zip(pieces, in_refs, out_refs):
        out_ref[...] = in_ref[low:high, :]


def normed_rows(inputs, gain, pieces=(), after=()):
    rows, width = inputs.shape
    n = len(pieces)

    def kernel(x_ref, gain_ref, *refs):
        refs = refs[:n] + refs[n + len(after) :]
        out_ref, inv_ref = refs[n : n + 2]
        x = x_ref[...]
        inv = lax.rsqrt(jnp.mean(x * x, -1, keepdims=True) + 1e-05)
        out_ref[...] = (x * inv * gain_ref[...]).astype(jnp.bfloat16)
        inv_ref[...] = inv
        pick(pieces, refs[:n], refs[n + 2 :])

    return call(
        kernel,
        [
            jax.ShapeDtypeStruct((rows, width), jnp.bfloat16),
            jax.ShapeDtypeStruct((rows, 1), jnp.float32),
        ]
        + picked_shapes(pieces),
        [inputs, gain] + [value for value, _, _ in pieces] + list(after),
        [VMEM] * (2 + n) + [ANY] * len(after),
        name="norm",
    )


def picked_rows(pieces, after=()):
    n = len(pieces)

    def kernel(*refs):
        pick(pieces, refs[:n], refs[n + len(after) :])

    return call(
        kernel,
        picked_shapes(pieces),
        [value for value, _, _ in pieces] + list(after),
        [VMEM] * n + [ANY] * len(after),
        name="pick",
    )


def cast_rows(inputs, after=()):
    def kernel(x_ref, *refs):
        refs[len(after)][...] = x_ref[...].astype(jnp.bfloat16)

    return call(
        kernel,
        [jax.ShapeDtypeStruct(inputs.shape, jnp.bfloat16)],
        (inputs, *after),
        [VMEM] + [ANY] * len(after),
        name="cast",
    )[0]


def sum_rows(totals, bounds, after=()):
    height = bounds[0][1] - bounds[0][0]
    pieces = [piece for _, pieces in totals for piece in pieces]
    n, m = len(totals), len(pieces)

    def kernel(*refs):
        terms, arrivals, outs = refs[:n], list(refs[n : n + m]), refs[-n:]
        for (term, moved), term_ref, out_ref in zip(totals, terms, outs):
            found = [(row, first, arrivals.pop(0)) for row, _, first in moved]
            for low in range(0, term.shape[0], height):
                total = term_ref[low : low + height, :]
                for row, first, ref in found:
                    if row == low:
                        total = total + ref[first : first + height, :].astype(jnp.float32)
                out_ref[low : low + height, :] = total.astype(jnp.bfloat16)

    return call(
        kernel,
        [jax.ShapeDtypeStruct(term.shape, jnp.bfloat16) for term, _ in totals],
        [term for term, _ in totals] + [value for _, value, _ in pieces] + list(after),
        [VMEM] * (n + m) + [ANY] * len(after),
        name="sum_rows",
    )


def block_copies(block_refs, keys, rows, all_rows, sems):
    return [
        pltpu.make_async_copy(
            ref, all_rows.at[pl.ds(rel * rows + low, ref.shape[0]), :], sems.at[i]
        )
        for i, (ref, (rel, low)) in enumerate(zip(block_refs, keys))
    ]


def turned(values, cosine, sine):
    return values * cosine + pltpu.roll(values, HD // 2, 1) * sine


def project_into(rows_ref, weight_ref, out_ref, cos_ref=None, sin_ref=None):
    features = out_ref.shape[1]
    for low in range(0, features, CHUNK):
        high = min(low + CHUNK, features)
        values = jnp.dot(
            rows_ref[...], weight_ref[:, low:high], preferred_element_type=jnp.float32
        )
        for head in range(0, high - low, HD):
            piece = values[:, head : head + HD]
            if cos_ref is not None:
                piece = turned(piece, cos_ref[...], sin_ref[...])
            out_ref[:, low + head : low + head + HD] = piece.astype(jnp.bfloat16)


def project(blocks, weights, cosine, sine, rows):
    keys = sorted(blocks)
    length, width = cosine.shape[0], blocks[0, 0].shape[1]
    features = weights[0].shape[1]
    n = len(keys)

    def kernel(*refs):
        block_refs, weight_refs = refs[:n], refs[n : n + 3]
        cos_ref, sin_ref = refs[n + 3 : n + 5]
        outs = refs[n + 5 : n + 8]
        all_rows, held, sems = refs[n + 8 :]
        copies = block_copies(block_refs, keys, rows, all_rows, sems)
        loads = [
            pltpu.make_async_copy(weight_refs[i], held.at[i], sems.at[n + i]) for i in range(3)
        ]
        for copy in copies + loads:
            copy.start()
        for copy in copies:
            copy.wait()
        for i in range(3):
            loads[i].wait()
            tables = (cos_ref, sin_ref) if i < 2 else ()
            project_into(all_rows, held.at[i], outs[i], *tables)

    return call(
        kernel,
        [jax.ShapeDtypeStruct((length, features), jnp.bfloat16)] * 3,
        [blocks[key] for key in keys] + list(weights) + [cosine, sine],
        [ANY] * (n + 3) + [VMEM, VMEM],
        [
            pltpu.VMEM((length, width), jnp.bfloat16),
            pltpu.VMEM((3, width, features), jnp.bfloat16),
            pltpu.SemaphoreType.DMA((n + 3,)),
        ],
        name="project",
    )


def term_outs(rows, width, count):
    bounds = part_bounds(rows, count)
    groups, later = messages_of(rows, count)

    def shape(keys, dtype):
        height = sum(bounds[part][1] - bounds[part][0] for _, part in keys)
        return jax.ShapeDtypeStruct((height, width), dtype)

    return [shape(keys, jnp.bfloat16) for keys in groups] + [
        shape([key], jnp.float32) for key in later
    ]


def store_terms(values, low, refs, rows, count):
    bounds = part_bounds(rows, count)
    groups, later = messages_of(rows, count)
    for ref, keys in zip(refs, groups + [[key] for key in later]):
        at = 0
        for rel, part in keys:
            first, last = bounds[part]
            piece = values[rel * rows + first : rel * rows + last]
            ref[at : at + last - first, low : low + values.shape[1]] = piece.astype(ref.dtype)
            at += last - first


def backward_heads(blocks, qkv, weight, cosine, sine, rows):
    in_keys = sorted(blocks)
    length, width = cosine.shape[0], blocks[0, 0].shape[1]
    features = qkv[0].shape[1]
    n = len(in_keys)
    step = min(length, 512)

    def kernel(*refs):
        block_refs, weight_ref = refs[:n], refs[n]
        q_ref, k_ref, v_ref, cos_ref, sin_ref = refs[n + 1 : n + 6]
        d_qkv = refs[n + 6 : n + 9]
        all_rows, held, d_attn, sems = refs[n + 9 :]
        copies = block_copies(block_refs, in_keys, rows, all_rows, sems)
        copies.append(pltpu.make_async_copy(weight_ref, held, sems.at[n]))
        for copy in copies:
            copy.start()
        for copy in copies:
            copy.wait()
        project_into(all_rows, held, d_attn)

        for head in range(features // HD):
            cols = slice(head * HD, (head + 1) * HD)
            key, value = k_ref[:, cols], v_ref[:, cols]
            d_key, d_value = 0.0, 0.0
            for low in range(0, length, step):
                part = slice(low, low + step)
                query, grad = q_ref[part, cols], d_attn[part, cols]
                scores = lax.dot_general(key, query, NT, preferred_element_type=jnp.float32)
                top = jnp.max(scores, 0, keepdims=True)
                raised = jnp.exp2((scores - top) * EXP2_SCALE)
                probs = raised * (1.0 / jnp.sum(raised, 0, keepdims=True))
                d_value += jnp.dot(
                    probs.astype(jnp.bfloat16), grad, preferred_element_type=jnp.float32
                )
                d_probs = lax.dot_general(value, grad, NT, preferred_element_type=jnp.float32)
                delta = jnp.sum(probs * d_probs, 0, keepdims=True)
                d_scores = (probs * (d_probs - delta) * HD ** (-0.5)).astype(jnp.bfloat16)
                d_key += jnp.dot(d_scores, query, preferred_element_type=jnp.float32)
                d_query = lax.dot_general(
                    key, d_scores, TN, preferred_element_type=jnp.float32
                ).T
                d_qkv[0][part, cols] = turned(
                    d_query, cos_ref[part, :], -sin_ref[part, :]
                ).astype(jnp.bfloat16)
            d_qkv[1][:, cols] = turned(d_key, cos_ref[...], -sin_ref[...]).astype(jnp.bfloat16)
            d_qkv[2][:, cols] = d_value.astype(jnp.bfloat16)

    return call(
        kernel,
        [jax.ShapeDtypeStruct((length, features), jnp.bfloat16)] * 3,
        [blocks[key] for key in in_keys] + [weight] + list(qkv) + [cosine, sine],
        [ANY] * (n + 1) + [VMEM] * 5,
        [
            pltpu.VMEM((length, width), jnp.bfloat16),
            pltpu.VMEM((width, features), jnp.bfloat16),
            pltpu.VMEM((length, features), jnp.bfloat16),
            pltpu.SemaphoreType.DMA((n + 1,)),
        ],
        flops=HEADS_WEIGHT,
        name="backward_heads",
    )


def backward_terms(d_qkv, weights, rows, count, after=()):
    length, features = d_qkv[0].shape
    width = weights[0].shape[0]
    shapes = term_outs(rows, width, count)

    def kernel(*refs):
        grads, weight_refs = refs[:3], refs[3:6]
        own_ref, *outs = refs[6 + len(after) : -2]
        held, sems = refs[-2:]
        loads = [pltpu.make_async_copy(weight_refs[i], held.at[i], sems.at[i]) for i in range(3)]
        for load in loads:
            load.start()
        for load in loads:
            load.wait()
        for low in range(0, width, CHUNK):
            total = 0.0
            for i in range(3):
                total += lax.dot_general(
                    grads[i][...],
                    held[i, low : low + CHUNK, :],
                    NT,
                    preferred_element_type=jnp.float32,
                )
            own_ref[:, low : low + CHUNK] = total[:rows]
            store_terms(total, low, outs, rows, count)

    own, *terms = call(
        kernel,
        [jax.ShapeDtypeStruct((rows, width), jnp.float32)] + shapes,
        list(d_qkv) + list(weights) + list(after),
        [VMEM] * 3 + [ANY] * (3 + len(after)),
        [pltpu.VMEM((3, width, features), jnp.bfloat16), pltpu.SemaphoreType.DMA((3,))],
        flops=TERMS_WEIGHT,
        name="backward_terms",
    )
    return own, terms


def forward_terms(qkv, act_in, weight, rows, count, after=()):
    length, features = qkv[0].shape
    width = weight.shape[0]
    shapes = term_outs(rows, width, count)
    step = min(length, 512)

    def kernel(*refs):
        q_ref, k_ref, v_ref, act_ref, weight_ref = refs[:5]
        own_ref, *outs = refs[5 + len(after) : -3]
        held, attn, sem = refs[-3:]
        load = pltpu.make_async_copy(weight_ref, held, sem)
        load.start()
        for head in range(features // HD):
            cols = slice(head * HD, (head + 1) * HD)
            for low in range(0, length, step):
                part = slice(low, low + step)
                scores = lax.dot_general(
                    q_ref[part, cols], k_ref[:, cols], NT, preferred_element_type=jnp.float32
                )
                top = jnp.max(scores, 1, keepdims=True)
                raised = jnp.exp2((scores - top) * EXP2_SCALE)
                total = jnp.sum(raised, 1, keepdims=True)
                mixed = jnp.dot(
                    raised.astype(jnp.bfloat16), v_ref[:, cols], preferred_element_type=jnp.float32
                )
                attn[part, cols] = (mixed * (1.0 / total)).astype(jnp.bfloat16)

        load.wait()
        for low in range(0, width, CHUNK):
            total = lax.dot_general(
                attn[...], held[low : low + CHUNK, :], NT, preferred_element_type=jnp.float32
            )
            own_ref[:, low : low + CHUNK] = total[:rows] + act_ref[:, low : low + CHUNK]
            store_terms(total, low, outs, rows, count)

    own, *terms = call(
        kernel,
        [jax.ShapeDtypeStruct((rows, width), jnp.float32)] + shapes,
        list(qkv) + [act_in, weight, *after],
        [VMEM] * 4 + [ANY] * (1 + len(after)),
        [
            pltpu.VMEM((width, features), jnp.bfloat16),
            pltpu.VMEM((length, features), jnp.bfloat16),
            pltpu.SemaphoreType.DMA,
        ],
        name="forward_terms",
    )
    return own, terms


def input_grad(own, pieces, saved, grad, inv, gain, bounds, after=()):
    keys = sorted(pieces)

    def kernel(own_ref, saved_ref, grad_ref, inv_ref, gain_ref, *refs):
        out_ref = refs[-1]
        for part, (low, high) in enumerate(bounds):
            total = own_ref[low:high, :]
            for ref, key in zip(refs, keys):
                if key[1] == part:
                    first = pieces[key][1]
                    total = total + ref[first : first + high - low, :].astype(jnp.float32)
            total = total * gain_ref[...]
            saved_rows = saved_ref[low:high, :]
            mean = jnp.mean(saved_rows * total, -1, keepdims=True)
            inv_rows = inv_ref[low:high, :]
            out_ref[low:high, :] = (
                grad_ref[low:high, :]
                + inv_rows * total
                - saved_rows * (inv_rows * inv_rows * inv_rows * mean)
            ).astype(jnp.bfloat16)

    return call(
        kernel,
        [jax.ShapeDtypeStruct(own.shape, jnp.bfloat16)],
        [own, saved, grad, inv, gain] + [pieces[key][0] for key in keys] + list(after),
        [VMEM] * (5 + len(keys)) + [ANY] * len(after),
        flops=INPUT_GRAD_WEIGHT,
        name="input_grad",
    )[0]


def activation_sum(own, pieces, bounds):
    keys = sorted(pieces)

    def kernel(own_ref, *refs):
        out_ref = refs[len(keys)]
        for part, (low, high) in enumerate(bounds):
            total = own_ref[low:high, :].astype(jnp.float32)
            for ref, key in zip(refs, keys):
                if key[1] == part:
                    first = pieces[key][1]
                    total = total + ref[first : first + high - low, :].astype(jnp.float32)
            out_ref[0, low:high, :] = total

    return call(
        kernel,
        [jax.ShapeDtypeStruct((1, *own.shape), jnp.float32)],
        [own] + [pieces[key][0] for key in keys],
        [VMEM] * (1 + len(keys)),
        flops=LAST_SUM_WEIGHT,
        name="activation_sum",
    )[0]


def widened(values, after=()):
    def kernel(in_ref, *refs):
        refs[len(after)][0] = in_ref[...].astype(jnp.float32)

    return call(
        kernel,
        [jax.ShapeDtypeStruct((1, *values.shape), jnp.float32)],
        (values, *after),
        [VMEM] + [ANY] * len(after),
        name="widen",
    )[0]


def rope_tables(positions):
    half_dim = HD // 2
    inverse = 10000.0 ** (-(jnp.arange(half_dim).astype(jnp.float32) * 2.0 / HD))
    angles = positions.astype(jnp.float32)[:, None] * inverse[None, :]
    cosine, sine = jnp.cos(angles), jnp.sin(angles)
    return jnp.concatenate([cosine, cosine], 1), jnp.concatenate([-sine, sine], 1)


def shards(x_fwd, x_bwd, grad_in, gain, w_query, w_key, w_value, w_out):
    act_in, saved_in, grad = x_fwd[0], x_bwd[0], grad_in[0]
    rows = act_in.shape[0]
    count = lax.axis_size("seq")
    bounds = part_bounds(rows, count)
    own_query, own_key, own_value, own_out = w_query[0], w_key[0], w_value[0], w_out[0]

    block_of = lax.axis_index("seq") ^ jnp.arange(count)
    positions = (block_of[:, None] * rows + jnp.arange(rows)[None, :]).reshape(-1)
    cosine, sine = rope_tables(positions)

    def last_arrivals(blocks):
        return [value for (rel, _), value in blocks.items() if rel == count - 1]

    projections = (own_query, own_key, own_value)
    normed_bwd, inv_bwd = normed_rows(saved_in, gain)
    grad_low = cast_rows(grad, [normed_bwd])
    all_bwd = gather_first(normed_bwd, "saved")
    all_grad = gather_first(grad_low, "grad")
    picked = picked_rows(second_hops(all_bwd, rows), [grad_low])
    all_bwd = gather_rest(all_bwd, picked, "saved")
    picked = picked_rows(second_hops(all_grad, rows), picked)
    all_grad = gather_rest(all_grad, picked, "grad")
    normed_fwd, _ = normed_rows(act_in, gain, after=picked)
    all_fwd = gather_first(normed_fwd, "input")

    qkv = project(all_bwd, projections, cosine, sine, rows)
    d_qkv = backward_heads(all_grad, qkv, own_out, cosine, sine, rows)
    picked = picked_rows(second_hops(all_fwd, rows), d_qkv[:1])
    all_fwd = gather_rest(all_fwd, picked, "input")
    d_own, d_terms = backward_terms(d_qkv, projections, rows, count, picked)
    qkv = project(all_fwd, projections, cosine, sine, rows)
    own, terms = forward_terms(qkv, act_in, own_out, rows, count)

    d_own, d_pieces, d_sums = scatter_blocks(d_own, d_terms, rows, across, "grad", [own])
    own, pieces, sums = scatter_blocks(
        own,
        terms,
        rows,
        lambda value, bit: across_and_on(value, 1 << bit),
        "branch",
        d_sums,
        close=True,
    )
    own = across_and_on(own, 0)
    d_input = input_grad(d_own, d_pieces, saved_in, grad, inv_bwd, gain, bounds, sums)
    act_next = activation_sum(own, pieces, bounds)
    return (act_next, widened(passed_along(d_input, "pipe", -1), [act_next]))


def solution(mesh):
    placed = (
        P("pipe", "seq", None),
        P("pipe", "seq", None),
        P("pipe", "seq", None),
        P("pipe", None),
        P("pipe", None, "seq"),
        P("pipe", None, "seq"),
        P("pipe", None, "seq"),
        P("pipe", None, "seq"),
    )
    return jax.shard_map(
        shards,
        mesh=mesh,
        in_specs=placed,
        out_specs=(P("pipe", "seq", None), P("pipe", "seq", None)),
        check_vma=False,
    )
```

```python
import functools
import math

import jax
import jax.numpy as jnp
from jax import lax
from jax.experimental import pallas as pl
from jax.experimental.pallas import tpu as pltpu
from jax.sharding import PartitionSpec as P

HD = 128
LANES = 128
CHUNK = 256
EXP2_SCALE = HD ** (-0.5) * math.log2(math.e)
NT = (((1,), (1,)), ((), ()))
TN = (((0,), (0,)), ((), ()))
HEADS_WEIGHT = 8_000_000_000
TERMS_WEIGHT = 3_000_000_000
INPUT_GRAD_WEIGHT = 8_000_000_000
LAST_SUM_WEIGHT = 8_000_000_000
FORWARD_WEIGHT = 5_000_000_000
MIB = 1024 * 1024


def bits_of(number):
    return [bit for bit in range(number.bit_length()) if (number >> bit) & 1]


def by_distance(count):
    return sorted(range(1, count), key=lambda rel: (len(bits_of(rel)), rel))


def part_bounds(rows, count):
    parts = 2 if count > 2 else 1
    return [(rows * i // parts, rows * (i + 1) // parts) for i in range(parts)]


def last_bit(rel, part):
    bits = bits_of(rel)
    return bits[part % len(bits)]


def ways_to(rel, bounds):
    ways = {}
    for part, (low, high) in enumerate(bounds):
        bit = last_bit(rel, part)
        ways[bit] = (min(low, ways.get(bit, (low, high))[0]), high)
    return [(bit, low, high) for bit, (low, high) in ways.items()]


def across(value, bit):
    count = lax.axis_size("seq")
    return lax.ppermute(value, "seq", [(i, i ^ (1 << bit)) for i in range(count)])


def across_and_on(value, flip):
    count, sections = lax.axis_size("seq"), lax.axis_size("pipe")
    pairs = [
        (p * count + i, (p + 1) % sections * count + (i ^ flip))
        for p in range(sections)
        for i in range(count)
    ]
    return lax.ppermute(value, ("pipe", "seq"), pairs)


def passed_along(value, axis, steps):
    count = lax.axis_size(axis)
    pairs = [(source, (source + steps) % count) for source in range(count)]
    return lax.ppermute(value, axis, pairs)


def onward_rows(count, bounds):
    return [
        (rel ^ (1 << bit), bit, low, high)
        for rel in by_distance(count)
        for bit, low, high in ways_to(rel, bounds)
    ]


def gather_first(own, what):
    count = lax.axis_size("seq")
    blocks = {(0, 0): own}
    for rel in by_distance(count):
        if len(bits_of(rel)) == 1:
            with jax.named_scope(f"gather_{what}_block{rel}"):
                blocks[rel, 0] = across(own, bits_of(rel)[0])
    return blocks


def second_hops(blocks, rows):
    count = lax.axis_size("seq")
    return [
        (blocks[rel, 0], low, high)
        for rel, bit, low, high in onward_rows(count, part_bounds(rows, count))
        if len(bits_of(rel)) == 1
    ]


def gather_rest(blocks, picked, what):
    count = lax.axis_size("seq")
    rows = blocks[0, 0].shape[0]
    picked = list(picked)
    for rel, bit, low, high in onward_rows(count, part_bounds(rows, count)):
        if rel == 0:
            continue
        value = picked.pop(0) if len(bits_of(rel)) == 1 else blocks[rel, low]
        if value.shape[0] > high - low:
            value = value[: high - low]
        with jax.named_scope(f"gather_{what}_block{rel ^ (1 << bit)}_row{low}"):
            blocks[rel ^ (1 << bit), low] = across(value, bit)
    return blocks


def messages_of(rows, count, whole):
    parts = range(len(part_bounds(rows, count)))
    later = {
        (rel ^ (1 << last_bit(rel, part)), part)
        for rel in range(1, count)
        for part in parts
        if len(bits_of(rel)) > 1
    }
    groups, waiting = {}, {}
    for rel in reversed(by_distance(count)):
        for part in parts:
            key = (rel, part)
            if whole and len(bits_of(rel)) == 1:
                waiting.setdefault(rel, []).append(key)
            elif key in later:
                waiting[key] = [key]
            else:
                groups.setdefault(key if whole else last_bit(*key), []).append(key)
    return list(groups.values()), list(waiting.values())


def row_of(keys, key, bounds):
    before = keys[: keys.index(key)]
    return sum(bounds[part][1] - bounds[part][0] for _, part in before)


def scatter_blocks(terms, rows, whole, send_last, what, after=()):
    count = lax.axis_size("seq")
    bounds = part_bounds(rows, count)
    groups, waiting = messages_of(rows, count, whole)
    arrived, final, sums = {}, {}, []

    def send(value, keys):
        bit = last_bit(*keys[0])
        targets = [(rel ^ (1 << bit), part) for rel, part in keys]
        with jax.named_scope(f"scatter_{what}_block{keys[0][0]}_part{keys[0][1]}"):
            moved = (across if any(rel for rel, _ in targets) else send_last)(value, bit)
        for key, target in zip(keys, targets):
            piece = (moved, row_of(keys, key, bounds))
            if target[0]:
                arrived.setdefault(target, []).append(piece)
            else:
                final[key] = piece

    for value, keys in zip(terms, groups):
        send(value, keys)
    values = terms[len(groups) :]
    for level in sorted({len(bits_of(keys[0][0])) for keys in waiting}, reverse=True):
        found = [i for i, keys in enumerate(waiting) if len(bits_of(keys[0][0])) == level]
        results = sum_rows(
            [
                (
                    values[i],
                    [
                        (row_of(waiting[i], key, bounds), *piece)
                        for key in waiting[i]
                        for piece in arrived.get(key, [])
                    ],
                )
                for i in found
            ],
            bounds,
            after,
        )
        sums += results
        for i, value in zip(found, results):
            send(value, waiting[i])
    return final, sums


def call(kernel, out_shapes, operands, in_specs, scratch=(), flops=1, vmem=10, name=None):
    return pl.pallas_call(
        kernel,
        out_shape=out_shapes,
        in_specs=in_specs,
        out_specs=[pl.BlockSpec(memory_space=pltpu.VMEM)] * len(out_shapes),
        scratch_shapes=list(scratch),
        compiler_params=pltpu.CompilerParams(vmem_limit_bytes=vmem * MIB),
        cost_estimate=pl.CostEstimate(flops=int(flops), bytes_accessed=1, transcendentals=0),
        name=name,
    )(*operands)


ANY = pl.BlockSpec(memory_space=pl.ANY)
VMEM = pl.BlockSpec(memory_space=pltpu.VMEM)


def picked_shapes(pieces):
    return [
        jax.ShapeDtypeStruct((high - low, value.shape[1]), value.dtype)
        for value, low, high in pieces
    ]


def pick(pieces, in_refs, out_refs):
    for (_, low, high), in_ref, out_ref in zip(pieces, in_refs, out_refs):
        out_ref[...] = in_ref[low:high, :]


def normed_rows(inputs, gain, pieces=(), after=()):
    rows, width = inputs.shape
    n = len(pieces)

    def kernel(x_ref, gain_ref, *refs):
        refs = refs[:n] + refs[n + len(after) :]
        out_ref, inv_ref = refs[n : n + 2]
        x = x_ref[...]
        inv = lax.rsqrt(jnp.mean(x * x, -1, keepdims=True) + 1e-05)
        out_ref[...] = (x * inv * gain_ref[...]).astype(jnp.bfloat16)
        inv_ref[...] = inv
        pick(pieces, refs[:n], refs[n + 2 :])

    return call(
        kernel,
        [
            jax.ShapeDtypeStruct((rows, width), jnp.bfloat16),
            jax.ShapeDtypeStruct((rows, 1), jnp.float32),
        ]
        + picked_shapes(pieces),
        [inputs, gain] + [value for value, _, _ in pieces] + list(after),
        [VMEM] * (2 + n) + [ANY] * len(after),
        name="norm",
    )


def picked_rows(pieces, after=()):
    n = len(pieces)

    def kernel(*refs):
        pick(pieces, refs[:n], refs[n + len(after) :])

    return call(
        kernel,
        picked_shapes(pieces),
        [value for value, _, _ in pieces] + list(after),
        [VMEM] * n + [ANY] * len(after),
        name="pick",
    )


def cast_rows(inputs, after=()):
    def kernel(x_ref, *refs):
        refs[len(after)][...] = x_ref[...].astype(jnp.bfloat16)

    return call(
        kernel,
        [jax.ShapeDtypeStruct(inputs.shape, jnp.bfloat16)],
        (inputs, *after),
        [VMEM] + [ANY] * len(after),
        name="cast",
    )[0]


def sum_rows(totals, bounds, after=()):
    height = bounds[0][1] - bounds[0][0]
    pieces = [piece for _, pieces in totals for piece in pieces]
    n, m = len(totals), len(pieces)

    def kernel(*refs):
        terms, arrivals, outs = refs[:n], list(refs[n : n + m]), refs[-n:]
        for (term, moved), term_ref, out_ref in zip(totals, terms, outs):
            found = [(row, first, arrivals.pop(0)) for row, _, first in moved]
            for low in range(0, term.shape[0], height):
                total = term_ref[low : low + height, :]
                for row, first, ref in found:
                    if row == low:
                        total = total + ref[first : first + height, :].astype(jnp.float32)
                out_ref[low : low + height, :] = total.astype(jnp.bfloat16)

    return call(
        kernel,
        [jax.ShapeDtypeStruct(term.shape, jnp.bfloat16) for term, _ in totals],
        [term for term, _ in totals] + [value for _, value, _ in pieces] + list(after),
        [VMEM] * (n + m) + [ANY] * len(after),
        name="sum_rows",
    )


def block_copies(block_refs, keys, rows, all_rows, sems):
    return [
        pltpu.make_async_copy(
            ref, all_rows.at[pl.ds(rel * rows + low, ref.shape[0]), :], sems.at[i]
        )
        for i, (ref, (rel, low)) in enumerate(zip(block_refs, keys))
    ]


def turned(values, cosine, sine):
    return values * cosine + pltpu.roll(values, HD // 2, 1) * sine


def project_into(rows_ref, weight_ref, out_ref, cos_ref=None, sin_ref=None):
    features = out_ref.shape[1]
    for low in range(0, features, CHUNK):
        high = min(low + CHUNK, features)
        values = jnp.dot(
            rows_ref[...], weight_ref[:, low:high], preferred_element_type=jnp.float32
        )
        for head in range(0, high - low, HD):
            piece = values[:, head : head + HD]
            if cos_ref is not None:
                piece = turned(piece, cos_ref[...], sin_ref[...])
            out_ref[:, low + head : low + head + HD] = piece.astype(jnp.bfloat16)


def project(blocks, weights, cosine, sine, rows, weight=1):
    keys = sorted(blocks)
    length, width = cosine.shape[0], blocks[0, 0].shape[1]
    features = weights[0].shape[1]
    n = len(keys)

    def kernel(*refs):
        block_refs, weight_refs = refs[:n], refs[n : n + 3]
        cos_ref, sin_ref = refs[n + 3 : n + 5]
        outs = refs[n + 5 : n + 8]
        all_rows, sems = refs[n + 8 :]
        copies = block_copies(block_refs, keys, rows, all_rows, sems)
        for copy in copies:
            copy.start()
        for copy in copies:
            copy.wait()
        for i in range(3):
            tables = (cos_ref, sin_ref) if i < 2 else ()
            project_into(all_rows, weight_refs[i], outs[i], *tables)

    return call(
        kernel,
        [jax.ShapeDtypeStruct((length, features), jnp.bfloat16)] * 3,
        [blocks[key] for key in keys] + list(weights) + [cosine, sine],
        [ANY] * n + [VMEM] * 5,
        [pltpu.VMEM((length, width), jnp.bfloat16), pltpu.SemaphoreType.DMA((n,))],
        flops=weight,
        vmem=20,
        name="project",
    )


def term_outs(rows, width, count, whole):
    bounds = part_bounds(rows, count)
    groups, waiting = messages_of(rows, count, whole)

    def shape(keys, dtype):
        height = sum(bounds[part][1] - bounds[part][0] for _, part in keys)
        return jax.ShapeDtypeStruct((height, width), dtype)

    return [shape(keys, jnp.bfloat16) for keys in groups] + [
        shape(keys, jnp.float32) for keys in waiting
    ]


def store_terms(values, low, refs, rows, count, whole):
    bounds = part_bounds(rows, count)
    groups, waiting = messages_of(rows, count, whole)
    for ref, keys in zip(refs, groups + waiting):
        at = 0
        for rel, part in keys:
            first, last = bounds[part]
            piece = values[rel * rows + first : rel * rows + last]
            ref[at : at + last - first, low : low + values.shape[1]] = piece.astype(ref.dtype)
            at += last - first


def backward_heads(blocks, qkv, weight, cosine, sine, rows):
    in_keys = sorted(blocks)
    length, width = cosine.shape[0], blocks[0, 0].shape[1]
    features = qkv[0].shape[1]
    n = len(in_keys)
    step = min(length, 512)

    def kernel(*refs):
        block_refs, weight_ref = refs[:n], refs[n]
        q_ref, k_ref, v_ref, cos_ref, sin_ref = refs[n + 1 : n + 6]
        d_qkv = refs[n + 6 : n + 9]
        all_rows, d_attn, sems = refs[n + 9 :]
        copies = block_copies(block_refs, in_keys, rows, all_rows, sems)
        for copy in copies:
            copy.start()
        for copy in copies:
            copy.wait()
        project_into(all_rows, weight_ref, d_attn)

        for head in range(features // HD):
            cols = slice(head * HD, (head + 1) * HD)
            key, value = k_ref[:, cols], v_ref[:, cols]
            d_key, d_value = 0.0, 0.0
            for low in range(0, length, step):
                part = slice(low, low + step)
                query, grad = q_ref[part, cols], d_attn[part, cols]
                scores = lax.dot_general(key, query, NT, preferred_element_type=jnp.float32)
                top = jnp.max(scores, 0, keepdims=True)
                raised = jnp.exp2((scores - top) * EXP2_SCALE)
                probs = raised * (1.0 / jnp.sum(raised, 0, keepdims=True))
                d_value += jnp.dot(
                    probs.astype(jnp.bfloat16), grad, preferred_element_type=jnp.float32
                )
                d_probs = lax.dot_general(value, grad, NT, preferred_element_type=jnp.float32)
                delta = jnp.sum(probs * d_probs, 0, keepdims=True)
                d_scores = (probs * (d_probs - delta) * HD ** (-0.5)).astype(jnp.bfloat16)
                d_key += jnp.dot(d_scores, query, preferred_element_type=jnp.float32)
                d_query = lax.dot_general(
                    key, d_scores, TN, preferred_element_type=jnp.float32
                ).T
                d_qkv[0][part, cols] = turned(
                    d_query, cos_ref[part, :], -sin_ref[part, :]
                ).astype(jnp.bfloat16)
            d_qkv[1][:, cols] = turned(d_key, cos_ref[...], -sin_ref[...]).astype(jnp.bfloat16)
            d_qkv[2][:, cols] = d_value.astype(jnp.bfloat16)

    return call(
        kernel,
        [jax.ShapeDtypeStruct((length, features), jnp.bfloat16)] * 3,
        [blocks[key] for key in in_keys] + [weight] + list(qkv) + [cosine, sine],
        [ANY] * n + [VMEM] * 6,
        [
            pltpu.VMEM((length, width), jnp.bfloat16),
            pltpu.VMEM((length, features), jnp.bfloat16),
            pltpu.SemaphoreType.DMA((n,)),
        ],
        vmem=28,
        flops=HEADS_WEIGHT,
        name="backward_heads",
    )


def backward_terms(d_qkv, weights, rows, count, whole, after=()):
    length, features = d_qkv[0].shape
    width = weights[0].shape[0]
    shapes = term_outs(rows, width, count, whole)

    def kernel(*refs):
        grads, weight_refs = refs[:3], refs[3:6]
        own_ref, *outs = refs[6 + len(after) :]
        for low in range(0, width, CHUNK):
            total = 0.0
            for i in range(3):
                total += lax.dot_general(
                    grads[i][...],
                    weight_refs[i][low : low + CHUNK, :],
                    NT,
                    preferred_element_type=jnp.float32,
                )
            own_ref[:, low : low + CHUNK] = total[:rows]
            store_terms(total, low, outs, rows, count, whole)

    own, *terms = call(
        kernel,
        [jax.ShapeDtypeStruct((rows, width), jnp.float32)] + shapes,
        list(d_qkv) + list(weights) + list(after),
        [VMEM] * 6 + [ANY] * len(after),
        vmem=24,
        flops=TERMS_WEIGHT,
        name="backward_terms",
    )
    return own, terms


def forward_terms(qkv, act_in, weight, rows, count, whole, after=()):
    length, features = qkv[0].shape
    width = weight.shape[0]
    shapes = term_outs(rows, width, count, whole)
    step = min(length, 512)

    def kernel(*refs):
        q_ref, k_ref, v_ref, act_ref, weight_ref = refs[:5]
        own_ref, *outs = refs[5 + len(after) : -1]
        attn = refs[-1]
        for head in range(features // HD):
            cols = slice(head * HD, (head + 1) * HD)
            for low in range(0, length, step):
                part = slice(low, low + step)
                scores = lax.dot_general(
                    q_ref[part, cols], k_ref[:, cols], NT, preferred_element_type=jnp.float32
                )
                top = jnp.max(scores, 1, keepdims=True)
                raised = jnp.exp2((scores - top) * EXP2_SCALE)
                total = jnp.sum(raised, 1, keepdims=True)
                mixed = jnp.dot(
                    raised.astype(jnp.bfloat16), v_ref[:, cols], preferred_element_type=jnp.float32
                )
                attn[part, cols] = (mixed * (1.0 / total)).astype(jnp.bfloat16)

        for low in range(0, width, CHUNK):
            total = lax.dot_general(
                attn[...], weight_ref[low : low + CHUNK, :], NT, preferred_element_type=jnp.float32
            )
            own = total[:rows] + act_ref[:, low : low + CHUNK]
            own_ref[:, low : low + CHUNK] = own.astype(jnp.bfloat16)
            store_terms(total, low, outs, rows, count, whole)

    own, *terms = call(
        kernel,
        [jax.ShapeDtypeStruct((rows, width), jnp.bfloat16)] + shapes,
        list(qkv) + [act_in, weight, *after],
        [VMEM] * 5 + [ANY] * len(after),
        [pltpu.VMEM((length, features), jnp.bfloat16)],
        vmem=24,
        flops=FORWARD_WEIGHT,
        name="forward_terms",
    )
    return own, terms


def input_grad(own, pieces, saved, grad, inv, gain, bounds, after=()):
    keys = sorted(pieces)

    def kernel(own_ref, saved_ref, grad_ref, inv_ref, gain_ref, *refs):
        out_ref = refs[-1]
        for part, (low, high) in enumerate(bounds):
            total = own_ref[low:high, :]
            for ref, key in zip(refs, keys):
                if key[1] == part:
                    first = pieces[key][1]
                    total = total + ref[first : first + high - low, :].astype(jnp.float32)
            total = total * gain_ref[...]
            saved_rows = saved_ref[low:high, :]
            mean = jnp.mean(saved_rows * total, -1, keepdims=True)
            inv_rows = inv_ref[low:high, :]
            out_ref[low:high, :] = (
                grad_ref[low:high, :]
                + inv_rows * total
                - saved_rows * (inv_rows * inv_rows * inv_rows * mean)
            ).astype(jnp.bfloat16)

    return call(
        kernel,
        [jax.ShapeDtypeStruct(own.shape, jnp.bfloat16)],
        [own, saved, grad, inv, gain] + [pieces[key][0] for key in keys] + list(after),
        [VMEM] * (5 + len(keys)) + [ANY] * len(after),
        flops=INPUT_GRAD_WEIGHT,
        name="input_grad",
    )[0]


def activation_sum(own, pieces, bounds):
    keys = sorted(pieces)

    def kernel(own_ref, *refs):
        out_ref = refs[len(keys)]
        for part, (low, high) in enumerate(bounds):
            total = own_ref[low:high, :].astype(jnp.float32)
            for ref, key in zip(refs, keys):
                if key[1] == part:
                    first = pieces[key][1]
                    total = total + ref[first : first + high - low, :].astype(jnp.float32)
            out_ref[0, low:high, :] = total

    return call(
        kernel,
        [jax.ShapeDtypeStruct((1, *own.shape), jnp.float32)],
        [own] + [pieces[key][0] for key in keys],
        [VMEM] * (1 + len(keys)),
        flops=LAST_SUM_WEIGHT,
        name="activation_sum",
    )[0]


def widened(values, after=()):
    def kernel(in_ref, *refs):
        refs[len(after)][0] = in_ref[...].astype(jnp.float32)

    return call(
        kernel,
        [jax.ShapeDtypeStruct((1, *values.shape), jnp.float32)],
        (values, *after),
        [VMEM] + [ANY] * len(after),
        name="widen",
    )[0]


def rope_tables(positions):
    half_dim = HD // 2
    inverse = 10000.0 ** (-(jnp.arange(half_dim).astype(jnp.float32) * 2.0 / HD))
    angles = positions.astype(jnp.float32)[:, None] * inverse[None, :]
    cosine, sine = jnp.cos(angles), jnp.sin(angles)
    return jnp.concatenate([cosine, cosine], 1), jnp.concatenate([-sine, sine], 1)


def shards(x_fwd, x_bwd, grad_in, gain, w_query, w_key, w_value, w_out):
    act_in, saved_in, grad = x_fwd[0], x_bwd[0], grad_in[0]
    rows = act_in.shape[0]
    count = lax.axis_size("seq")
    bounds = part_bounds(rows, count)
    own_query, own_key, own_value, own_out = w_query[0], w_key[0], w_value[0], w_out[0]

    block_of = lax.axis_index("seq") ^ jnp.arange(count)
    positions = (block_of[:, None] * rows + jnp.arange(rows)[None, :]).reshape(-1)
    cosine, sine = rope_tables(positions)

    def last_arrivals(blocks):
        return [value for (rel, _), value in blocks.items() if rel == count - 1]

    projections = (own_query, own_key, own_value)
    normed_bwd, inv_bwd = normed_rows(saved_in, gain)
    grad_low = cast_rows(grad, [normed_bwd])
    all_bwd = gather_first(normed_bwd, "saved")
    all_grad = gather_first(grad_low, "grad")
    picked = picked_rows(second_hops(all_bwd, rows), [grad_low])
    all_bwd = gather_rest(all_bwd, picked, "saved")
    picked = picked_rows(second_hops(all_grad, rows), picked)
    all_grad = gather_rest(all_grad, picked, "grad")
    normed_fwd, _ = normed_rows(act_in, gain, after=picked)
    all_fwd = gather_first(normed_fwd, "input")

    qkv = project(all_bwd, projections, cosine, sine, rows)
    d_qkv = backward_heads(all_grad, qkv, own_out, cosine, sine, rows)
    picked = picked_rows(second_hops(all_fwd, rows), d_qkv[:1])
    all_fwd = gather_rest(all_fwd, picked, "input")
    d_own, d_terms = backward_terms(d_qkv, projections, rows, count, False, picked)
    qkv = project(all_fwd, projections, cosine, sine, rows, FORWARD_WEIGHT)
    own, terms = forward_terms(qkv, act_in, own_out, rows, count, True)

    d_pieces, d_sums = scatter_blocks(d_terms, rows, False, across, "grad", [own])
    pieces, sums = scatter_blocks(
        terms, rows, True, lambda value, bit: across_and_on(value, 1 << bit), "branch", d_sums
    )
    own = across_and_on(own, 0)
    d_input = input_grad(d_own, d_pieces, saved_in, grad, inv_bwd, gain, bounds, sums)
    act_next = activation_sum(own, pieces, bounds)
    return (act_next, widened(passed_along(d_input, "pipe", -1), [act_next]))


def solution(mesh):
    placed = (
        P("pipe", "seq", None),
        P("pipe", "seq", None),
        P("pipe", "seq", None),
        P("pipe", None),
        P("pipe", None, "seq"),
        P("pipe", None, "seq"),
        P("pipe", None, "seq"),
        P("pipe", None, "seq"),
    )
    return jax.shard_map(
        shards,
        mesh=mesh,
        in_specs=placed,
        out_specs=(P("pipe", "seq", None), P("pipe", "seq", None)),
        check_vma=False,
    )
```

```python
import functools
import math

import jax
import jax.numpy as jnp
from jax import lax
from jax.experimental import pallas as pl
from jax.experimental.pallas import tpu as pltpu
from jax.sharding import PartitionSpec as P

HD = 128
LANES = 128
CHUNK = 256
EXP2_SCALE = HD ** (-0.5) * math.log2(math.e)
NT = (((1,), (1,)), ((), ()))
TN = (((0,), (0,)), ((), ()))
HEADS_WEIGHT = 8_000_000_000
TERMS_WEIGHT = 3_000_000_000
INPUT_GRAD_WEIGHT = 8_000_000_000
LAST_SUM_WEIGHT = 8_000_000_000
FORWARD_WEIGHT = 5_000_000_000
MIB = 1024 * 1024


def bits_of(number):
    return [bit for bit in range(number.bit_length()) if (number >> bit) & 1]


def by_distance(count):
    return sorted(range(1, count), key=lambda rel: (len(bits_of(rel)), rel))


def part_bounds(rows, count):
    parts = 2 if count > 2 else 1
    return [(rows * i // parts, rows * (i + 1) // parts) for i in range(parts)]


def last_bit(rel, part):
    bits = bits_of(rel)
    return bits[part % len(bits)]


def ways_to(rel, bounds):
    ways = {}
    for part, (low, high) in enumerate(bounds):
        bit = last_bit(rel, part)
        ways[bit] = (min(low, ways.get(bit, (low, high))[0]), high)
    return [(bit, low, high) for bit, (low, high) in ways.items()]


def across(value, bit):
    count = lax.axis_size("seq")
    return lax.ppermute(value, "seq", [(i, i ^ (1 << bit)) for i in range(count)])


def across_and_on(value, flip):
    count, sections = lax.axis_size("seq"), lax.axis_size("pipe")
    pairs = [
        (p * count + i, (p + 1) % sections * count + (i ^ flip))
        for p in range(sections)
        for i in range(count)
    ]
    return lax.ppermute(value, ("pipe", "seq"), pairs)


def passed_along(value, axis, steps):
    count = lax.axis_size(axis)
    pairs = [(source, (source + steps) % count) for source in range(count)]
    return lax.ppermute(value, axis, pairs)


def onward_rows(count, bounds):
    return [
        (rel ^ (1 << bit), bit, low, high)
        for rel in by_distance(count)
        for bit, low, high in ways_to(rel, bounds)
    ]


def gather_first(own, what):
    count = lax.axis_size("seq")
    blocks = {(0, 0): own}
    for rel in by_distance(count):
        if len(bits_of(rel)) == 1:
            with jax.named_scope(f"gather_{what}_block{rel}"):
                blocks[rel, 0] = across(own, bits_of(rel)[0])
    return blocks


def second_hops(blocks, rows):
    count = lax.axis_size("seq")
    return [
        (blocks[rel, 0], low, high)
        for rel, bit, low, high in onward_rows(count, part_bounds(rows, count))
        if len(bits_of(rel)) == 1
    ]


def gather_rest(blocks, picked, what):
    count = lax.axis_size("seq")
    rows = blocks[0, 0].shape[0]
    picked = list(picked)
    for rel, bit, low, high in onward_rows(count, part_bounds(rows, count)):
        if rel == 0:
            continue
        value = picked.pop(0) if len(bits_of(rel)) == 1 else blocks[rel, low]
        if value.shape[0] > high - low:
            value = value[: high - low]
        with jax.named_scope(f"gather_{what}_block{rel ^ (1 << bit)}_row{low}"):
            blocks[rel ^ (1 << bit), low] = across(value, bit)
    return blocks


def messages_of(rows, count, joined):
    parts = range(len(part_bounds(rows, count)))
    later = {
        (rel ^ (1 << last_bit(rel, part)), part)
        for rel in range(1, count)
        for part in parts
        if len(bits_of(rel)) > 1
    }
    keys = [(rel, part) for rel in reversed(by_distance(count)) for part in parts]
    groups = {}
    for key in keys:
        if key not in later:
            groups.setdefault(last_bit(*key) if joined else key, []).append(key)
    return list(groups.values()), [key for key in keys if key in later]


class Scatter:

    def __init__(self, terms, rows, joined, send_last, what):
        count = lax.axis_size("seq")
        self.bounds = part_bounds(rows, count)
        self.groups, waiting = messages_of(rows, count, joined)
        self.leaving = list(terms[: len(self.groups)])
        self.waiting = dict(zip(waiting, terms[len(self.groups) :]))
        self.send_last, self.what = send_last, what
        self.arrived, self.final = {}, {}

    def send(self, value, keys):
        bit = last_bit(*keys[0])
        targets = [(rel ^ (1 << bit), part) for rel, part in keys]
        onward = any(rel for rel, _ in targets)
        with jax.named_scope(f"scatter_{self.what}_block{keys[0][0]}_part{keys[0][1]}"):
            moved = (across if onward else self.send_last)(value, bit)
        first = 0
        for key, target in zip(keys, targets):
            if target[0]:
                self.arrived.setdefault(target, []).append((moved, first))
            else:
                self.final[key] = (moved, first)
            first += self.bounds[key[1]][1] - self.bounds[key[1]][0]

    def onward(self):
        return [i for i, keys in enumerate(self.groups) if len(bits_of(keys[0][0])) > 1]

    def send_groups(self, places):
        for i in places:
            self.send(self.leaving[i], self.groups[i])

    def send_sums(self, handed_on=(), after=()):
        for level in sorted({len(bits_of(rel)) for rel, _ in self.waiting}, reverse=True):
            keys = [key for key in self.waiting if len(bits_of(key[0])) == level]
            totals = [(self.waiting[key], self.arrived[key]) for key in keys]
            results = sum_rows(totals, handed_on, after)
            handed_on = results[len(keys) :]
            for key, value in zip(keys, results):
                self.send(value, [key])
        return handed_on


def call(kernel, out_shapes, operands, in_specs, scratch=(), flops=1, vmem=10, name=None):
    return pl.pallas_call(
        kernel,
        out_shape=out_shapes,
        in_specs=in_specs,
        out_specs=[pl.BlockSpec(memory_space=pltpu.VMEM)] * len(out_shapes),
        scratch_shapes=list(scratch),
        compiler_params=pltpu.CompilerParams(vmem_limit_bytes=vmem * MIB),
        cost_estimate=pl.CostEstimate(flops=int(flops), bytes_accessed=1, transcendentals=0),
        name=name,
    )(*operands)


ANY = pl.BlockSpec(memory_space=pl.ANY)
VMEM = pl.BlockSpec(memory_space=pltpu.VMEM)


def picked_shapes(pieces):
    return [
        jax.ShapeDtypeStruct((high - low, value.shape[1]), value.dtype)
        for value, low, high in pieces
    ]


def pick(pieces, in_refs, out_refs):
    for (_, low, high), in_ref, out_ref in zip(pieces, in_refs, out_refs):
        out_ref[...] = in_ref[low:high, :]


def normed_rows(inputs, gain, pieces=(), after=()):
    rows, width = inputs.shape
    n = len(pieces)

    def kernel(x_any, gain_any, *refs):
        refs, (x_ref, gain_ref, sems) = refs[:n] + refs[n + len(after) : -3], refs[-3:]
        out_ref, inv_ref = refs[n : n + 2]
        copies = [
            pltpu.make_async_copy(source, held, sems.at[i])
            for i, (source, held) in enumerate([(x_any, x_ref), (gain_any, gain_ref)])
        ]
        for copy in copies:
            copy.start()
        for copy in copies:
            copy.wait()
        x = x_ref[...]
        inv = lax.rsqrt(jnp.mean(x * x, -1, keepdims=True) + 1e-05)
        out_ref[...] = (x * inv * gain_ref[...]).astype(jnp.bfloat16)
        inv_ref[...] = inv
        pick(pieces, refs[:n], refs[n + 2 :])

    return call(
        kernel,
        [
            jax.ShapeDtypeStruct((rows, width), jnp.bfloat16),
            jax.ShapeDtypeStruct((rows, 1), jnp.float32),
        ]
        + picked_shapes(pieces),
        [inputs, gain] + [value for value, _, _ in pieces] + list(after),
        [ANY] * 2 + [VMEM] * n + [ANY] * len(after),
        [
            pltpu.VMEM(inputs.shape, jnp.float32),
            pltpu.VMEM(gain.shape, jnp.float32),
            pltpu.SemaphoreType.DMA((2,)),
        ],
        name="norm",
    )


def picked_rows(pieces, after=()):
    n = len(pieces)

    def kernel(*refs):
        pick(pieces, refs[:n], refs[n + len(after) :])

    return call(
        kernel,
        picked_shapes(pieces),
        [value for value, _, _ in pieces] + list(after),
        [VMEM] * n + [ANY] * len(after),
        name="pick",
    )


def cast_rows(inputs, after=()):
    def kernel(x_ref, *refs):
        refs[len(after)][...] = x_ref[...].astype(jnp.bfloat16)

    return call(
        kernel,
        [jax.ShapeDtypeStruct(inputs.shape, jnp.bfloat16)],
        (inputs, *after),
        [VMEM] + [ANY] * len(after),
        name="cast",
    )[0]


def sum_rows(totals, handed_on=(), after=()):
    pieces = [piece for _, pieces in totals for piece in pieces]
    n, m, k = len(totals), len(pieces), len(handed_on)

    def kernel(*refs):
        arrivals, outs = list(refs[n : n + m]), refs[-n - k :]
        for (term, moved), term_ref, out_ref in zip(totals, refs, outs):
            total = term_ref[...]
            for _, first in moved:
                ref = arrivals.pop(0)
                total = total + ref[first : first + term.shape[0], :].astype(jnp.float32)
            out_ref[...] = total.astype(jnp.bfloat16)
        for in_ref, out_ref in zip(refs[n + m : n + m + k], outs[n:]):
            out_ref[...] = in_ref[...]

    return call(
        kernel,
        [jax.ShapeDtypeStruct(term.shape, jnp.bfloat16) for term, _ in totals]
        + [jax.ShapeDtypeStruct(value.shape, value.dtype) for value in handed_on],
        [term for term, _ in totals]
        + [value for value, _ in pieces]
        + list(handed_on)
        + list(after),
        [VMEM] * (n + m + k) + [ANY] * len(after),
        name="sum_rows",
    )


def block_copies(block_refs, keys, rows, all_rows, sems):
    return [
        pltpu.make_async_copy(
            ref, all_rows.at[pl.ds(rel * rows + low, ref.shape[0]), :], sems.at[i]
        )
        for i, (ref, (rel, low)) in enumerate(zip(block_refs, keys))
    ]


def turned(values, cosine, sine):
    return values * cosine + pltpu.roll(values, HD // 2, 1) * sine


def project_into(rows_ref, weight_ref, out_ref, cos_ref=None, sin_ref=None):
    features = out_ref.shape[1]
    for low in range(0, features, CHUNK):
        high = min(low + CHUNK, features)
        values = jnp.dot(
            rows_ref[...], weight_ref[:, low:high], preferred_element_type=jnp.float32
        )
        for head in range(0, high - low, HD):
            piece = values[:, head : head + HD]
            if cos_ref is not None:
                piece = turned(piece, cos_ref[...], sin_ref[...])
            out_ref[:, low + head : low + head + HD] = piece.astype(jnp.bfloat16)


def project(blocks, weights, cosine, sine, rows, weight=1):
    keys = sorted(blocks)
    length, width = cosine.shape[0], blocks[0, 0].shape[1]
    features = weights[0].shape[1]
    n = len(keys)

    def kernel(*refs):
        block_refs, weight_refs = refs[:n], refs[n : n + 3]
        cos_ref, sin_ref = refs[n + 3 : n + 5]
        outs = refs[n + 5 : n + 8]
        all_rows, sems = refs[n + 8 :]
        copies = block_copies(block_refs, keys, rows, all_rows, sems)
        for copy in copies:
            copy.start()
        for copy in copies:
            copy.wait()
        for i in range(3):
            tables = (cos_ref, sin_ref) if i < 2 else ()
            project_into(all_rows, weight_refs[i], outs[i], *tables)

    return call(
        kernel,
        [jax.ShapeDtypeStruct((length, features), jnp.bfloat16)] * 3,
        [blocks[key] for key in keys] + list(weights) + [cosine, sine],
        [ANY] * n + [VMEM] * 5,
        [pltpu.VMEM((length, width), jnp.bfloat16), pltpu.SemaphoreType.DMA((n,))],
        flops=weight,
        vmem=20,
        name="project",
    )


def term_outs(rows, width, count, joined):
    bounds = part_bounds(rows, count)
    groups, waiting = messages_of(rows, count, joined)

    def shape(keys, dtype):
        height = sum(bounds[part][1] - bounds[part][0] for _, part in keys)
        return jax.ShapeDtypeStruct((height, width), dtype)

    return [shape(keys, jnp.bfloat16) for keys in groups] + [
        shape([key], jnp.float32) for key in waiting
    ]


def store_terms(values, low, refs, rows, count, joined):
    bounds = part_bounds(rows, count)
    groups, waiting = messages_of(rows, count, joined)
    for ref, keys in zip(refs, groups + [[key] for key in waiting]):
        at = 0
        for rel, part in keys:
            first, last = bounds[part]
            piece = values[rel * rows + first : rel * rows + last]
            ref[at : at + last - first, low : low + values.shape[1]] = piece.astype(ref.dtype)
            at += last - first


def backward_heads(blocks, qkv, weight, cosine, sine, rows):
    in_keys = sorted(blocks)
    length, width = cosine.shape[0], blocks[0, 0].shape[1]
    features = qkv[0].shape[1]
    n = len(in_keys)
    step = min(length, 512)

    def kernel(*refs):
        block_refs, weight_ref = refs[:n], refs[n]
        q_ref, k_ref, v_ref, cos_ref, sin_ref = refs[n + 1 : n + 6]
        d_qkv = refs[n + 6 : n + 9]
        all_rows, d_attn, sems = refs[n + 9 :]
        copies = block_copies(block_refs, in_keys, rows, all_rows, sems)
        for copy in copies:
            copy.start()
        for copy in copies:
            copy.wait()
        project_into(all_rows, weight_ref, d_attn)

        for head in range(features // HD):
            cols = slice(head * HD, (head + 1) * HD)
            key, value = k_ref[:, cols], v_ref[:, cols]
            d_key, d_value = 0.0, 0.0
            for low in range(0, length, step):
                part = slice(low, low + step)
                query, grad = q_ref[part, cols], d_attn[part, cols]
                scores = lax.dot_general(key, query, NT, preferred_element_type=jnp.float32)
                top = jnp.max(scores, 0, keepdims=True)
                raised = jnp.exp2((scores - top) * EXP2_SCALE)
                probs = raised * (1.0 / jnp.sum(raised, 0, keepdims=True))
                d_value += jnp.dot(
                    probs.astype(jnp.bfloat16), grad, preferred_element_type=jnp.float32
                )
                d_probs = lax.dot_general(value, grad, NT, preferred_element_type=jnp.float32)
                delta = jnp.sum(probs * d_probs, 0, keepdims=True)
                d_scores = (probs * (d_probs - delta) * HD ** (-0.5)).astype(jnp.bfloat16)
                d_key += jnp.dot(d_scores, query, preferred_element_type=jnp.float32)
                d_query = lax.dot_general(
                    key, d_scores, TN, preferred_element_type=jnp.float32
                ).T
                d_qkv[0][part, cols] = turned(
                    d_query, cos_ref[part, :], -sin_ref[part, :]
                ).astype(jnp.bfloat16)
            d_qkv[1][:, cols] = turned(d_key, cos_ref[...], -sin_ref[...]).astype(jnp.bfloat16)
            d_qkv[2][:, cols] = d_value.astype(jnp.bfloat16)

    return call(
        kernel,
        [jax.ShapeDtypeStruct((length, features), jnp.bfloat16)] * 3,
        [blocks[key] for key in in_keys] + [weight] + list(qkv) + [cosine, sine],
        [ANY] * n + [VMEM] * 6,
        [
            pltpu.VMEM((length, width), jnp.bfloat16),
            pltpu.VMEM((length, features), jnp.bfloat16),
            pltpu.SemaphoreType.DMA((n,)),
        ],
        vmem=28,
        flops=HEADS_WEIGHT,
        name="backward_heads",
    )


def backward_terms(d_qkv, weights, rows, count, joined, after=()):
    length, features = d_qkv[0].shape
    width = weights[0].shape[0]
    shapes = term_outs(rows, width, count, joined)

    def kernel(*refs):
        grads, weight_refs = refs[:3], refs[3:6]
        own_ref, *outs = refs[6 + len(after) :]
        for low in range(0, width, CHUNK):
            total = 0.0
            for i in range(3):
                total += lax.dot_general(
                    grads[i][...],
                    weight_refs[i][low : low + CHUNK, :],
                    NT,
                    preferred_element_type=jnp.float32,
                )
            own_ref[:, low : low + CHUNK] = total[:rows]
            store_terms(total, low, outs, rows, count, joined)

    own, *terms = call(
        kernel,
        [jax.ShapeDtypeStruct((rows, width), jnp.float32)] + shapes,
        list(d_qkv) + list(weights) + list(after),
        [VMEM] * 6 + [ANY] * len(after),
        vmem=24,
        flops=TERMS_WEIGHT,
        name="backward_terms",
    )
    return own, terms


def forward_terms(qkv, act_in, weight, rows, count, joined, after=()):
    length, features = qkv[0].shape
    width = weight.shape[0]
    shapes = term_outs(rows, width, count, joined)
    step = min(length, 512)

    def kernel(*refs):
        q_ref, k_ref, v_ref, act_ref, weight_ref = refs[:5]
        own_ref, *outs = refs[5 + len(after) : -1]
        attn = refs[-1]
        for head in range(features // HD):
            cols = slice(head * HD, (head + 1) * HD)
            for low in range(0, length, step):
                part = slice(low, low + step)
                scores = lax.dot_general(
                    q_ref[part, cols], k_ref[:, cols], NT, preferred_element_type=jnp.float32
                )
                top = jnp.max(scores, 1, keepdims=True)
                raised = jnp.exp2((scores - top) * EXP2_SCALE)
                total = jnp.sum(raised, 1, keepdims=True)
                mixed = jnp.dot(
                    raised.astype(jnp.bfloat16), v_ref[:, cols], preferred_element_type=jnp.float32
                )
                attn[part, cols] = (mixed * (1.0 / total)).astype(jnp.bfloat16)

        for low in range(0, width, CHUNK):
            total = lax.dot_general(
                attn[...], weight_ref[low : low + CHUNK, :], NT, preferred_element_type=jnp.float32
            )
            own = total[:rows] + act_ref[:, low : low + CHUNK]
            own_ref[:, low : low + CHUNK] = own.astype(jnp.bfloat16)
            store_terms(total, low, outs, rows, count, joined)

    own, *terms = call(
        kernel,
        [jax.ShapeDtypeStruct((rows, width), jnp.bfloat16)] + shapes,
        list(qkv) + [act_in, weight, *after],
        [VMEM] * 5 + [ANY] * len(after),
        [pltpu.VMEM((length, features), jnp.bfloat16)],
        vmem=24,
        flops=FORWARD_WEIGHT,
        name="forward_terms",
    )
    return own, terms


def input_grad(own, pieces, saved, grad, inv, gain, bounds, after=()):
    keys = sorted(pieces)

    def kernel(own_ref, saved_ref, grad_ref, inv_ref, gain_ref, *refs):
        out_ref = refs[-1]
        for part, (low, high) in enumerate(bounds):
            total = own_ref[low:high, :]
            for ref, key in zip(refs, keys):
                if key[1] == part:
                    first = pieces[key][1]
                    total = total + ref[first : first + high - low, :].astype(jnp.float32)
            total = total * gain_ref[...]
            saved_rows = saved_ref[low:high, :]
            mean = jnp.mean(saved_rows * total, -1, keepdims=True)
            inv_rows = inv_ref[low:high, :]
            out_ref[low:high, :] = (
                grad_ref[low:high, :]
                + inv_rows * total
                - saved_rows * (inv_rows * inv_rows * inv_rows * mean)
            ).astype(jnp.bfloat16)

    return call(
        kernel,
        [jax.ShapeDtypeStruct(own.shape, jnp.bfloat16)],
        [own, saved, grad, inv, gain] + [pieces[key][0] for key in keys] + list(after),
        [VMEM] * (5 + len(keys)) + [ANY] * len(after),
        flops=INPUT_GRAD_WEIGHT,
        name="input_grad",
    )[0]


def activation_sum(own, pieces, bounds, after=()):
    keys = sorted(pieces)

    def kernel(own_ref, *refs):
        out_ref = refs[-1]
        for part, (low, high) in enumerate(bounds):
            total = own_ref[low:high, :].astype(jnp.float32)
            for ref, key in zip(refs, keys):
                if key[1] == part:
                    first = pieces[key][1]
                    total = total + ref[first : first + high - low, :].astype(jnp.float32)
            out_ref[0, low:high, :] = total

    return call(
        kernel,
        [jax.ShapeDtypeStruct((1, *own.shape), jnp.float32)],
        [own] + [pieces[key][0] for key in keys] + list(after),
        [VMEM] * (1 + len(keys)) + [ANY] * len(after),
        flops=LAST_SUM_WEIGHT,
        name="activation_sum",
    )[0]


def widened(values):
    def kernel(in_ref, out_ref):
        out_ref[0] = in_ref[...].astype(jnp.float32)

    return call(
        kernel,
        [jax.ShapeDtypeStruct((1, *values.shape), jnp.float32)],
        (values,),
        [VMEM],
        name="widen",
    )[0]


def rope_tables(positions):
    half_dim = HD // 2
    inverse = 10000.0 ** (-(jnp.arange(half_dim).astype(jnp.float32) * 2.0 / HD))
    angles = positions.astype(jnp.float32)[:, None] * inverse[None, :]
    cosine, sine = jnp.cos(angles), jnp.sin(angles)
    return jnp.concatenate([cosine, cosine], 1), jnp.concatenate([-sine, sine], 1)


def shards(x_fwd, x_bwd, grad_in, gain, w_query, w_key, w_value, w_out):
    act_in, saved_in, grad = x_fwd[0], x_bwd[0], grad_in[0]
    rows = act_in.shape[0]
    count = lax.axis_size("seq")
    bounds = part_bounds(rows, count)
    own_query, own_key, own_value, own_out = w_query[0], w_key[0], w_value[0], w_out[0]

    block_of = lax.axis_index("seq") ^ jnp.arange(count)
    positions = (block_of[:, None] * rows + jnp.arange(rows)[None, :]).reshape(-1)
    cosine, sine = rope_tables(positions)

    def last_arrivals(blocks):
        return [value for (rel, _), value in blocks.items() if rel == count - 1]

    projections = (own_query, own_key, own_value)
    normed_bwd, inv_bwd = normed_rows(saved_in, gain)
    grad_low = cast_rows(grad, [normed_bwd])
    all_bwd = gather_first(normed_bwd, "saved")
    all_grad = gather_first(grad_low, "grad")
    picked = picked_rows(second_hops(all_bwd, rows), [grad_low])
    all_bwd = gather_rest(all_bwd, picked, "saved")
    picked = picked_rows(second_hops(all_grad, rows), picked)
    all_grad = gather_rest(all_grad, picked, "grad")
    normed_fwd, _ = normed_rows(act_in, gain, after=picked)
    all_fwd = gather_first(normed_fwd, "input")

    qkv = project(all_bwd, projections, cosine, sine, rows)
    d_qkv = backward_heads(all_grad, qkv, own_out, cosine, sine, rows)
    picked = picked_rows(second_hops(all_fwd, rows), d_qkv[:1])
    all_fwd = gather_rest(all_fwd, picked, "input")
    d_own, d_terms = backward_terms(d_qkv, projections, rows, count, True, picked)
    qkv = project(all_fwd, projections, cosine, sine, rows, FORWARD_WEIGHT)
    own, terms = forward_terms(qkv, act_in, own_out, rows, count, False)

    back = Scatter(d_terms, rows, True, across, "grad")
    front = Scatter(
        terms, rows, False, lambda value, bit: across_and_on(value, 1 << bit), "branch"
    )
    back.send_groups(range(len(back.groups)))
    onward = front.onward()
    front.send_groups([i for i in range(len(front.groups)) if i not in onward])
    own = across_and_on(own, 0)
    soon = [own] + [value for value, _ in front.final.values()]
    held = back.send_sums([front.leaving[i] for i in onward], [terms[0]])
    for i, value in zip(onward, held):
        front.leaving[i] = value
    front.send_groups(onward)
    d_input = input_grad(d_own, back.final, saved_in, grad, inv_bwd, gain, bounds, soon)
    front.send_sums(after=[d_input])
    grad_prev = widened(passed_along(d_input, "pipe", -1))
    return (activation_sum(own, front.final, bounds, [grad_prev]), grad_prev)


def solution(mesh):
    placed = (
        P("pipe", "seq", None),
        P("pipe", "seq", None),
        P("pipe", "seq", None),
        P("pipe", None),
        P("pipe", None, "seq"),
        P("pipe", None, "seq"),
        P("pipe", None, "seq"),
        P("pipe", None, "seq"),
    )
    return jax.shard_map(
        shards,
        mesh=mesh,
        in_specs=placed,
        out_specs=(P("pipe", "seq", None), P("pipe", "seq", None)),
        check_vma=False,
    )
```

```python
import functools
import math

import jax
import jax.numpy as jnp
from jax import lax
from jax.experimental import pallas as pl
from jax.experimental.pallas import tpu as pltpu
from jax.sharding import PartitionSpec as P

HD = 128
LANES = 128
CHUNK = 256
EXP2_SCALE = HD ** (-0.5) * math.log2(math.e)
NT = (((1,), (1,)), ((), ()))
TN = (((0,), (0,)), ((), ()))
HEADS_WEIGHT = 8_000_000_000
TERMS_WEIGHT = 3_000_000_000
INPUT_GRAD_WEIGHT = 8_000_000_000
LAST_SUM_WEIGHT = 8_000_000_000
FORWARD_WEIGHT = 5_000_000_000
MIB = 1024 * 1024


def bits_of(number):
    return [bit for bit in range(number.bit_length()) if (number >> bit) & 1]


def by_distance(count):
    return sorted(range(1, count), key=lambda rel: (len(bits_of(rel)), rel))


def part_bounds(rows, count):
    parts = 2 if count > 2 else 1
    return [(rows * i // parts, rows * (i + 1) // parts) for i in range(parts)]


def last_bit(rel, part):
    bits = bits_of(rel)
    return bits[part % len(bits)]


def ways_to(rel, bounds):
    ways = {}
    for part, (low, high) in enumerate(bounds):
        bit = last_bit(rel, part)
        ways[bit] = (min(low, ways.get(bit, (low, high))[0]), high)
    return [(bit, low, high) for bit, (low, high) in ways.items()]


def across(value, bit):
    count = lax.axis_size("seq")
    return lax.ppermute(value, "seq", [(i, i ^ (1 << bit)) for i in range(count)])


def across_and_on(value, flip):
    count, sections = lax.axis_size("seq"), lax.axis_size("pipe")
    pairs = [
        (p * count + i, (p + 1) % sections * count + (i ^ flip))
        for p in range(sections)
        for i in range(count)
    ]
    return lax.ppermute(value, ("pipe", "seq"), pairs)


def passed_along(value, axis, steps):
    count = lax.axis_size(axis)
    pairs = [(source, (source + steps) % count) for source in range(count)]
    return lax.ppermute(value, axis, pairs)


def onward_rows(count, bounds):
    return [
        (rel ^ (1 << bit), bit, low, high)
        for rel in by_distance(count)
        for bit, low, high in ways_to(rel, bounds)
    ]


def goes_on(rel, low, count, bounds):
    return any(
        rel == at and first <= low < last for at, _, first, last in onward_rows(count, bounds)
    )


def gather_first(own, what):
    count = lax.axis_size("seq")
    blocks = {(0, 0): own}
    for rel in by_distance(count):
        if len(bits_of(rel)) == 1:
            with jax.named_scope(f"gather_{what}_block{rel}"):
                blocks[rel, 0] = across(own, bits_of(rel)[0])
    return blocks


def gather_parts(blocks, own_parts, bounds, early, what):
    count = lax.axis_size("seq")
    for rel in by_distance(count):
        for value, (low, _) in zip(own_parts, bounds):
            blocks.setdefault((0, low), value)
            if len(bits_of(rel)) == 1 and goes_on(rel, low, count, bounds) == early:
                with jax.named_scope(f"gather_{what}_block{rel}_first{low}"):
                    blocks[rel, low] = across(value, bits_of(rel)[0])
    return blocks


def second_hops(blocks, bounds):
    hops = []
    for rel, _, low, high in onward_rows(lax.axis_size("seq"), bounds):
        if len(bits_of(rel)) == 1:
            first = low if (rel, low) in blocks else 0
            hops.append((blocks[rel, first], low - first, high - first))
    return hops


def gather_rest(blocks, picked, bounds, what):
    count = lax.axis_size("seq")
    picked = list(picked)
    for rel, bit, low, high in onward_rows(count, bounds):
        if rel == 0:
            continue
        value = picked.pop(0) if len(bits_of(rel)) == 1 else blocks[rel, low]
        if value.shape[0] > high - low:
            value = value[: high - low]
        with jax.named_scope(f"gather_{what}_block{rel ^ (1 << bit)}_row{low}"):
            blocks[rel ^ (1 << bit), low] = across(value, bit)
    return blocks


def messages_of(rows, count, joined):
    parts = range(len(part_bounds(rows, count)))
    later = {
        (rel ^ (1 << last_bit(rel, part)), part)
        for rel in range(1, count)
        for part in parts
        if len(bits_of(rel)) > 1
    }
    keys = [(rel, part) for rel in reversed(by_distance(count)) for part in parts]
    groups = {}
    for key in keys:
        if key not in later:
            groups.setdefault(last_bit(*key) if joined else key, []).append(key)
    return list(groups.values()), [key for key in keys if key in later]


class Scatter:

    def __init__(self, terms, rows, joined, send_last, what):
        count = lax.axis_size("seq")
        self.bounds = part_bounds(rows, count)
        self.groups, waiting = messages_of(rows, count, joined)
        self.leaving = list(terms[: len(self.groups)])
        self.waiting = dict(zip(waiting, terms[len(self.groups) :]))
        self.send_last, self.what = send_last, what
        self.arrived, self.final = {}, {}

    def send(self, value, keys):
        bit = last_bit(*keys[0])
        targets = [(rel ^ (1 << bit), part) for rel, part in keys]
        onward = any(rel for rel, _ in targets)
        with jax.named_scope(f"scatter_{self.what}_block{keys[0][0]}_part{keys[0][1]}"):
            moved = (across if onward else self.send_last)(value, bit)
        first = 0
        for key, target in zip(keys, targets):
            if target[0]:
                self.arrived.setdefault(target, []).append((moved, first))
            else:
                self.final[key] = (moved, first)
            first += self.bounds[key[1]][1] - self.bounds[key[1]][0]

    def onward(self):
        return [i for i, keys in enumerate(self.groups) if len(bits_of(keys[0][0])) > 1]

    def send_groups(self, places):
        for i in places:
            self.send(self.leaving[i], self.groups[i])

    def send_sums(self, after=()):
        sums = []
        for level in sorted({len(bits_of(rel)) for rel, _ in self.waiting}, reverse=True):
            keys = [key for key in self.waiting if len(bits_of(key[0])) == level]
            totals = [(self.waiting[key], self.arrived[key]) for key in keys]
            results = sum_rows(totals, after)
            sums += results
            for key, value in zip(keys, results):
                self.send(value, [key])
        return sums


def call(kernel, out_shapes, operands, in_specs, scratch=(), flops=1, vmem=10, name=None):
    return pl.pallas_call(
        kernel,
        out_shape=out_shapes,
        in_specs=in_specs,
        out_specs=[pl.BlockSpec(memory_space=pltpu.VMEM)] * len(out_shapes),
        scratch_shapes=list(scratch),
        compiler_params=pltpu.CompilerParams(vmem_limit_bytes=vmem * MIB),
        cost_estimate=pl.CostEstimate(flops=int(flops), bytes_accessed=1, transcendentals=0),
        name=name,
    )(*operands)


ANY = pl.BlockSpec(memory_space=pl.ANY)
HBM = pl.BlockSpec(memory_space=pltpu.HBM)
VMEM = pl.BlockSpec(memory_space=pltpu.VMEM)


def normed_rows(inputs, gain, bounds, after=()):
    rows, width = inputs.shape

    def kernel(x_any, gain_any, *refs):
        *outs, inv_ref, x_ref, gain_ref, sems = refs[len(after) :]
        copies = [
            pltpu.make_async_copy(source, held, sems.at[i])
            for i, (source, held) in enumerate([(x_any, x_ref), (gain_any, gain_ref)])
        ]
        for copy in copies:
            copy.start()
        for copy in copies:
            copy.wait()
        for out_ref, (low, high) in zip(outs, bounds):
            x = x_ref[low:high, :]
            inv = lax.rsqrt(jnp.mean(x * x, -1, keepdims=True) + 1e-05)
            out_ref[...] = (x * inv * gain_ref[...]).astype(jnp.bfloat16)
            inv_ref[low:high, :] = inv

    *parts, inv = call(
        kernel,
        [jax.ShapeDtypeStruct((high - low, width), jnp.bfloat16) for low, high in bounds]
        + [jax.ShapeDtypeStruct((rows, 1), jnp.float32)],
        [inputs, gain, *after],
        [HBM] * 2 + [ANY] * len(after),
        [
            pltpu.VMEM(inputs.shape, jnp.float32),
            pltpu.VMEM(gain.shape, jnp.float32),
            pltpu.SemaphoreType.DMA((2,)),
        ],
        name="norm",
    )
    return parts, inv


def picked_rows(pieces, after=()):
    n = len(pieces)

    def kernel(*refs):
        outs, sems = refs[n + len(after) : -1], refs[-1]
        copies = [
            pltpu.make_async_copy(ref.at[pl.ds(low, high - low), :], out_ref, sems.at[i])
            for i, (ref, out_ref, (_, low, high)) in enumerate(zip(refs, outs, pieces))
        ]
        for copy in copies:
            copy.start()
        for copy in copies:
            copy.wait()

    return call(
        kernel,
        [
            jax.ShapeDtypeStruct((high - low, value.shape[1]), value.dtype)
            for value, low, high in pieces
        ],
        [value for value, _, _ in pieces] + list(after),
        [ANY] * (n + len(after)),
        [pltpu.SemaphoreType.DMA((n,))],
        name="pick",
    )


def cast_rows(inputs, after=()):
    def kernel(x_ref, *refs):
        refs[len(after)][...] = x_ref[...].astype(jnp.bfloat16)

    return call(
        kernel,
        [jax.ShapeDtypeStruct(inputs.shape, jnp.bfloat16)],
        (inputs, *after),
        [VMEM] + [ANY] * len(after),
        name="cast",
    )[0]


def sum_rows(totals, after=()):
    pieces = [piece for _, pieces in totals for piece in pieces]
    n, m = len(totals), len(pieces)

    def kernel(*refs):
        arrivals, outs = list(refs[n : n + m]), refs[-n:]
        for (term, moved), term_ref, out_ref in zip(totals, refs, outs):
            total = term_ref[...]
            for _, first in moved:
                ref = arrivals.pop(0)
                total = total + ref[first : first + term.shape[0], :].astype(jnp.float32)
            out_ref[...] = total.astype(jnp.bfloat16)

    return call(
        kernel,
        [jax.ShapeDtypeStruct(term.shape, jnp.bfloat16) for term, _ in totals],
        [term for term, _ in totals] + [value for value, _ in pieces] + list(after),
        [VMEM] * (n + m) + [ANY] * len(after),
        name="sum_rows",
    )


def block_copies(block_refs, keys, rows, all_rows, sems):
    return [
        pltpu.make_async_copy(
            ref, all_rows.at[pl.ds(rel * rows + low, ref.shape[0]), :], sems.at[i]
        )
        for i, (ref, (rel, low)) in enumerate(zip(block_refs, keys))
    ]


def turned(values, cosine, sine):
    return values * cosine + pltpu.roll(values, HD // 2, 1) * sine


def project_into(rows_ref, weight_ref, out_ref, cos_ref=None, sin_ref=None):
    features = out_ref.shape[1]
    for low in range(0, features, CHUNK):
        high = min(low + CHUNK, features)
        values = jnp.dot(
            rows_ref[...], weight_ref[:, low:high], preferred_element_type=jnp.float32
        )
        for head in range(0, high - low, HD):
            piece = values[:, head : head + HD]
            if cos_ref is not None:
                piece = turned(piece, cos_ref[...], sin_ref[...])
            out_ref[:, low + head : low + head + HD] = piece.astype(jnp.bfloat16)


def project(blocks, weights, cosine, sine, rows, weight=1):
    keys = sorted(blocks)
    length, width = cosine.shape[0], blocks[0, 0].shape[1]
    features = weights[0].shape[1]
    n = len(keys)

    def kernel(*refs):
        block_refs, weight_refs = refs[:n], refs[n : n + 3]
        cos_ref, sin_ref = refs[n + 3 : n + 5]
        outs = refs[n + 5 : n + 8]
        all_rows, sems = refs[n + 8 :]
        copies = block_copies(block_refs, keys, rows, all_rows, sems)
        for copy in copies:
            copy.start()
        for copy in copies:
            copy.wait()
        for i in range(3):
            tables = (cos_ref, sin_ref) if i < 2 else ()
            project_into(all_rows, weight_refs[i], outs[i], *tables)

    return call(
        kernel,
        [jax.ShapeDtypeStruct((length, features), jnp.bfloat16)] * 3,
        [blocks[key] for key in keys] + list(weights) + [cosine, sine],
        [ANY] * n + [VMEM] * 5,
        [pltpu.VMEM((length, width), jnp.bfloat16), pltpu.SemaphoreType.DMA((n,))],
        flops=weight,
        vmem=20,
        name="project",
    )


def term_outs(rows, width, count, joined):
    bounds = part_bounds(rows, count)
    groups, waiting = messages_of(rows, count, joined)

    def shape(keys, dtype):
        height = sum(bounds[part][1] - bounds[part][0] for _, part in keys)
        return jax.ShapeDtypeStruct((height, width), dtype)

    return [shape(keys, jnp.bfloat16) for keys in groups] + [
        shape([key], jnp.float32) for key in waiting
    ]


def store_terms(values, low, refs, rows, count, joined):
    bounds = part_bounds(rows, count)
    groups, waiting = messages_of(rows, count, joined)
    for ref, keys in zip(refs, groups + [[key] for key in waiting]):
        at = 0
        for rel, part in keys:
            first, last = bounds[part]
            piece = values[rel * rows + first : rel * rows + last]
            ref[at : at + last - first, low : low + values.shape[1]] = piece.astype(ref.dtype)
            at += last - first


def backward_heads(blocks, qkv, weight, cosine, sine, rows):
    in_keys = sorted(blocks)
    length, width = cosine.shape[0], blocks[0, 0].shape[1]
    features = qkv[0].shape[1]
    n = len(in_keys)
    step = min(length, 512)

    def kernel(*refs):
        block_refs, weight_ref = refs[:n], refs[n]
        q_ref, k_ref, v_ref, cos_ref, sin_ref = refs[n + 1 : n + 6]
        d_qkv = refs[n + 6 : n + 9]
        all_rows, d_attn, sems = refs[n + 9 :]
        copies = block_copies(block_refs, in_keys, rows, all_rows, sems)
        for copy in copies:
            copy.start()
        for copy in copies:
            copy.wait()
        project_into(all_rows, weight_ref, d_attn)

        for head in range(features // HD):
            cols = slice(head * HD, (head + 1) * HD)
            key, value = k_ref[:, cols], v_ref[:, cols]
            d_key, d_value = 0.0, 0.0
            for low in range(0, length, step):
                part = slice(low, low + step)
                query, grad = q_ref[part, cols], d_attn[part, cols]
                scores = lax.dot_general(key, query, NT, preferred_element_type=jnp.float32)
                top = jnp.max(scores, 0, keepdims=True)
                raised = jnp.exp2((scores - top) * EXP2_SCALE)
                probs = raised * (1.0 / jnp.sum(raised, 0, keepdims=True))
                d_value += jnp.dot(
                    probs.astype(jnp.bfloat16), grad, preferred_element_type=jnp.float32
                )
                d_probs = lax.dot_general(value, grad, NT, preferred_element_type=jnp.float32)
                delta = jnp.sum(probs * d_probs, 0, keepdims=True)
                d_scores = (probs * (d_probs - delta) * HD ** (-0.5)).astype(jnp.bfloat16)
                d_key += jnp.dot(d_scores, query, preferred_element_type=jnp.float32)
                d_query = lax.dot_general(
                    key, d_scores, TN, preferred_element_type=jnp.float32
                ).T
                d_qkv[0][part, cols] = turned(
                    d_query, cos_ref[part, :], -sin_ref[part, :]
                ).astype(jnp.bfloat16)
            d_qkv[1][:, cols] = turned(d_key, cos_ref[...], -sin_ref[...]).astype(jnp.bfloat16)
            d_qkv[2][:, cols] = d_value.astype(jnp.bfloat16)

    return call(
        kernel,
        [jax.ShapeDtypeStruct((length, features), jnp.bfloat16)] * 3,
        [blocks[key] for key in in_keys] + [weight] + list(qkv) + [cosine, sine],
        [ANY] * n + [VMEM] * 6,
        [
            pltpu.VMEM((length, width), jnp.bfloat16),
            pltpu.VMEM((length, features), jnp.bfloat16),
            pltpu.SemaphoreType.DMA((n,)),
        ],
        vmem=28,
        flops=HEADS_WEIGHT,
        name="backward_heads",
    )


def backward_terms(d_qkv, weights, rows, count, joined, after=()):
    length, features = d_qkv[0].shape
    width = weights[0].shape[0]
    shapes = term_outs(rows, width, count, joined)

    def kernel(*refs):
        grads, weight_refs = refs[:3], refs[3:6]
        own_ref, *outs = refs[6 + len(after) :]
        for low in range(0, width, CHUNK):
            total = 0.0
            for i in range(3):
                total += lax.dot_general(
                    grads[i][...],
                    weight_refs[i][low : low + CHUNK, :],
                    NT,
                    preferred_element_type=jnp.float32,
                )
            own_ref[:, low : low + CHUNK] = total[:rows]
            store_terms(total, low, outs, rows, count, joined)

    own, *terms = call(
        kernel,
        [jax.ShapeDtypeStruct((rows, width), jnp.float32)] + shapes,
        list(d_qkv) + list(weights) + list(after),
        [VMEM] * 6 + [ANY] * len(after),
        vmem=24,
        flops=TERMS_WEIGHT,
        name="backward_terms",
    )
    return own, terms


def forward_terms(qkv, act_in, weight, rows, count, joined, after=()):
    length, features = qkv[0].shape
    width = weight.shape[0]
    shapes = term_outs(rows, width, count, joined)
    step = min(length, 512)

    def kernel(*refs):
        q_ref, k_ref, v_ref, act_ref, weight_ref = refs[:5]
        own_ref, *outs = refs[5 + len(after) : -1]
        attn = refs[-1]
        for head in range(features // HD):
            cols = slice(head * HD, (head + 1) * HD)
            for low in range(0, length, step):
                part = slice(low, low + step)
                scores = lax.dot_general(
                    q_ref[part, cols], k_ref[:, cols], NT, preferred_element_type=jnp.float32
                )
                top = jnp.max(scores, 1, keepdims=True)
                raised = jnp.exp2((scores - top) * EXP2_SCALE)
                total = jnp.sum(raised, 1, keepdims=True)
                mixed = jnp.dot(
                    raised.astype(jnp.bfloat16), v_ref[:, cols], preferred_element_type=jnp.float32
                )
                attn[part, cols] = (mixed * (1.0 / total)).astype(jnp.bfloat16)

        for low in range(0, width, CHUNK):
            total = lax.dot_general(
                attn[...], weight_ref[low : low + CHUNK, :], NT, preferred_element_type=jnp.float32
            )
            own = total[:rows] + act_ref[:, low : low + CHUNK]
            own_ref[:, low : low + CHUNK] = own.astype(jnp.bfloat16)
            store_terms(total, low, outs, rows, count, joined)

    own, *terms = call(
        kernel,
        [jax.ShapeDtypeStruct((rows, width), jnp.bfloat16)] + shapes,
        list(qkv) + [act_in, weight, *after],
        [VMEM] * 5 + [ANY] * len(after),
        [pltpu.VMEM((length, features), jnp.bfloat16)],
        vmem=24,
        flops=FORWARD_WEIGHT,
        name="forward_terms",
    )
    return own, terms


def input_grad(own, pieces, saved, grad, inv, gain, bounds, after=()):
    keys = sorted(pieces)

    def kernel(own_ref, saved_ref, grad_ref, inv_ref, gain_ref, *refs):
        out_ref = refs[-1]
        for part, (low, high) in enumerate(bounds):
            total = own_ref[low:high, :]
            for ref, key in zip(refs, keys):
                if key[1] == part:
                    first = pieces[key][1]
                    total = total + ref[first : first + high - low, :].astype(jnp.float32)
            total = total * gain_ref[...]
            saved_rows = saved_ref[low:high, :]
            mean = jnp.mean(saved_rows * total, -1, keepdims=True)
            inv_rows = inv_ref[low:high, :]
            out_ref[low:high, :] = (
                grad_ref[low:high, :]
                + inv_rows * total
                - saved_rows * (inv_rows * inv_rows * inv_rows * mean)
            ).astype(jnp.bfloat16)

    return call(
        kernel,
        [jax.ShapeDtypeStruct(own.shape, jnp.bfloat16)],
        [own, saved, grad, inv, gain] + [pieces[key][0] for key in keys] + list(after),
        [VMEM] * (5 + len(keys)) + [ANY] * len(after),
        flops=INPUT_GRAD_WEIGHT,
        name="input_grad",
    )[0]


def added_pieces(total, pieces, refs, part, height):
    for ref, (key, (_, first)) in zip(refs, pieces.items()):
        if key[1] == part:
            total = total + ref[first : first + height, :].astype(jnp.float32)
    return total


def activation_sum(base, pieces, bounds, after=()):
    def kernel(base_ref, *refs):
        for part, (low, high) in enumerate(bounds):
            total = base_ref[low:high, :].astype(jnp.float32)
            refs[-1][0, low:high, :] = added_pieces(total, pieces, refs, part, high - low)

    return call(
        kernel,
        [jax.ShapeDtypeStruct((1, *base.shape), jnp.float32)],
        [base] + [value for value, _ in pieces.values()] + list(after),
        [VMEM] * (1 + len(pieces)) + [ANY] * len(after),
        flops=LAST_SUM_WEIGHT,
        name="activation_sum",
    )[0]


def widened(values, base, pieces, bounds):
    def kernel(in_ref, base_ref, *refs):
        out_ref, sum_ref = refs[-2:]
        out_ref[0] = in_ref[...].astype(jnp.float32)
        for part, (low, high) in enumerate(bounds):
            total = base_ref[low:high, :].astype(jnp.float32)
            sum_ref[low:high, :] = added_pieces(total, pieces, refs, part, high - low)

    return call(
        kernel,
        [
            jax.ShapeDtypeStruct((1, *values.shape), jnp.float32),
            jax.ShapeDtypeStruct(base.shape, jnp.float32),
        ],
        [values, base] + [value for value, _ in pieces.values()],
        [VMEM] * (2 + len(pieces)),
        name="widen",
    )


def rope_tables(positions):
    half_dim = HD // 2
    inverse = 10000.0 ** (-(jnp.arange(half_dim).astype(jnp.float32) * 2.0 / HD))
    angles = positions.astype(jnp.float32)[:, None] * inverse[None, :]
    cosine, sine = jnp.cos(angles), jnp.sin(angles)
    return jnp.concatenate([cosine, cosine], 1), jnp.concatenate([-sine, sine], 1)


def shards(x_fwd, x_bwd, grad_in, gain, w_query, w_key, w_value, w_out):
    act_in, saved_in, grad = x_fwd[0], x_bwd[0], grad_in[0]
    rows = act_in.shape[0]
    count = lax.axis_size("seq")
    bounds = part_bounds(rows, count)
    own_query, own_key, own_value, own_out = w_query[0], w_key[0], w_value[0], w_out[0]

    block_of = lax.axis_index("seq") ^ jnp.arange(count)
    positions = (block_of[:, None] * rows + jnp.arange(rows)[None, :]).reshape(-1)
    cosine, sine = rope_tables(positions)

    whole = [(0, rows)]
    projections = (own_query, own_key, own_value)
    (normed_bwd,), inv_bwd = normed_rows(saved_in, gain, whole)
    grad_low = cast_rows(grad, [normed_bwd])
    all_bwd = gather_first(normed_bwd, "saved")
    all_grad = gather_first(grad_low, "grad")
    picked = picked_rows(second_hops(all_bwd, bounds), [grad_low])
    all_bwd = gather_rest(all_bwd, picked, bounds, "saved")
    picked = picked_rows(second_hops(all_grad, bounds), picked)
    all_grad = gather_rest(all_grad, picked, bounds, "grad")
    normed_fwd, _ = normed_rows(act_in, gain, bounds, picked)
    all_fwd = gather_parts({}, normed_fwd, bounds, True, "input")

    qkv = project(all_bwd, projections, cosine, sine, rows)
    handed_on = picked_rows([(value, 0, value.shape[0]) for value in normed_fwd], qkv[:1])
    all_fwd = gather_parts(all_fwd, handed_on, bounds, False, "input")
    d_qkv = backward_heads(all_grad, qkv, own_out, cosine, sine, rows)
    picked = picked_rows(second_hops(all_fwd, bounds), d_qkv[:1])
    all_fwd = gather_rest(all_fwd, picked, bounds, "input")
    d_own, d_terms = backward_terms(d_qkv, projections, rows, count, True, picked)
    qkv = project(all_fwd, projections, cosine, sine, rows, FORWARD_WEIGHT)
    own, terms = forward_terms(qkv, act_in, own_out, rows, count, False)

    back = Scatter(d_terms, rows, True, across, "grad")
    front = Scatter(
        terms, rows, False, lambda value, bit: across_and_on(value, 1 << bit), "branch"
    )
    back.send_groups(range(len(back.groups)))
    onward = front.onward()
    front.send_groups([i for i in range(len(front.groups)) if i not in onward])
    own = across_and_on(own, 0)
    soon = dict(front.final)
    sums = back.send_sums([terms[0]])
    held = picked_rows(
        [(front.leaving[i], 0, front.leaving[i].shape[0]) for i in onward], [own, *sums]
    )
    for i, value in zip(onward, held):
        front.leaving[i] = value
    front.send_groups(onward)
    d_input = input_grad(
        d_own,
        back.final,
        saved_in,
        grad,
        inv_bwd,
        gain,
        bounds,
        [value for value, _ in soon.values()],
    )
    front.send_sums([d_input])
    grad_prev, base = widened(passed_along(d_input, "pipe", -1), own, soon, bounds)
    last = {key: piece for key, piece in front.final.items() if key not in soon}
    return (activation_sum(base, last, bounds), grad_prev)


def solution(mesh):
    placed = (
        P("pipe", "seq", None),
        P("pipe", "seq", None),
        P("pipe", "seq", None),
        P("pipe", None),
        P("pipe", None, "seq"),
        P("pipe", None, "seq"),
        P("pipe", None, "seq"),
        P("pipe", None, "seq"),
    )
    return jax.shard_map(
        shards,
        mesh=mesh,
        in_specs=placed,
        out_specs=(P("pipe", "seq", None), P("pipe", "seq", None)),
        check_vma=False,
    )
```

```python
import functools
import math

import jax
import jax.numpy as jnp
from jax import lax
from jax.experimental import pallas as pl
from jax.experimental.pallas import tpu as pltpu
from jax.sharding import PartitionSpec as P

HD = 128
LANES = 128
CHUNK = 256
EXP2_SCALE = HD ** (-0.5) * math.log2(math.e)
NT = (((1,), (1,)), ((), ()))
TN = (((0,), (0,)), ((), ()))
HEADS_WEIGHT = 8_000_000_000
TERMS_WEIGHT = 3_000_000_000
INPUT_GRAD_WEIGHT = 8_000_000_000
LAST_SUM_WEIGHT = 8_000_000_000
FORWARD_WEIGHT = 5_000_000_000
MIB = 1024 * 1024


def bits_of(number):
    return [bit for bit in range(number.bit_length()) if (number >> bit) & 1]


def by_distance(count):
    return sorted(range(1, count), key=lambda rel: (len(bits_of(rel)), rel))


def part_bounds(rows, count):
    parts = 2 if count > 2 else 1
    return [(rows * i // parts, rows * (i + 1) // parts) for i in range(parts)]


def last_bit(rel, part):
    bits = bits_of(rel)
    return bits[part % len(bits)]


def ways_to(rel, bounds):
    ways = {}
    for part, (low, high) in enumerate(bounds):
        bit = last_bit(rel, part)
        ways[bit] = (min(low, ways.get(bit, (low, high))[0]), high)
    return [(bit, low, high) for bit, (low, high) in ways.items()]


def across(value, bit):
    count = lax.axis_size("seq")
    return lax.ppermute(value, "seq", [(i, i ^ (1 << bit)) for i in range(count)])


def across_and_on(value, flip):
    count, sections = lax.axis_size("seq"), lax.axis_size("pipe")
    pairs = [
        (p * count + i, (p + 1) % sections * count + (i ^ flip))
        for p in range(sections)
        for i in range(count)
    ]
    return lax.ppermute(value, ("pipe", "seq"), pairs)


def passed_along(value, axis, steps):
    count = lax.axis_size(axis)
    pairs = [(source, (source + steps) % count) for source in range(count)]
    return lax.ppermute(value, axis, pairs)


def onward_rows(count, bounds):
    return [
        (rel ^ (1 << bit), bit, low, high)
        for rel in by_distance(count)
        for bit, low, high in ways_to(rel, bounds)
    ]


def goes_on(rel, low, count, bounds):
    return any(
        rel == at and first <= low < last for at, _, first, last in onward_rows(count, bounds)
    )


def gather_first(own, what):
    count = lax.axis_size("seq")
    blocks = {(0, 0): own}
    for rel in by_distance(count):
        if len(bits_of(rel)) == 1:
            with jax.named_scope(f"gather_{what}_block{rel}"):
                blocks[rel, 0] = across(own, bits_of(rel)[0])
    return blocks


def gather_parts(blocks, own_parts, bounds, early, what):
    count = lax.axis_size("seq")
    for rel in by_distance(count):
        for value, (low, _) in zip(own_parts, bounds):
            blocks.setdefault((0, low), value)
            if len(bits_of(rel)) == 1 and goes_on(rel, low, count, bounds) == early:
                with jax.named_scope(f"gather_{what}_block{rel}_first{low}"):
                    blocks[rel, low] = across(value, bits_of(rel)[0])
    return blocks


def second_hops(blocks, bounds):
    hops = []
    for rel, _, low, high in onward_rows(lax.axis_size("seq"), bounds):
        if len(bits_of(rel)) == 1:
            first = low if (rel, low) in blocks else 0
            hops.append((blocks[rel, first], low - first, high - first))
    return hops


def gather_rest(blocks, picked, bounds, what):
    count = lax.axis_size("seq")
    picked = list(picked)
    for rel, bit, low, high in onward_rows(count, bounds):
        if rel == 0:
            continue
        value = picked.pop(0) if len(bits_of(rel)) == 1 else blocks[rel, low]
        if value.shape[0] > high - low:
            value = value[: high - low]
        with jax.named_scope(f"gather_{what}_block{rel ^ (1 << bit)}_row{low}"):
            blocks[rel ^ (1 << bit), low] = across(value, bit)
    return blocks


def messages_of(rows, count, joined):
    parts = range(len(part_bounds(rows, count)))
    later = {
        (rel ^ (1 << last_bit(rel, part)), part)
        for rel in range(1, count)
        for part in parts
        if len(bits_of(rel)) > 1
    }
    keys = [(rel, part) for rel in reversed(by_distance(count)) for part in parts]
    groups = {}
    for key in keys:
        if key not in later:
            groups.setdefault(last_bit(*key) if joined else key, []).append(key)
    return list(groups.values()), [key for key in keys if key in later]


class Scatter:

    def __init__(self, terms, rows, joined, send_last, what):
        count = lax.axis_size("seq")
        self.bounds = part_bounds(rows, count)
        self.groups, waiting = messages_of(rows, count, joined)
        self.leaving = list(terms[: len(self.groups)])
        self.waiting = dict(zip(waiting, terms[len(self.groups) :]))
        self.send_last, self.what = send_last, what
        self.arrived, self.final = {}, {}

    def send(self, value, keys):
        bit = last_bit(*keys[0])
        targets = [(rel ^ (1 << bit), part) for rel, part in keys]
        onward = any(rel for rel, _ in targets)
        with jax.named_scope(f"scatter_{self.what}_block{keys[0][0]}_part{keys[0][1]}"):
            moved = (across if onward else self.send_last)(value, bit)
        first = 0
        for key, target in zip(keys, targets):
            if target[0]:
                self.arrived.setdefault(target, []).append((moved, first))
            else:
                self.final[key] = (moved, first)
            first += self.bounds[key[1]][1] - self.bounds[key[1]][0]

    def onward(self):
        return [i for i, keys in enumerate(self.groups) if len(bits_of(keys[0][0])) > 1]

    def send_groups(self, places):
        for i in places:
            self.send(self.leaving[i], self.groups[i])

    def send_sums(self, after=()):
        sums = []
        for level in sorted({len(bits_of(rel)) for rel, _ in self.waiting}, reverse=True):
            keys = [key for key in self.waiting if len(bits_of(key[0])) == level]
            totals = [(self.waiting[key], self.arrived[key]) for key in keys]
            results = sum_rows(totals, after)
            sums += results
            for key, value in zip(keys, results):
                self.send(value, [key])
        return sums


def call(kernel, out_shapes, operands, in_specs, scratch=(), flops=1, vmem=10, name=None):
    return pl.pallas_call(
        kernel,
        out_shape=out_shapes,
        in_specs=in_specs,
        out_specs=[pl.BlockSpec(memory_space=pltpu.VMEM)] * len(out_shapes),
        scratch_shapes=list(scratch),
        compiler_params=pltpu.CompilerParams(vmem_limit_bytes=vmem * MIB),
        cost_estimate=pl.CostEstimate(flops=int(flops), bytes_accessed=1, transcendentals=0),
        name=name,
    )(*operands)


ANY = pl.BlockSpec(memory_space=pl.ANY)
HBM = pl.BlockSpec(memory_space=pltpu.HBM)
VMEM = pl.BlockSpec(memory_space=pltpu.VMEM)


def normed_rows(inputs, gain, bounds, after=(), vmem=10):
    rows, width = inputs.shape

    def kernel(x_any, gain_any, *refs):
        *outs, inv_ref, x_ref, gain_ref, sems = refs[len(after) :]
        copies = [
            pltpu.make_async_copy(source, held, sems.at[i])
            for i, (source, held) in enumerate([(x_any, x_ref), (gain_any, gain_ref)])
        ]
        for copy in copies:
            copy.start()
        for copy in copies:
            copy.wait()
        for out_ref, (low, high) in zip(outs, bounds):
            x = x_ref[low:high, :]
            inv = lax.rsqrt(jnp.mean(x * x, -1, keepdims=True) + 1e-05)
            out_ref[...] = (x * inv * gain_ref[...]).astype(jnp.bfloat16)
            inv_ref[low:high, :] = inv

    *parts, inv = call(
        kernel,
        [jax.ShapeDtypeStruct((high - low, width), jnp.bfloat16) for low, high in bounds]
        + [jax.ShapeDtypeStruct((rows, 1), jnp.float32)],
        [inputs, gain, *after],
        [HBM] * 2 + [ANY] * len(after),
        [
            pltpu.VMEM(inputs.shape, jnp.float32),
            pltpu.VMEM(gain.shape, jnp.float32),
            pltpu.SemaphoreType.DMA((2,)),
        ],
        vmem=vmem,
        name="norm",
    )
    return parts, inv


def picked_rows(pieces, after=()):
    n = len(pieces)

    def kernel(*refs):
        outs, sems = refs[n + len(after) : -1], refs[-1]
        copies = [
            pltpu.make_async_copy(ref.at[pl.ds(low, high - low), :], out_ref, sems.at[i])
            for i, (ref, out_ref, (_, low, high)) in enumerate(zip(refs, outs, pieces))
        ]
        for copy in copies:
            copy.start()
        for copy in copies:
            copy.wait()

    return call(
        kernel,
        [
            jax.ShapeDtypeStruct((high - low, value.shape[1]), value.dtype)
            for value, low, high in pieces
        ],
        [value for value, _, _ in pieces] + list(after),
        [ANY] * (n + len(after)),
        [pltpu.SemaphoreType.DMA((n,))],
        name="pick",
    )


def cast_rows(inputs, after=()):
    def kernel(x_ref, *refs):
        refs[len(after)][...] = x_ref[...].astype(jnp.bfloat16)

    return call(
        kernel,
        [jax.ShapeDtypeStruct(inputs.shape, jnp.bfloat16)],
        (inputs, *after),
        [VMEM] + [ANY] * len(after),
        name="cast",
    )[0]


def sum_rows(totals, after=()):
    pieces = [piece for _, pieces in totals for piece in pieces]
    n, m = len(totals), len(pieces)

    def kernel(*refs):
        arrivals, outs = list(refs[n : n + m]), refs[-n:]
        for (term, moved), term_ref, out_ref in zip(totals, refs, outs):
            total = term_ref[...]
            for _, first in moved:
                ref = arrivals.pop(0)
                total = total + ref[first : first + term.shape[0], :].astype(jnp.float32)
            out_ref[...] = total.astype(jnp.bfloat16)

    return call(
        kernel,
        [jax.ShapeDtypeStruct(term.shape, jnp.bfloat16) for term, _ in totals],
        [term for term, _ in totals] + [value for value, _ in pieces] + list(after),
        [VMEM] * (n + m) + [ANY] * len(after),
        name="sum_rows",
    )


def block_copies(block_refs, keys, rows, all_rows, sems):
    return [
        pltpu.make_async_copy(
            ref, all_rows.at[pl.ds(rel * rows + low, ref.shape[0]), :], sems.at[i]
        )
        for i, (ref, (rel, low)) in enumerate(zip(block_refs, keys))
    ]


def turned(values, cosine, sine):
    return values * cosine + pltpu.roll(values, HD // 2, 1) * sine


def project_into(rows_ref, weight_ref, out_ref, cos_ref=None, sin_ref=None):
    features = out_ref.shape[1]
    for low in range(0, features, CHUNK):
        high = min(low + CHUNK, features)
        values = jnp.dot(
            rows_ref[...], weight_ref[:, low:high], preferred_element_type=jnp.float32
        )
        for head in range(0, high - low, HD):
            piece = values[:, head : head + HD]
            if cos_ref is not None:
                piece = turned(piece, cos_ref[...], sin_ref[...])
            out_ref[:, low + head : low + head + HD] = piece.astype(jnp.bfloat16)


def project(blocks, weights, cosine, sine, rows, weight=1):
    keys = sorted(blocks)
    length, width = cosine.shape[0], blocks[0, 0].shape[1]
    features = weights[0].shape[1]
    n = len(keys)

    def kernel(*refs):
        block_refs, weight_refs = refs[:n], refs[n : n + 3]
        cos_ref, sin_ref = refs[n + 3 : n + 5]
        outs = refs[n + 5 : n + 8]
        all_rows, sems = refs[n + 8 :]
        copies = block_copies(block_refs, keys, rows, all_rows, sems)
        for copy in copies:
            copy.start()
        for copy in copies:
            copy.wait()
        for i in range(3):
            tables = (cos_ref, sin_ref) if i < 2 else ()
            project_into(all_rows, weight_refs[i], outs[i], *tables)

    return call(
        kernel,
        [jax.ShapeDtypeStruct((length, features), jnp.bfloat16)] * 3,
        [blocks[key] for key in keys] + list(weights) + [cosine, sine],
        [ANY] * n + [VMEM] * 5,
        [pltpu.VMEM((length, width), jnp.bfloat16), pltpu.SemaphoreType.DMA((n,))],
        flops=weight,
        vmem=20,
        name="project",
    )


def term_outs(rows, width, count, joined):
    bounds = part_bounds(rows, count)
    groups, waiting = messages_of(rows, count, joined)

    def shape(keys, dtype):
        height = sum(bounds[part][1] - bounds[part][0] for _, part in keys)
        return jax.ShapeDtypeStruct((height, width), dtype)

    return [shape(keys, jnp.bfloat16) for keys in groups] + [
        shape([key], jnp.float32) for key in waiting
    ]


def store_terms(values, low, refs, rows, count, joined):
    bounds = part_bounds(rows, count)
    groups, waiting = messages_of(rows, count, joined)
    for ref, keys in zip(refs, groups + [[key] for key in waiting]):
        at = 0
        for rel, part in keys:
            first, last = bounds[part]
            piece = values[rel * rows + first : rel * rows + last]
            ref[at : at + last - first, low : low + values.shape[1]] = piece.astype(ref.dtype)
            at += last - first


def backward_heads(blocks, qkv, weight, cosine, sine, rows):
    in_keys = sorted(blocks)
    length, width = cosine.shape[0], blocks[0, 0].shape[1]
    features = qkv[0].shape[1]
    n = len(in_keys)
    step = min(length, 512)

    def kernel(*refs):
        block_refs, weight_ref = refs[:n], refs[n]
        q_ref, k_ref, v_ref, cos_ref, sin_ref = refs[n + 1 : n + 6]
        d_qkv = refs[n + 6 : n + 9]
        all_rows, d_attn, sems = refs[n + 9 :]
        copies = block_copies(block_refs, in_keys, rows, all_rows, sems)
        for copy in copies:
            copy.start()
        for copy in copies:
            copy.wait()
        project_into(all_rows, weight_ref, d_attn)

        for head in range(features // HD):
            cols = slice(head * HD, (head + 1) * HD)
            key, value = k_ref[:, cols], v_ref[:, cols]
            d_key, d_value = 0.0, 0.0
            for low in range(0, length, step):
                part = slice(low, low + step)
                query, grad = q_ref[part, cols], d_attn[part, cols]
                scores = lax.dot_general(key, query, NT, preferred_element_type=jnp.float32)
                top = jnp.max(scores, 0, keepdims=True)
                raised = jnp.exp2((scores - top) * EXP2_SCALE)
                probs = raised * (1.0 / jnp.sum(raised, 0, keepdims=True))
                d_value += jnp.dot(
                    probs.astype(jnp.bfloat16), grad, preferred_element_type=jnp.float32
                )
                d_probs = lax.dot_general(value, grad, NT, preferred_element_type=jnp.float32)
                delta = jnp.sum(probs * d_probs, 0, keepdims=True)
                d_scores = (probs * (d_probs - delta) * HD ** (-0.5)).astype(jnp.bfloat16)
                d_key += jnp.dot(d_scores, query, preferred_element_type=jnp.float32)
                d_query = lax.dot_general(
                    key, d_scores, TN, preferred_element_type=jnp.float32
                ).T
                d_qkv[0][part, cols] = turned(
                    d_query, cos_ref[part, :], -sin_ref[part, :]
                ).astype(jnp.bfloat16)
            d_qkv[1][:, cols] = turned(d_key, cos_ref[...], -sin_ref[...]).astype(jnp.bfloat16)
            d_qkv[2][:, cols] = d_value.astype(jnp.bfloat16)

    return call(
        kernel,
        [jax.ShapeDtypeStruct((length, features), jnp.bfloat16)] * 3,
        [blocks[key] for key in in_keys] + [weight] + list(qkv) + [cosine, sine],
        [ANY] * n + [VMEM] * 6,
        [
            pltpu.VMEM((length, width), jnp.bfloat16),
            pltpu.VMEM((length, features), jnp.bfloat16),
            pltpu.SemaphoreType.DMA((n,)),
        ],
        vmem=28,
        flops=HEADS_WEIGHT,
        name="backward_heads",
    )


def backward_terms(d_qkv, weights, rows, count, joined, after=()):
    length, features = d_qkv[0].shape
    width = weights[0].shape[0]
    shapes = term_outs(rows, width, count, joined)

    def kernel(*refs):
        grads, weight_refs = refs[:3], refs[3:6]
        own_ref, *outs = refs[6 + len(after) :]
        for low in range(0, width, CHUNK):
            total = 0.0
            for i in range(3):
                total += lax.dot_general(
                    grads[i][...],
                    weight_refs[i][low : low + CHUNK, :],
                    NT,
                    preferred_element_type=jnp.float32,
                )
            own_ref[:, low : low + CHUNK] = total[:rows]
            store_terms(total, low, outs, rows, count, joined)

    own, *terms = call(
        kernel,
        [jax.ShapeDtypeStruct((rows, width), jnp.float32)] + shapes,
        list(d_qkv) + list(weights) + list(after),
        [VMEM] * 6 + [ANY] * len(after),
        vmem=24,
        flops=TERMS_WEIGHT,
        name="backward_terms",
    )
    return own, terms


def forward_terms(qkv, act_in, weight, rows, count, joined, after=()):
    length, features = qkv[0].shape
    width = weight.shape[0]
    shapes = term_outs(rows, width, count, joined)
    step = min(length, 512)

    def kernel(*refs):
        q_ref, k_ref, v_ref, act_ref, weight_ref = refs[:5]
        own_ref, *outs = refs[5 + len(after) : -1]
        attn = refs[-1]
        for head in range(features // HD):
            cols = slice(head * HD, (head + 1) * HD)
            for low in range(0, length, step):
                part = slice(low, low + step)
                scores = lax.dot_general(
                    q_ref[part, cols], k_ref[:, cols], NT, preferred_element_type=jnp.float32
                )
                top = jnp.max(scores, 1, keepdims=True)
                raised = jnp.exp2((scores - top) * EXP2_SCALE)
                total = jnp.sum(raised, 1, keepdims=True)
                mixed = jnp.dot(
                    raised.astype(jnp.bfloat16), v_ref[:, cols], preferred_element_type=jnp.float32
                )
                attn[part, cols] = (mixed * (1.0 / total)).astype(jnp.bfloat16)

        for low in range(0, width, CHUNK):
            total = lax.dot_general(
                attn[...], weight_ref[low : low + CHUNK, :], NT, preferred_element_type=jnp.float32
            )
            own = total[:rows] + act_ref[:, low : low + CHUNK]
            own_ref[:, low : low + CHUNK] = own.astype(jnp.bfloat16)
            store_terms(total, low, outs, rows, count, joined)

    own, *terms = call(
        kernel,
        [jax.ShapeDtypeStruct((rows, width), jnp.bfloat16)] + shapes,
        list(qkv) + [act_in, weight, *after],
        [VMEM] * 5 + [ANY] * len(after),
        [pltpu.VMEM((length, features), jnp.bfloat16)],
        vmem=24,
        flops=FORWARD_WEIGHT,
        name="forward_terms",
    )
    return own, terms


def input_grad(own, pieces, saved, grad, inv, gain, bounds, after=()):
    keys = sorted(pieces)

    def kernel(own_ref, saved_ref, grad_ref, inv_ref, gain_ref, *refs):
        out_ref = refs[-1]
        for part, (low, high) in enumerate(bounds):
            total = own_ref[low:high, :]
            for ref, key in zip(refs, keys):
                if key[1] == part:
                    first = pieces[key][1]
                    total = total + ref[first : first + high - low, :].astype(jnp.float32)
            total = total * gain_ref[...]
            saved_rows = saved_ref[low:high, :]
            mean = jnp.mean(saved_rows * total, -1, keepdims=True)
            inv_rows = inv_ref[low:high, :]
            out_ref[low:high, :] = (
                grad_ref[low:high, :]
                + inv_rows * total
                - saved_rows * (inv_rows * inv_rows * inv_rows * mean)
            ).astype(jnp.bfloat16)

    return call(
        kernel,
        [jax.ShapeDtypeStruct(own.shape, jnp.bfloat16)],
        [own, saved, grad, inv, gain] + [pieces[key][0] for key in keys] + list(after),
        [VMEM] * (5 + len(keys)) + [ANY] * len(after),
        flops=INPUT_GRAD_WEIGHT,
        name="input_grad",
    )[0]


def added_pieces(total, pieces, refs, part, height):
    for ref, (key, (_, first)) in zip(refs, pieces.items()):
        if key[1] == part:
            total = total + ref[first : first + height, :].astype(jnp.float32)
    return total


def activation_sum(base, pieces, bounds, after=()):
    def kernel(base_ref, *refs):
        for part, (low, high) in enumerate(bounds):
            total = base_ref[low:high, :].astype(jnp.float32)
            refs[-1][0, low:high, :] = added_pieces(total, pieces, refs, part, high - low)

    return call(
        kernel,
        [jax.ShapeDtypeStruct((1, *base.shape), jnp.float32)],
        [base] + [value for value, _ in pieces.values()] + list(after),
        [VMEM] * (1 + len(pieces)) + [ANY] * len(after),
        flops=LAST_SUM_WEIGHT,
        name="activation_sum",
    )[0]


def widened(values, base, pieces, bounds):
    def kernel(in_ref, base_ref, *refs):
        out_ref, sum_ref = refs[-2:]
        out_ref[0] = in_ref[...].astype(jnp.float32)
        for part, (low, high) in enumerate(bounds):
            total = base_ref[low:high, :].astype(jnp.float32)
            sum_ref[low:high, :] = added_pieces(total, pieces, refs, part, high - low)

    return call(
        kernel,
        [
            jax.ShapeDtypeStruct((1, *values.shape), jnp.float32),
            jax.ShapeDtypeStruct(base.shape, jnp.float32),
        ],
        [values, base] + [value for value, _ in pieces.values()],
        [VMEM] * (2 + len(pieces)),
        name="widen",
    )


def rope_tables(positions):
    half_dim = HD // 2
    inverse = 10000.0 ** (-(jnp.arange(half_dim).astype(jnp.float32) * 2.0 / HD))
    angles = positions.astype(jnp.float32)[:, None] * inverse[None, :]
    cosine, sine = jnp.cos(angles), jnp.sin(angles)
    return jnp.concatenate([cosine, cosine], 1), jnp.concatenate([-sine, sine], 1)


def shards(x_fwd, x_bwd, grad_in, gain, w_query, w_key, w_value, w_out):
    act_in, saved_in, grad = x_fwd[0], x_bwd[0], grad_in[0]
    rows = act_in.shape[0]
    count = lax.axis_size("seq")
    bounds = part_bounds(rows, count)
    own_query, own_key, own_value, own_out = w_query[0], w_key[0], w_value[0], w_out[0]

    block_of = lax.axis_index("seq") ^ jnp.arange(count)
    positions = (block_of[:, None] * rows + jnp.arange(rows)[None, :]).reshape(-1)
    cosine, sine = rope_tables(positions)

    whole = [(0, rows)]
    projections = (own_query, own_key, own_value)
    (normed_bwd,), inv_bwd = normed_rows(saved_in, gain, whole, vmem=62)
    grad_low = cast_rows(grad, [normed_bwd])
    all_bwd = gather_first(normed_bwd, "saved")
    all_grad = gather_first(grad_low, "grad")
    normed_fwd, _ = normed_rows(act_in, gain, bounds)
    picked = picked_rows(second_hops(all_bwd, bounds), [grad_low])
    all_bwd = gather_rest(all_bwd, picked, bounds, "saved")
    n = len(bounds)
    handed_on = [(value, 0, value.shape[0]) for value in normed_fwd]
    picked = picked_rows(handed_on + second_hops(all_grad, bounds), picked)
    all_fwd = gather_parts({}, picked[:n], bounds, True, "input")
    all_grad = gather_rest(all_grad, picked[n:], bounds, "grad")

    qkv = project(all_bwd, projections, cosine, sine, rows)
    all_fwd = gather_parts(all_fwd, picked_rows(handed_on, qkv[:1]), bounds, False, "input")
    d_qkv = backward_heads(all_grad, qkv, own_out, cosine, sine, rows)
    picked = picked_rows(second_hops(all_fwd, bounds), d_qkv[:1])
    all_fwd = gather_rest(all_fwd, picked, bounds, "input")
    d_own, d_terms = backward_terms(d_qkv, projections, rows, count, True, picked)
    qkv = project(all_fwd, projections, cosine, sine, rows, FORWARD_WEIGHT)
    own, terms = forward_terms(qkv, act_in, own_out, rows, count, False)

    back = Scatter(d_terms, rows, True, across, "grad")
    front = Scatter(
        terms, rows, False, lambda value, bit: across_and_on(value, 1 << bit), "branch"
    )
    back.send_groups(range(len(back.groups)))
    onward = front.onward()
    front.send_groups([i for i in range(len(front.groups)) if i not in onward])
    soon = dict(front.final)
    ready = [value for value, _ in soon.values()]
    sums = back.send_sums([terms[0]])
    held = picked_rows([(front.leaving[i], 0, front.leaving[i].shape[0]) for i in onward], sums)
    for i, value in zip(onward, held):
        front.leaving[i] = value
    front.send_groups(onward)
    (own,) = picked_rows([(own, 0, rows)], [*ready, *held])
    own = across_and_on(own, 0)
    d_input = input_grad(
        d_own,
        back.final,
        saved_in,
        grad,
        inv_bwd,
        gain,
        bounds,
        ready,
    )
    front.send_sums([d_input])
    grad_prev, base = widened(passed_along(d_input, "pipe", -1), own, soon, bounds)
    last = {key: piece for key, piece in front.final.items() if key not in soon}
    return (activation_sum(base, last, bounds), grad_prev)


def solution(mesh):
    placed = (
        P("pipe", "seq", None),
        P("pipe", "seq", None),
        P("pipe", "seq", None),
        P("pipe", None),
        P("pipe", None, "seq"),
        P("pipe", None, "seq"),
        P("pipe", None, "seq"),
        P("pipe", None, "seq"),
    )
    return jax.shard_map(
        shards,
        mesh=mesh,
        in_specs=placed,
        out_specs=(P("pipe", "seq", None), P("pipe", "seq", None)),
        check_vma=False,
    )
```

```python
import functools
import math

import jax
import jax.numpy as jnp
from jax import lax
from jax.experimental import pallas as pl
from jax.experimental.pallas import tpu as pltpu
from jax.sharding import PartitionSpec as P

HD = 128
LANES = 128
CHUNK = 256
EXP2_SCALE = HD ** (-0.5) * math.log2(math.e)
NT = (((1,), (1,)), ((), ()))
TN = (((0,), (0,)), ((), ()))
HEADS_WEIGHT = 8_000_000_000
TERMS_WEIGHT = 3_000_000_000
INPUT_GRAD_WEIGHT = 8_000_000_000
LAST_SUM_WEIGHT = 8_000_000_000
FORWARD_WEIGHT = 5_000_000_000
MIB = 1024 * 1024


def bits_of(number):
    return [bit for bit in range(number.bit_length()) if (number >> bit) & 1]


def by_distance(count):
    return sorted(range(1, count), key=lambda rel: (len(bits_of(rel)), rel))


def part_bounds(rows, count):
    parts = 2 if count > 2 else 1
    return [(rows * i // parts, rows * (i + 1) // parts) for i in range(parts)]


def last_bit(rel, part):
    bits = bits_of(rel)
    return bits[part % len(bits)]


def ways_to(rel, bounds):
    ways = {}
    for part, (low, high) in enumerate(bounds):
        bit = last_bit(rel, part)
        ways[bit] = (min(low, ways.get(bit, (low, high))[0]), high)
    return [(bit, low, high) for bit, (low, high) in ways.items()]


def across(value, bit):
    count = lax.axis_size("seq")
    return lax.ppermute(value, "seq", [(i, i ^ (1 << bit)) for i in range(count)])


def across_and_on(value, flip):
    count, sections = lax.axis_size("seq"), lax.axis_size("pipe")
    pairs = [
        (p * count + i, (p + 1) % sections * count + (i ^ flip))
        for p in range(sections)
        for i in range(count)
    ]
    return lax.ppermute(value, ("pipe", "seq"), pairs)


def passed_along(value, axis, steps):
    count = lax.axis_size(axis)
    pairs = [(source, (source + steps) % count) for source in range(count)]
    return lax.ppermute(value, axis, pairs)


def onward_rows(count, bounds):
    return [
        (rel ^ (1 << bit), bit, low, high)
        for rel in by_distance(count)
        for bit, low, high in ways_to(rel, bounds)
    ]


def goes_on(rel, low, count, bounds):
    return any(
        rel == at and first <= low < last for at, _, first, last in onward_rows(count, bounds)
    )


def gather_first(own, what):
    count = lax.axis_size("seq")
    blocks = {(0, 0): own}
    for rel in by_distance(count):
        if len(bits_of(rel)) == 1:
            with jax.named_scope(f"gather_{what}_block{rel}"):
                blocks[rel, 0] = across(own, bits_of(rel)[0])
    return blocks


def gather_parts(blocks, own_parts, bounds, early, what):
    count = lax.axis_size("seq")
    for rel in by_distance(count):
        for value, (low, _) in zip(own_parts, bounds):
            blocks.setdefault((0, low), value)
            if len(bits_of(rel)) == 1 and goes_on(rel, low, count, bounds) == early:
                with jax.named_scope(f"gather_{what}_block{rel}_first{low}"):
                    blocks[rel, low] = across(value, bits_of(rel)[0])
    return blocks


def second_hops(blocks, bounds):
    hops = []
    for rel, _, low, high in onward_rows(lax.axis_size("seq"), bounds):
        if len(bits_of(rel)) == 1:
            first = low if (rel, low) in blocks else 0
            hops.append((blocks[rel, first], low - first, high - first))
    return hops


def gather_rest(blocks, picked, bounds, what):
    count = lax.axis_size("seq")
    picked = list(picked)
    for rel, bit, low, high in onward_rows(count, bounds):
        if rel == 0:
            continue
        value = picked.pop(0) if len(bits_of(rel)) == 1 else blocks[rel, low]
        if value.shape[0] > high - low:
            value = value[: high - low]
        with jax.named_scope(f"gather_{what}_block{rel ^ (1 << bit)}_row{low}"):
            blocks[rel ^ (1 << bit), low] = across(value, bit)
    return blocks


def messages_of(rows, count, joined):
    parts = range(len(part_bounds(rows, count)))
    later = {
        (rel ^ (1 << last_bit(rel, part)), part)
        for rel in range(1, count)
        for part in parts
        if len(bits_of(rel)) > 1
    }
    groups, waiting = {}, {}
    for rel in reversed(by_distance(count)):
        for part in parts:
            key = (rel, part)
            if not joined and len(bits_of(rel)) == 1:
                waiting.setdefault(rel, []).append(key)
            elif key in later:
                waiting[key] = [key]
            else:
                groups.setdefault(last_bit(*key) if joined else key, []).append(key)
    return list(groups.values()), list(waiting.values())


class Scatter:

    def __init__(self, terms, rows, joined, send_last, what):
        count = lax.axis_size("seq")
        self.bounds = part_bounds(rows, count)
        self.groups, waiting = messages_of(rows, count, joined)
        self.leaving = list(terms[: len(self.groups)])
        self.waiting = list(zip(waiting, terms[len(self.groups) :]))
        self.send_last, self.what = send_last, what
        self.arrived, self.final = {}, {}

    def send(self, value, keys):
        bit = last_bit(*keys[0])
        targets = [(rel ^ (1 << bit), part) for rel, part in keys]
        onward = any(rel for rel, _ in targets)
        with jax.named_scope(f"scatter_{self.what}_block{keys[0][0]}_part{keys[0][1]}"):
            moved = (across if onward else self.send_last)(value, bit)
        first = 0
        for key, target in zip(keys, targets):
            if target[0]:
                self.arrived.setdefault(target, []).append((moved, first))
            else:
                self.final[key] = (moved, first)
            first += self.bounds[key[1]][1] - self.bounds[key[1]][0]

    def send_groups(self):
        for value, keys in zip(self.leaving, self.groups):
            self.send(value, keys)

    def send_sums(self, after=()):
        sums = []
        height = self.bounds[0][1] - self.bounds[0][0]
        levels = {len(bits_of(keys[0][0])) for keys, _ in self.waiting}
        for level in sorted(levels, reverse=True):
            found = [pair for pair in self.waiting if len(bits_of(pair[0][0][0])) == level]
            totals = [
                (term, [self.arrived.get(key, []) for key in keys]) for keys, term in found
            ]
            results = sum_rows(totals, height, after)
            sums += results
            for (keys, _), value in zip(found, results):
                self.send(value, keys)
        return sums


def call(kernel, out_shapes, operands, in_specs, scratch=(), flops=1, vmem=10, name=None):
    return pl.pallas_call(
        kernel,
        out_shape=out_shapes,
        in_specs=in_specs,
        out_specs=[pl.BlockSpec(memory_space=pltpu.VMEM)] * len(out_shapes),
        scratch_shapes=list(scratch),
        compiler_params=pltpu.CompilerParams(vmem_limit_bytes=vmem * MIB),
        cost_estimate=pl.CostEstimate(flops=int(flops), bytes_accessed=1, transcendentals=0),
        name=name,
    )(*operands)


ANY = pl.BlockSpec(memory_space=pl.ANY)
HBM = pl.BlockSpec(memory_space=pltpu.HBM)
VMEM = pl.BlockSpec(memory_space=pltpu.VMEM)


def normed_rows(inputs, gain, bounds, after=(), vmem=10):
    rows, width = inputs.shape

    def kernel(x_any, gain_any, *refs):
        *outs, inv_ref, x_ref, gain_ref, sems = refs[len(after) :]
        copies = [
            pltpu.make_async_copy(source, held, sems.at[i])
            for i, (source, held) in enumerate([(x_any, x_ref), (gain_any, gain_ref)])
        ]
        for copy in copies:
            copy.start()
        for copy in copies:
            copy.wait()
        for out_ref, (low, high) in zip(outs, bounds):
            x = x_ref[low:high, :]
            inv = lax.rsqrt(jnp.mean(x * x, -1, keepdims=True) + 1e-05)
            out_ref[...] = (x * inv * gain_ref[...]).astype(jnp.bfloat16)
            inv_ref[low:high, :] = inv

    *parts, inv = call(
        kernel,
        [jax.ShapeDtypeStruct((high - low, width), jnp.bfloat16) for low, high in bounds]
        + [jax.ShapeDtypeStruct((rows, 1), jnp.float32)],
        [inputs, gain, *after],
        [HBM] * 2 + [ANY] * len(after),
        [
            pltpu.VMEM(inputs.shape, jnp.float32),
            pltpu.VMEM(gain.shape, jnp.float32),
            pltpu.SemaphoreType.DMA((2,)),
        ],
        vmem=vmem,
        name="norm",
    )
    return parts, inv


def picked_rows(pieces, after=()):
    n = len(pieces)

    def kernel(*refs):
        outs, sems = refs[n + len(after) : -1], refs[-1]
        copies = [
            pltpu.make_async_copy(ref.at[pl.ds(low, high - low), :], out_ref, sems.at[i])
            for i, (ref, out_ref, (_, low, high)) in enumerate(zip(refs, outs, pieces))
        ]
        for copy in copies:
            copy.start()
        for copy in copies:
            copy.wait()

    return call(
        kernel,
        [
            jax.ShapeDtypeStruct((high - low, value.shape[1]), value.dtype)
            for value, low, high in pieces
        ],
        [value for value, _, _ in pieces] + list(after),
        [ANY] * (n + len(after)),
        [pltpu.SemaphoreType.DMA((n,))],
        name="pick",
    )


def cast_rows(inputs, after=()):
    def kernel(x_ref, *refs):
        refs[len(after)][...] = x_ref[...].astype(jnp.bfloat16)

    return call(
        kernel,
        [jax.ShapeDtypeStruct(inputs.shape, jnp.bfloat16)],
        (inputs, *after),
        [VMEM] + [ANY] * len(after),
        name="cast",
    )[0]


def sum_rows(totals, height, after=()):
    pieces = [piece for _, parts in totals for moved in parts for piece in moved]
    n, m = len(totals), len(pieces)

    def kernel(*refs):
        arrivals, outs = list(refs[n : n + m]), refs[-n:]
        for (_, parts), term_ref, out_ref in zip(totals, refs, outs):
            for i, moved in enumerate(parts):
                here = slice(i * height, (i + 1) * height)
                total = term_ref[here, :]
                for _, first in moved:
                    ref = arrivals.pop(0)
                    total = total + ref[first : first + height, :].astype(jnp.float32)
                out_ref[here, :] = total.astype(jnp.bfloat16)

    return call(
        kernel,
        [jax.ShapeDtypeStruct(term.shape, jnp.bfloat16) for term, _ in totals],
        [term for term, _ in totals] + [value for value, _ in pieces] + list(after),
        [VMEM] * (n + m) + [ANY] * len(after),
        name="sum_rows",
    )


def block_copies(block_refs, keys, rows, all_rows, sems):
    return [
        pltpu.make_async_copy(
            ref, all_rows.at[pl.ds(rel * rows + low, ref.shape[0]), :], sems.at[i]
        )
        for i, (ref, (rel, low)) in enumerate(zip(block_refs, keys))
    ]


def turned(values, cosine, sine):
    return values * cosine + pltpu.roll(values, HD // 2, 1) * sine


def project_into(rows_ref, weight_ref, out_ref, cos_ref=None, sin_ref=None):
    features = out_ref.shape[1]
    for low in range(0, features, CHUNK):
        high = min(low + CHUNK, features)
        values = jnp.dot(
            rows_ref[...], weight_ref[:, low:high], preferred_element_type=jnp.float32
        )
        for head in range(0, high - low, HD):
            piece = values[:, head : head + HD]
            if cos_ref is not None:
                piece = turned(piece, cos_ref[...], sin_ref[...])
            out_ref[:, low + head : low + head + HD] = piece.astype(jnp.bfloat16)


def project(blocks, weights, cosine, sine, rows, weight=1):
    keys = sorted(blocks)
    length, width = cosine.shape[0], blocks[0, 0].shape[1]
    features = weights[0].shape[1]
    n = len(keys)

    def kernel(*refs):
        block_refs, weight_refs = refs[:n], refs[n : n + 3]
        cos_ref, sin_ref = refs[n + 3 : n + 5]
        outs = refs[n + 5 : n + 8]
        all_rows, sems = refs[n + 8 :]
        copies = block_copies(block_refs, keys, rows, all_rows, sems)
        for copy in copies:
            copy.start()
        for copy in copies:
            copy.wait()
        for i in range(3):
            tables = (cos_ref, sin_ref) if i < 2 else ()
            project_into(all_rows, weight_refs[i], outs[i], *tables)

    return call(
        kernel,
        [jax.ShapeDtypeStruct((length, features), jnp.bfloat16)] * 3,
        [blocks[key] for key in keys] + list(weights) + [cosine, sine],
        [ANY] * n + [VMEM] * 5,
        [pltpu.VMEM((length, width), jnp.bfloat16), pltpu.SemaphoreType.DMA((n,))],
        flops=weight,
        vmem=20,
        name="project",
    )


def term_outs(rows, width, count, joined):
    bounds = part_bounds(rows, count)
    groups, waiting = messages_of(rows, count, joined)

    def shape(keys, dtype):
        height = sum(bounds[part][1] - bounds[part][0] for _, part in keys)
        return jax.ShapeDtypeStruct((height, width), dtype)

    return [shape(keys, jnp.bfloat16) for keys in groups] + [
        shape(keys, jnp.float32) for keys in waiting
    ]


def store_terms(values, low, refs, rows, count, joined):
    bounds = part_bounds(rows, count)
    groups, waiting = messages_of(rows, count, joined)
    for ref, keys in zip(refs, groups + waiting):
        at = 0
        for rel, part in keys:
            first, last = bounds[part]
            piece = values[rel * rows + first : rel * rows + last]
            ref[at : at + last - first, low : low + values.shape[1]] = piece.astype(ref.dtype)
            at += last - first


def backward_heads(blocks, qkv, weight, cosine, sine, rows):
    in_keys = sorted(blocks)
    length, width = cosine.shape[0], blocks[0, 0].shape[1]
    features = qkv[0].shape[1]
    n = len(in_keys)
    step = min(length, 512)

    def kernel(*refs):
        block_refs, weight_ref = refs[:n], refs[n]
        q_ref, k_ref, v_ref, cos_ref, sin_ref = refs[n + 1 : n + 6]
        d_qkv = refs[n + 6 : n + 9]
        all_rows, d_attn, sems = refs[n + 9 :]
        copies = block_copies(block_refs, in_keys, rows, all_rows, sems)
        for copy in copies:
            copy.start()
        for copy in copies:
            copy.wait()
        project_into(all_rows, weight_ref, d_attn)

        for head in range(features // HD):
            cols = slice(head * HD, (head + 1) * HD)
            key, value = k_ref[:, cols], v_ref[:, cols]
            d_key, d_value = 0.0, 0.0
            for low in range(0, length, step):
                part = slice(low, low + step)
                query, grad = q_ref[part, cols], d_attn[part, cols]
                scores = lax.dot_general(key, query, NT, preferred_element_type=jnp.float32)
                top = jnp.max(scores, 0, keepdims=True)
                raised = jnp.exp2((scores - top) * EXP2_SCALE)
                probs = raised * (1.0 / jnp.sum(raised, 0, keepdims=True))
                d_value += jnp.dot(
                    probs.astype(jnp.bfloat16), grad, preferred_element_type=jnp.float32
                )
                d_probs = lax.dot_general(value, grad, NT, preferred_element_type=jnp.float32)
                delta = jnp.sum(probs * d_probs, 0, keepdims=True)
                d_scores = (probs * (d_probs - delta) * HD ** (-0.5)).astype(jnp.bfloat16)
                d_key += jnp.dot(d_scores, query, preferred_element_type=jnp.float32)
                d_query = lax.dot_general(
                    key, d_scores, TN, preferred_element_type=jnp.float32
                ).T
                d_qkv[0][part, cols] = turned(
                    d_query, cos_ref[part, :], -sin_ref[part, :]
                ).astype(jnp.bfloat16)
            d_qkv[1][:, cols] = turned(d_key, cos_ref[...], -sin_ref[...]).astype(jnp.bfloat16)
            d_qkv[2][:, cols] = d_value.astype(jnp.bfloat16)

    return call(
        kernel,
        [jax.ShapeDtypeStruct((length, features), jnp.bfloat16)] * 3,
        [blocks[key] for key in in_keys] + [weight] + list(qkv) + [cosine, sine],
        [ANY] * n + [VMEM] * 6,
        [
            pltpu.VMEM((length, width), jnp.bfloat16),
            pltpu.VMEM((length, features), jnp.bfloat16),
            pltpu.SemaphoreType.DMA((n,)),
        ],
        vmem=28,
        flops=HEADS_WEIGHT,
        name="backward_heads",
    )


def backward_terms(d_qkv, weights, rows, count, joined, after=()):
    length, features = d_qkv[0].shape
    width = weights[0].shape[0]
    shapes = term_outs(rows, width, count, joined)

    def kernel(*refs):
        grads, weight_refs = refs[:3], refs[3:6]
        own_ref, *outs = refs[6 + len(after) :]
        for low in range(0, width, CHUNK):
            total = 0.0
            for i in range(3):
                total += lax.dot_general(
                    grads[i][...],
                    weight_refs[i][low : low + CHUNK, :],
                    NT,
                    preferred_element_type=jnp.float32,
                )
            own_ref[:, low : low + CHUNK] = total[:rows]
            store_terms(total, low, outs, rows, count, joined)

    own, *terms = call(
        kernel,
        [jax.ShapeDtypeStruct((rows, width), jnp.float32)] + shapes,
        list(d_qkv) + list(weights) + list(after),
        [VMEM] * 6 + [ANY] * len(after),
        vmem=24,
        flops=TERMS_WEIGHT,
        name="backward_terms",
    )
    return own, terms


def forward_terms(qkv, act_in, weight, rows, count, joined, after=()):
    length, features = qkv[0].shape
    width = weight.shape[0]
    shapes = term_outs(rows, width, count, joined)
    step = min(length, 512)

    def kernel(*refs):
        q_ref, k_ref, v_ref, act_ref, weight_ref = refs[:5]
        own_ref, *outs = refs[5 + len(after) : -1]
        attn = refs[-1]
        for head in range(features // HD):
            cols = slice(head * HD, (head + 1) * HD)
            for low in range(0, length, step):
                part = slice(low, low + step)
                scores = lax.dot_general(
                    q_ref[part, cols], k_ref[:, cols], NT, preferred_element_type=jnp.float32
                )
                top = jnp.max(scores, 1, keepdims=True)
                raised = jnp.exp2((scores - top) * EXP2_SCALE)
                total = jnp.sum(raised, 1, keepdims=True)
                mixed = jnp.dot(
                    raised.astype(jnp.bfloat16), v_ref[:, cols], preferred_element_type=jnp.float32
                )
                attn[part, cols] = (mixed * (1.0 / total)).astype(jnp.bfloat16)

        for low in range(0, width, CHUNK):
            total = lax.dot_general(
                attn[...], weight_ref[low : low + CHUNK, :], NT, preferred_element_type=jnp.float32
            )
            own = total[:rows] + act_ref[:, low : low + CHUNK]
            own_ref[:, low : low + CHUNK] = own.astype(jnp.bfloat16)
            store_terms(total, low, outs, rows, count, joined)

    own, *terms = call(
        kernel,
        [jax.ShapeDtypeStruct((rows, width), jnp.bfloat16)] + shapes,
        list(qkv) + [act_in, weight, *after],
        [VMEM] * 5 + [ANY] * len(after),
        [pltpu.VMEM((length, features), jnp.bfloat16)],
        vmem=24,
        flops=FORWARD_WEIGHT,
        name="forward_terms",
    )
    return own, terms


def input_grad(own, pieces, saved, grad, inv, gain, bounds, after=()):
    keys = sorted(pieces)

    def kernel(own_ref, saved_ref, grad_ref, inv_ref, gain_ref, *refs):
        out_ref = refs[-1]
        for part, (low, high) in enumerate(bounds):
            total = own_ref[low:high, :]
            for ref, key in zip(refs, keys):
                if key[1] == part:
                    first = pieces[key][1]
                    total = total + ref[first : first + high - low, :].astype(jnp.float32)
            total = total * gain_ref[...]
            saved_rows = saved_ref[low:high, :]
            mean = jnp.mean(saved_rows * total, -1, keepdims=True)
            inv_rows = inv_ref[low:high, :]
            out_ref[low:high, :] = (
                grad_ref[low:high, :]
                + inv_rows * total
                - saved_rows * (inv_rows * inv_rows * inv_rows * mean)
            ).astype(jnp.bfloat16)

    return call(
        kernel,
        [jax.ShapeDtypeStruct(own.shape, jnp.bfloat16)],
        [own, saved, grad, inv, gain] + [pieces[key][0] for key in keys] + list(after),
        [VMEM] * (5 + len(keys)) + [ANY] * len(after),
        flops=INPUT_GRAD_WEIGHT,
        name="input_grad",
    )[0]


def added_pieces(total, pieces, refs, part, height):
    for ref, (key, (_, first)) in zip(refs, pieces.items()):
        if key[1] == part:
            total = total + ref[first : first + height, :].astype(jnp.float32)
    return total


def activation_sum(base, pieces, bounds, after=()):
    def kernel(base_ref, *refs):
        for part, (low, high) in enumerate(bounds):
            total = base_ref[low:high, :].astype(jnp.float32)
            refs[-1][0, low:high, :] = added_pieces(total, pieces, refs, part, high - low)

    return call(
        kernel,
        [jax.ShapeDtypeStruct((1, *base.shape), jnp.float32)],
        [base] + [value for value, _ in pieces.values()] + list(after),
        [VMEM] * (1 + len(pieces)) + [ANY] * len(after),
        flops=LAST_SUM_WEIGHT,
        name="activation_sum",
    )[0]


def widened(values, after=()):
    def kernel(in_ref, *refs):
        refs[-1][0] = in_ref[...].astype(jnp.float32)

    return call(
        kernel,
        [jax.ShapeDtypeStruct((1, *values.shape), jnp.float32)],
        [values, *after],
        [VMEM] + [ANY] * len(after),
        name="widen",
    )[0]


def rope_tables(positions):
    half_dim = HD // 2
    inverse = 10000.0 ** (-(jnp.arange(half_dim).astype(jnp.float32) * 2.0 / HD))
    angles = positions.astype(jnp.float32)[:, None] * inverse[None, :]
    cosine, sine = jnp.cos(angles), jnp.sin(angles)
    return jnp.concatenate([cosine, cosine], 1), jnp.concatenate([-sine, sine], 1)


def shards(x_fwd, x_bwd, grad_in, gain, w_query, w_key, w_value, w_out):
    act_in, saved_in, grad = x_fwd[0], x_bwd[0], grad_in[0]
    rows = act_in.shape[0]
    count = lax.axis_size("seq")
    bounds = part_bounds(rows, count)
    own_query, own_key, own_value, own_out = w_query[0], w_key[0], w_value[0], w_out[0]

    block_of = lax.axis_index("seq") ^ jnp.arange(count)
    positions = (block_of[:, None] * rows + jnp.arange(rows)[None, :]).reshape(-1)
    cosine, sine = rope_tables(positions)

    whole = [(0, rows)]
    projections = (own_query, own_key, own_value)
    (normed_bwd,), inv_bwd = normed_rows(saved_in, gain, whole, vmem=62)
    grad_low = cast_rows(grad, [normed_bwd])
    all_bwd = gather_first(normed_bwd, "saved")
    all_grad = gather_first(grad_low, "grad")
    normed_fwd, _ = normed_rows(act_in, gain, bounds)
    picked = picked_rows(second_hops(all_bwd, bounds), [grad_low])
    all_bwd = gather_rest(all_bwd, picked, bounds, "saved")
    n = len(bounds)
    handed_on = [(value, 0, value.shape[0]) for value in normed_fwd]
    picked = picked_rows(handed_on + second_hops(all_grad, bounds), picked)
    all_fwd = gather_parts({}, picked[:n], bounds, True, "input")
    all_grad = gather_rest(all_grad, picked[n:], bounds, "grad")

    qkv = project(all_bwd, projections, cosine, sine, rows)
    all_fwd = gather_parts(all_fwd, picked_rows(handed_on, qkv[:1]), bounds, False, "input")
    d_qkv = backward_heads(all_grad, qkv, own_out, cosine, sine, rows)
    picked = picked_rows(second_hops(all_fwd, bounds), d_qkv[:1])
    all_fwd = gather_rest(all_fwd, picked, bounds, "input")
    d_own, d_terms = backward_terms(d_qkv, projections, rows, count, True, picked)
    qkv = project(all_fwd, projections, cosine, sine, rows, FORWARD_WEIGHT)
    own, terms = forward_terms(qkv, act_in, own_out, rows, count, False)

    back = Scatter(d_terms, rows, True, across, "grad")
    front = Scatter(
        terms, rows, False, lambda value, bit: across_and_on(value, 1 << bit), "branch"
    )
    back.send_groups()
    front.send_groups()
    own = across_and_on(own, 0)
    d_sums = back.send_sums([terms[0]])
    sums = front.send_sums(d_sums)
    d_input = input_grad(
        d_own, back.final, saved_in, grad, inv_bwd, gain, bounds, [own, *sums]
    )
    act_next = activation_sum(own, front.final, bounds)
    return (act_next, widened(passed_along(d_input, "pipe", -1), [act_next]))


def solution(mesh):
    placed = (
        P("pipe", "seq", None),
        P("pipe", "seq", None),
        P("pipe", "seq", None),
        P("pipe", None),
        P("pipe", None, "seq"),
        P("pipe", None, "seq"),
        P("pipe", None, "seq"),
        P("pipe", None, "seq"),
    )
    return jax.shard_map(
        shards,
        mesh=mesh,
        in_specs=placed,
        out_specs=(P("pipe", "seq", None), P("pipe", "seq", None)),
        check_vma=False,
    )
```

```python
import functools
import math

import jax
import jax.numpy as jnp
from jax import lax
from jax.experimental import pallas as pl
from jax.experimental.pallas import tpu as pltpu
from jax.sharding import PartitionSpec as P

HD = 128
LANES = 128
CHUNK = 256
EXP2_SCALE = HD ** (-0.5) * math.log2(math.e)
NT = (((1,), (1,)), ((), ()))
TN = (((0,), (0,)), ((), ()))
HEADS_WEIGHT = 8_000_000_000
TERMS_WEIGHT = 3_000_000_000
INPUT_GRAD_WEIGHT = 8_000_000_000
LAST_SUM_WEIGHT = 8_000_000_000
FORWARD_WEIGHT = 5_000_000_000
MIB = 1024 * 1024


def bits_of(number):
    return [bit for bit in range(number.bit_length()) if (number >> bit) & 1]


def by_distance(count):
    return sorted(range(1, count), key=lambda rel: (len(bits_of(rel)), rel))


def part_bounds(rows, count):
    parts = 2 if count > 2 else 1
    return [(rows * i // parts, rows * (i + 1) // parts) for i in range(parts)]


def last_bit(rel, part):
    bits = bits_of(rel)
    return bits[part % len(bits)]


def ways_to(rel, bounds):
    ways = {}
    for part, (low, high) in enumerate(bounds):
        bit = last_bit(rel, part)
        ways[bit] = (min(low, ways.get(bit, (low, high))[0]), high)
    return [(bit, low, high) for bit, (low, high) in ways.items()]


def across(value, bit):
    count = lax.axis_size("seq")
    return lax.ppermute(value, "seq", [(i, i ^ (1 << bit)) for i in range(count)])


def across_and_on(value, flip):
    count, sections = lax.axis_size("seq"), lax.axis_size("pipe")
    pairs = [
        (p * count + i, (p + 1) % sections * count + (i ^ flip))
        for p in range(sections)
        for i in range(count)
    ]
    return lax.ppermute(value, ("pipe", "seq"), pairs)


def passed_along(value, axis, steps):
    count = lax.axis_size(axis)
    pairs = [(source, (source + steps) % count) for source in range(count)]
    return lax.ppermute(value, axis, pairs)


def onward_rows(count, bounds):
    return [
        (rel ^ (1 << bit), bit, low, high)
        for rel in by_distance(count)
        for bit, low, high in ways_to(rel, bounds)
    ]


def goes_on(rel, low, count, bounds):
    return any(
        rel == at and first <= low < last for at, _, first, last in onward_rows(count, bounds)
    )


def gather_first(own, what):
    count = lax.axis_size("seq")
    blocks = {(0, 0): own}
    for rel in by_distance(count):
        if len(bits_of(rel)) == 1:
            with jax.named_scope(f"gather_{what}_block{rel}"):
                blocks[rel, 0] = across(own, bits_of(rel)[0])
    return blocks


def gather_parts(blocks, own_parts, bounds, early, what):
    count = lax.axis_size("seq")
    for rel in by_distance(count):
        for value, (low, _) in zip(own_parts, bounds):
            blocks.setdefault((0, low), value)
            if len(bits_of(rel)) == 1 and goes_on(rel, low, count, bounds) == early:
                with jax.named_scope(f"gather_{what}_block{rel}_first{low}"):
                    blocks[rel, low] = across(value, bits_of(rel)[0])
    return blocks


def second_hops(blocks, bounds):
    hops = []
    for rel, _, low, high in onward_rows(lax.axis_size("seq"), bounds):
        if len(bits_of(rel)) == 1:
            first = low if (rel, low) in blocks else 0
            hops.append((blocks[rel, first], low - first, high - first))
    return hops


def gather_rest(blocks, picked, bounds, what):
    count = lax.axis_size("seq")
    picked = list(picked)
    for rel, bit, low, high in onward_rows(count, bounds):
        if rel == 0:
            continue
        value = picked.pop(0) if len(bits_of(rel)) == 1 else blocks[rel, low]
        if value.shape[0] > high - low:
            value = value[: high - low]
        with jax.named_scope(f"gather_{what}_block{rel ^ (1 << bit)}_row{low}"):
            blocks[rel ^ (1 << bit), low] = across(value, bit)
    return blocks


def messages_of(rows, count, joined):
    parts = range(len(part_bounds(rows, count)))
    later = {
        (rel ^ (1 << last_bit(rel, part)), part)
        for rel in range(1, count)
        for part in parts
        if len(bits_of(rel)) > 1
    }
    groups, waiting = {}, {}
    for rel in reversed(by_distance(count)):
        for part in parts:
            key = (rel, part)
            if not joined and len(bits_of(rel)) == 1:
                waiting.setdefault(rel, []).append(key)
            elif key in later:
                waiting[key] = [key]
            else:
                groups.setdefault(last_bit(*key) if joined else key, []).append(key)
    return list(groups.values()), list(waiting.values())


class Scatter:

    def __init__(self, terms, rows, joined, send_last, what):
        count = lax.axis_size("seq")
        self.bounds = part_bounds(rows, count)
        self.groups, waiting = messages_of(rows, count, joined)
        self.leaving = list(terms[: len(self.groups)])
        self.waiting = list(zip(waiting, terms[len(self.groups) :]))
        self.send_last, self.what = send_last, what
        self.arrived, self.final = {}, {}

    def send(self, value, keys):
        bit = last_bit(*keys[0])
        targets = [(rel ^ (1 << bit), part) for rel, part in keys]
        onward = any(rel for rel, _ in targets)
        with jax.named_scope(f"scatter_{self.what}_block{keys[0][0]}_part{keys[0][1]}"):
            moved = (across if onward else self.send_last)(value, bit)
        first = 0
        for key, target in zip(keys, targets):
            if target[0]:
                self.arrived.setdefault(target, []).append((moved, first))
            else:
                self.final[key] = (moved, first)
            first += self.bounds[key[1]][1] - self.bounds[key[1]][0]

    def send_groups(self):
        for value, keys in zip(self.leaving, self.groups):
            self.send(value, keys)

    def send_sums(self, after=()):
        sums = []
        height = self.bounds[0][1] - self.bounds[0][0]
        levels = {len(bits_of(keys[0][0])) for keys, _ in self.waiting}
        for level in sorted(levels, reverse=True):
            found = [pair for pair in self.waiting if len(bits_of(pair[0][0][0])) == level]
            totals = [
                (term, [self.arrived.get(key, []) for key in keys]) for keys, term in found
            ]
            results = sum_rows(totals, height, after)
            sums += results
            for (keys, _), value in zip(found, results):
                self.send(value, keys)
        return sums


def call(kernel, out_shapes, operands, in_specs, scratch=(), flops=1, vmem=10, name=None):
    return pl.pallas_call(
        kernel,
        out_shape=out_shapes,
        in_specs=in_specs,
        out_specs=[pl.BlockSpec(memory_space=pltpu.VMEM)] * len(out_shapes),
        scratch_shapes=list(scratch),
        compiler_params=pltpu.CompilerParams(vmem_limit_bytes=vmem * MIB),
        cost_estimate=pl.CostEstimate(flops=int(flops), bytes_accessed=1, transcendentals=0),
        name=name,
    )(*operands)


ANY = pl.BlockSpec(memory_space=pl.ANY)
HBM = pl.BlockSpec(memory_space=pltpu.HBM)
VMEM = pl.BlockSpec(memory_space=pltpu.VMEM)


def normed_rows(inputs, gain, bounds, after=(), vmem=10):
    rows, width = inputs.shape

    def kernel(x_any, gain_any, *refs):
        *outs, inv_ref, x_ref, gain_ref, sems = refs[len(after) :]
        copies = [
            pltpu.make_async_copy(source, held, sems.at[i])
            for i, (source, held) in enumerate([(x_any, x_ref), (gain_any, gain_ref)])
        ]
        for copy in copies:
            copy.start()
        for copy in copies:
            copy.wait()
        for out_ref, (low, high) in zip(outs, bounds):
            x = x_ref[low:high, :]
            inv = lax.rsqrt(jnp.mean(x * x, -1, keepdims=True) + 1e-05)
            out_ref[...] = (x * inv * gain_ref[...]).astype(jnp.bfloat16)
            inv_ref[low:high, :] = inv

    *parts, inv = call(
        kernel,
        [jax.ShapeDtypeStruct((high - low, width), jnp.bfloat16) for low, high in bounds]
        + [jax.ShapeDtypeStruct((rows, 1), jnp.float32)],
        [inputs, gain, *after],
        [HBM] * 2 + [ANY] * len(after),
        [
            pltpu.VMEM(inputs.shape, jnp.float32),
            pltpu.VMEM(gain.shape, jnp.float32),
            pltpu.SemaphoreType.DMA((2,)),
        ],
        vmem=vmem,
        name="norm",
    )
    return parts, inv


def picked_rows(pieces, after=()):
    n = len(pieces)

    def kernel(*refs):
        outs, sems = refs[n + len(after) : -1], refs[-1]
        copies = [
            pltpu.make_async_copy(ref.at[pl.ds(low, high - low), :], out_ref, sems.at[i])
            for i, (ref, out_ref, (_, low, high)) in enumerate(zip(refs, outs, pieces))
        ]
        for copy in copies:
            copy.start()
        for copy in copies:
            copy.wait()

    return call(
        kernel,
        [
            jax.ShapeDtypeStruct((high - low, value.shape[1]), value.dtype)
            for value, low, high in pieces
        ],
        [value for value, _, _ in pieces] + list(after),
        [ANY] * (n + len(after)),
        [pltpu.SemaphoreType.DMA((n,))],
        name="pick",
    )


def cast_rows(inputs, after=()):
    def kernel(x_ref, *refs):
        refs[len(after)][...] = x_ref[...].astype(jnp.bfloat16)

    return call(
        kernel,
        [jax.ShapeDtypeStruct(inputs.shape, jnp.bfloat16)],
        (inputs, *after),
        [VMEM] + [ANY] * len(after),
        name="cast",
    )[0]


def sum_rows(totals, height, after=()):
    pieces = [piece for _, parts in totals for moved in parts for piece in moved]
    n, m = len(totals), len(pieces)

    def kernel(*refs):
        arrivals, outs = list(refs[n : n + m]), refs[-n:]
        for (_, parts), term_ref, out_ref in zip(totals, refs, outs):
            for i, moved in enumerate(parts):
                here = slice(i * height, (i + 1) * height)
                total = term_ref[here, :]
                for _, first in moved:
                    ref = arrivals.pop(0)
                    total = total + ref[first : first + height, :].astype(jnp.float32)
                out_ref[here, :] = total.astype(jnp.bfloat16)

    return call(
        kernel,
        [jax.ShapeDtypeStruct(term.shape, jnp.bfloat16) for term, _ in totals],
        [term for term, _ in totals] + [value for value, _ in pieces] + list(after),
        [VMEM] * (n + m) + [ANY] * len(after),
        name="sum_rows",
    )


def block_copies(block_refs, keys, rows, all_rows, sems):
    return [
        pltpu.make_async_copy(
            ref, all_rows.at[pl.ds(rel * rows + low, ref.shape[0]), :], sems.at[i]
        )
        for i, (ref, (rel, low)) in enumerate(zip(block_refs, keys))
    ]


def turned(values, cosine, sine):
    return values * cosine + pltpu.roll(values, HD // 2, 1) * sine


def project_into(rows_ref, weight_ref, out_ref, cos_ref=None, sin_ref=None):
    features = out_ref.shape[1]
    for low in range(0, features, CHUNK):
        high = min(low + CHUNK, features)
        values = jnp.dot(
            rows_ref[...], weight_ref[:, low:high], preferred_element_type=jnp.float32
        )
        for head in range(0, high - low, HD):
            piece = values[:, head : head + HD]
            if cos_ref is not None:
                piece = turned(piece, cos_ref[...], sin_ref[...])
            out_ref[:, low + head : low + head + HD] = piece.astype(jnp.bfloat16)


def project(blocks, weights, cosine, sine, rows, weight=1):
    keys = sorted(blocks)
    length, width = cosine.shape[0], blocks[0, 0].shape[1]
    features = weights[0].shape[1]
    n = len(keys)

    def kernel(*refs):
        block_refs, weight_refs = refs[:n], refs[n : n + 3]
        cos_ref, sin_ref = refs[n + 3 : n + 5]
        outs = refs[n + 5 : n + 8]
        all_rows, sems = refs[n + 8 :]
        copies = block_copies(block_refs, keys, rows, all_rows, sems)
        for copy in copies:
            copy.start()
        for copy in copies:
            copy.wait()
        for i in range(3):
            tables = (cos_ref, sin_ref) if i < 2 else ()
            project_into(all_rows, weight_refs[i], outs[i], *tables)

    return call(
        kernel,
        [jax.ShapeDtypeStruct((length, features), jnp.bfloat16)] * 3,
        [blocks[key] for key in keys] + list(weights) + [cosine, sine],
        [ANY] * n + [VMEM] * 5,
        [pltpu.VMEM((length, width), jnp.bfloat16), pltpu.SemaphoreType.DMA((n,))],
        flops=weight,
        vmem=20,
        name="project",
    )


def term_outs(rows, width, count, joined):
    bounds = part_bounds(rows, count)
    groups, waiting = messages_of(rows, count, joined)

    def shape(keys, dtype):
        height = sum(bounds[part][1] - bounds[part][0] for _, part in keys)
        return jax.ShapeDtypeStruct((height, width), dtype)

    return [shape(keys, jnp.bfloat16) for keys in groups] + [
        shape(keys, jnp.float32) for keys in waiting
    ]


def store_terms(values, low, refs, rows, count, joined):
    bounds = part_bounds(rows, count)
    groups, waiting = messages_of(rows, count, joined)
    for ref, keys in zip(refs, groups + waiting):
        at = 0
        for rel, part in keys:
            first, last = bounds[part]
            piece = values[rel * rows + first : rel * rows + last]
            ref[at : at + last - first, low : low + values.shape[1]] = piece.astype(ref.dtype)
            at += last - first


def backward_heads(blocks, qkv, weight, cosine, sine, rows):
    in_keys = sorted(blocks)
    length, width = cosine.shape[0], blocks[0, 0].shape[1]
    features = qkv[0].shape[1]
    n = len(in_keys)
    step = min(length, 512)

    def kernel(*refs):
        block_refs, weight_ref = refs[:n], refs[n]
        q_ref, k_ref, v_ref, cos_ref, sin_ref = refs[n + 1 : n + 6]
        d_qkv = refs[n + 6 : n + 9]
        all_rows, d_attn, sems = refs[n + 9 :]
        copies = block_copies(block_refs, in_keys, rows, all_rows, sems)
        for copy in copies:
            copy.start()
        for copy in copies:
            copy.wait()
        project_into(all_rows, weight_ref, d_attn)

        for head in range(features // HD):
            cols = slice(head * HD, (head + 1) * HD)
            key, value = k_ref[:, cols], v_ref[:, cols]
            d_key, d_value = 0.0, 0.0
            for low in range(0, length, step):
                part = slice(low, low + step)
                query, grad = q_ref[part, cols], d_attn[part, cols]
                scores = lax.dot_general(key, query, NT, preferred_element_type=jnp.float32)
                top = jnp.max(scores, 0, keepdims=True)
                raised = jnp.exp2((scores - top) * EXP2_SCALE)
                probs = raised * (1.0 / jnp.sum(raised, 0, keepdims=True))
                d_value += jnp.dot(
                    probs.astype(jnp.bfloat16), grad, preferred_element_type=jnp.float32
                )
                d_probs = lax.dot_general(value, grad, NT, preferred_element_type=jnp.float32)
                delta = jnp.sum(probs * d_probs, 0, keepdims=True)
                d_scores = (probs * (d_probs - delta) * HD ** (-0.5)).astype(jnp.bfloat16)
                d_key += jnp.dot(d_scores, query, preferred_element_type=jnp.float32)
                d_query = lax.dot_general(
                    key, d_scores, TN, preferred_element_type=jnp.float32
                ).T
                d_qkv[0][part, cols] = turned(
                    d_query, cos_ref[part, :], -sin_ref[part, :]
                ).astype(jnp.bfloat16)
            d_qkv[1][:, cols] = turned(d_key, cos_ref[...], -sin_ref[...]).astype(jnp.bfloat16)
            d_qkv[2][:, cols] = d_value.astype(jnp.bfloat16)

    return call(
        kernel,
        [jax.ShapeDtypeStruct((length, features), jnp.bfloat16)] * 3,
        [blocks[key] for key in in_keys] + [weight] + list(qkv) + [cosine, sine],
        [ANY] * n + [VMEM] * 6,
        [
            pltpu.VMEM((length, width), jnp.bfloat16),
            pltpu.VMEM((length, features), jnp.bfloat16),
            pltpu.SemaphoreType.DMA((n,)),
        ],
        vmem=28,
        flops=HEADS_WEIGHT,
        name="backward_heads",
    )


def backward_terms(d_qkv, weights, rows, count, joined, after=()):
    length, features = d_qkv[0].shape
    width = weights[0].shape[0]
    shapes = term_outs(rows, width, count, joined)

    def kernel(*refs):
        grads, weight_refs = refs[:3], refs[3:6]
        own_ref, *outs = refs[6 + len(after) :]
        for low in range(0, width, CHUNK):
            total = 0.0
            for i in range(3):
                total += lax.dot_general(
                    grads[i][...],
                    weight_refs[i][low : low + CHUNK, :],
                    NT,
                    preferred_element_type=jnp.float32,
                )
            own_ref[:, low : low + CHUNK] = total[:rows]
            store_terms(total, low, outs, rows, count, joined)

    own, *terms = call(
        kernel,
        [jax.ShapeDtypeStruct((rows, width), jnp.float32)] + shapes,
        list(d_qkv) + list(weights) + list(after),
        [VMEM] * 6 + [ANY] * len(after),
        vmem=24,
        flops=TERMS_WEIGHT,
        name="backward_terms",
    )
    return own, terms


def forward_terms(qkv, act_in, weight, rows, count, joined, after=()):
    length, features = qkv[0].shape
    width = weight.shape[0]
    shapes = term_outs(rows, width, count, joined)
    step = min(length, 512)

    def kernel(*refs):
        q_ref, k_ref, v_ref, act_ref, weight_ref = refs[:5]
        own_ref, *outs = refs[5 + len(after) : -1]
        attn = refs[-1]
        for head in range(features // HD):
            cols = slice(head * HD, (head + 1) * HD)
            for low in range(0, length, step):
                part = slice(low, low + step)
                scores = lax.dot_general(
                    q_ref[part, cols], k_ref[:, cols], NT, preferred_element_type=jnp.float32
                )
                top = jnp.max(scores, 1, keepdims=True)
                raised = jnp.exp2((scores - top) * EXP2_SCALE)
                total = jnp.sum(raised, 1, keepdims=True)
                mixed = jnp.dot(
                    raised.astype(jnp.bfloat16), v_ref[:, cols], preferred_element_type=jnp.float32
                )
                attn[part, cols] = (mixed * (1.0 / total)).astype(jnp.bfloat16)

        for low in range(0, width, CHUNK):
            total = lax.dot_general(
                attn[...], weight_ref[low : low + CHUNK, :], NT, preferred_element_type=jnp.float32
            )
            own = total[:rows] + act_ref[:, low : low + CHUNK]
            own_ref[:, low : low + CHUNK] = own.astype(jnp.bfloat16)
            store_terms(total, low, outs, rows, count, joined)

    own, *terms = call(
        kernel,
        [jax.ShapeDtypeStruct((rows, width), jnp.bfloat16)] + shapes,
        list(qkv) + [act_in, weight, *after],
        [VMEM] * 5 + [ANY] * len(after),
        [pltpu.VMEM((length, features), jnp.bfloat16)],
        vmem=24,
        flops=FORWARD_WEIGHT,
        name="forward_terms",
    )
    return own, terms


def input_grad(own, pieces, saved, grad, inv, gain, bounds, after=()):
    keys = sorted(pieces)

    def kernel(own_ref, saved_ref, grad_ref, inv_ref, gain_ref, *refs):
        out_ref = refs[-1]
        for part, (low, high) in enumerate(bounds):
            total = own_ref[low:high, :]
            for ref, key in zip(refs, keys):
                if key[1] == part:
                    first = pieces[key][1]
                    total = total + ref[first : first + high - low, :].astype(jnp.float32)
            total = total * gain_ref[...]
            saved_rows = saved_ref[low:high, :]
            mean = jnp.mean(saved_rows * total, -1, keepdims=True)
            inv_rows = inv_ref[low:high, :]
            out_ref[low:high, :] = (
                grad_ref[low:high, :]
                + inv_rows * total
                - saved_rows * (inv_rows * inv_rows * inv_rows * mean)
            ).astype(jnp.bfloat16)

    return call(
        kernel,
        [jax.ShapeDtypeStruct(own.shape, jnp.bfloat16)],
        [own, saved, grad, inv, gain] + [pieces[key][0] for key in keys] + list(after),
        [VMEM] * (5 + len(keys)) + [ANY] * len(after),
        flops=INPUT_GRAD_WEIGHT,
        name="input_grad",
    )[0]


def added_pieces(total, pieces, refs, part, height):
    for ref, (key, (_, first)) in zip(refs, pieces.items()):
        if key[1] == part:
            total = total + ref[first : first + height, :].astype(jnp.float32)
    return total


def activation_sum(base, pieces, bounds):
    def kernel(base_ref, *refs):
        out_ref, mark_ref = refs[-2:]
        for part, (low, high) in enumerate(bounds):
            total = base_ref[low:high, :].astype(jnp.float32)
            out_ref[0, low:high, :] = added_pieces(total, pieces, refs, part, high - low)
        mark_ref[...] = jnp.zeros_like(mark_ref)

    return call(
        kernel,
        [
            jax.ShapeDtypeStruct((1, *base.shape), jnp.float32),
            jax.ShapeDtypeStruct((8, LANES), jnp.float32),
        ],
        [base] + [value for value, _ in pieces.values()],
        [VMEM] * (1 + len(pieces)),
        flops=LAST_SUM_WEIGHT,
        name="activation_sum",
    )


def widened(values, bounds, after=()):
    def kernel(in_any, *refs):
        out_ref, held, sems = refs[-3:]
        copies = [
            pltpu.make_async_copy(
                in_any.at[pl.ds(low, high - low), :],
                held.at[pl.ds(low, high - low), :],
                sems.at[i],
            )
            for i, (low, high) in enumerate(bounds)
        ]
        for copy in copies:
            copy.start()
        for copy, (low, high) in zip(copies, bounds):
            copy.wait()
            out_ref[0, low:high, :] = held[low:high, :].astype(jnp.float32)

    return call(
        kernel,
        [jax.ShapeDtypeStruct((1, *values.shape), jnp.float32)],
        [values, *after],
        [ANY] * (1 + len(after)),
        [
            pltpu.VMEM(values.shape, values.dtype),
            pltpu.SemaphoreType.DMA((len(bounds),)),
        ],
        name="widen",
    )[0]


def rope_tables(positions):
    half_dim = HD // 2
    inverse = 10000.0 ** (-(jnp.arange(half_dim).astype(jnp.float32) * 2.0 / HD))
    angles = positions.astype(jnp.float32)[:, None] * inverse[None, :]
    cosine, sine = jnp.cos(angles), jnp.sin(angles)
    return jnp.concatenate([cosine, cosine], 1), jnp.concatenate([-sine, sine], 1)


def shards(x_fwd, x_bwd, grad_in, gain, w_query, w_key, w_value, w_out):
    act_in, saved_in, grad = x_fwd[0], x_bwd[0], grad_in[0]
    rows = act_in.shape[0]
    count = lax.axis_size("seq")
    bounds = part_bounds(rows, count)
    own_query, own_key, own_value, own_out = w_query[0], w_key[0], w_value[0], w_out[0]

    block_of = lax.axis_index("seq") ^ jnp.arange(count)
    positions = (block_of[:, None] * rows + jnp.arange(rows)[None, :]).reshape(-1)
    cosine, sine = rope_tables(positions)

    whole = [(0, rows)]
    projections = (own_query, own_key, own_value)
    (normed_bwd,), inv_bwd = normed_rows(saved_in, gain, whole, vmem=62)
    grad_low = cast_rows(grad, [normed_bwd])
    all_bwd = gather_first(normed_bwd, "saved")
    all_grad = gather_first(grad_low, "grad")
    normed_fwd, _ = normed_rows(act_in, gain, bounds)
    picked = picked_rows(second_hops(all_bwd, bounds), [grad_low])
    all_bwd = gather_rest(all_bwd, picked, bounds, "saved")
    n = len(bounds)
    handed_on = [(value, 0, value.shape[0]) for value in normed_fwd]
    picked = picked_rows(handed_on + second_hops(all_grad, bounds), picked)
    all_fwd = gather_parts({}, picked[:n], bounds, True, "input")
    all_grad = gather_rest(all_grad, picked[n:], bounds, "grad")

    qkv = project(all_bwd, projections, cosine, sine, rows)
    all_fwd = gather_parts(all_fwd, picked_rows(handed_on, qkv[:1]), bounds, False, "input")
    d_qkv = backward_heads(all_grad, qkv, own_out, cosine, sine, rows)
    picked = picked_rows(second_hops(all_fwd, bounds), d_qkv[:1])
    all_fwd = gather_rest(all_fwd, picked, bounds, "input")
    d_own, d_terms = backward_terms(d_qkv, projections, rows, count, True, picked)
    qkv = project(all_fwd, projections, cosine, sine, rows, FORWARD_WEIGHT)
    own, terms = forward_terms(qkv, act_in, own_out, rows, count, False)

    back = Scatter(d_terms, rows, True, across, "grad")
    front = Scatter(
        terms, rows, False, lambda value, bit: across_and_on(value, 1 << bit), "branch"
    )
    back.send_groups()
    front.send_groups()
    d_sums = back.send_sums([terms[0]])
    own = across_and_on(own, 0)
    sums = front.send_sums(d_sums)
    d_input = input_grad(
        d_own, back.final, saved_in, grad, inv_bwd, gain, bounds, sums
    )
    act_next, mark = activation_sum(own, front.final, bounds)
    return (act_next, widened(passed_along(d_input, "pipe", -1), bounds, [mark]))


def solution(mesh):
    placed = (
        P("pipe", "seq", None),
        P("pipe", "seq", None),
        P("pipe", "seq", None),
        P("pipe", None),
        P("pipe", None, "seq"),
        P("pipe", None, "seq"),
        P("pipe", None, "seq"),
        P("pipe", None, "seq"),
    )
    return jax.shard_map(
        shards,
        mesh=mesh,
        in_specs=placed,
        out_specs=(P("pipe", "seq", None), P("pipe", "seq", None)),
        check_vma=False,
    )
```

```python
import functools
import math

import jax
import jax.numpy as jnp
from jax import lax
from jax.experimental import pallas as pl
from jax.experimental.pallas import tpu as pltpu
from jax.sharding import PartitionSpec as P

HD = 128
LANES = 128
CHUNK = 256
EXP2_SCALE = HD ** (-0.5) * math.log2(math.e)
NT = (((1,), (1,)), ((), ()))
TN = (((0,), (0,)), ((), ()))
HEADS_WEIGHT = 8_000_000_000
TERMS_WEIGHT = 3_000_000_000
INPUT_GRAD_WEIGHT = 8_000_000_000
LAST_SUM_WEIGHT = 8_000_000_000
FORWARD_WEIGHT = 5_000_000_000
SUMS_WEIGHT = 6000000000
MIB = 1024 * 1024


def bits_of(number):
    return [bit for bit in range(number.bit_length()) if (number >> bit) & 1]


def by_distance(count):
    return sorted(range(1, count), key=lambda rel: (len(bits_of(rel)), rel))


def part_bounds(rows, count):
    parts = 2 if count > 2 else 1
    return [(rows * i // parts, rows * (i + 1) // parts) for i in range(parts)]


def last_bit(rel, part):
    bits = bits_of(rel)
    return bits[part % len(bits)]


def ways_to(rel, bounds):
    ways = {}
    for part, (low, high) in enumerate(bounds):
        bit = last_bit(rel, part)
        ways[bit] = (min(low, ways.get(bit, (low, high))[0]), high)
    return [(bit, low, high) for bit, (low, high) in ways.items()]


def across(value, bit):
    count = lax.axis_size("seq")
    return lax.ppermute(value, "seq", [(i, i ^ (1 << bit)) for i in range(count)])


def across_and_on(value, flip):
    count, sections = lax.axis_size("seq"), lax.axis_size("pipe")
    pairs = [
        (p * count + i, (p + 1) % sections * count + (i ^ flip))
        for p in range(sections)
        for i in range(count)
    ]
    return lax.ppermute(value, ("pipe", "seq"), pairs)


def passed_along(value, axis, steps):
    count = lax.axis_size(axis)
    pairs = [(source, (source + steps) % count) for source in range(count)]
    return lax.ppermute(value, axis, pairs)


def onward_rows(count, bounds):
    return [
        (rel ^ (1 << bit), bit, low, high)
        for rel in by_distance(count)
        for bit, low, high in ways_to(rel, bounds)
    ]


def goes_on(rel, low, count, bounds):
    return any(
        rel == at and first <= low < last for at, _, first, last in onward_rows(count, bounds)
    )


def gather_first(own, what):
    count = lax.axis_size("seq")
    blocks = {(0, 0): own}
    for rel in by_distance(count):
        if len(bits_of(rel)) == 1:
            with jax.named_scope(f"gather_{what}_block{rel}"):
                blocks[rel, 0] = across(own, bits_of(rel)[0])
    return blocks


def gather_parts(blocks, own_parts, bounds, early, what):
    count = lax.axis_size("seq")
    for rel in by_distance(count):
        for value, (low, _) in zip(own_parts, bounds):
            blocks.setdefault((0, low), value)
            if len(bits_of(rel)) == 1 and goes_on(rel, low, count, bounds) == early:
                with jax.named_scope(f"gather_{what}_block{rel}_first{low}"):
                    blocks[rel, low] = across(value, bits_of(rel)[0])
    return blocks


def second_hops(blocks, bounds):
    hops = []
    for rel, _, low, high in onward_rows(lax.axis_size("seq"), bounds):
        if len(bits_of(rel)) == 1:
            first = low if (rel, low) in blocks else 0
            hops.append((blocks[rel, first], low - first, high - first))
    return hops


def gather_rest(blocks, picked, bounds, what):
    count = lax.axis_size("seq")
    picked = list(picked)
    for rel, bit, low, high in onward_rows(count, bounds):
        if rel == 0:
            continue
        value = picked.pop(0) if len(bits_of(rel)) == 1 else blocks[rel, low]
        if value.shape[0] > high - low:
            value = value[: high - low]
        with jax.named_scope(f"gather_{what}_block{rel ^ (1 << bit)}_row{low}"):
            blocks[rel ^ (1 << bit), low] = across(value, bit)
    return blocks


def messages_of(rows, count, joined):
    parts = range(len(part_bounds(rows, count)))
    later = {
        (rel ^ (1 << last_bit(rel, part)), part)
        for rel in range(1, count)
        for part in parts
        if len(bits_of(rel)) > 1
    }
    groups, waiting = {}, {}
    for rel in reversed(by_distance(count)):
        for part in parts:
            key = (rel, part)
            if not joined and len(bits_of(rel)) == 1:
                waiting.setdefault(rel, []).append(key)
            elif key in later:
                waiting[key] = [key]
            else:
                groups.setdefault(last_bit(*key) if joined else key, []).append(key)
    return list(groups.values()), list(waiting.values())


class Scatter:

    def __init__(self, terms, rows, joined, send_last, what):
        count = lax.axis_size("seq")
        self.bounds = part_bounds(rows, count)
        self.groups, waiting = messages_of(rows, count, joined)
        self.leaving = list(terms[: len(self.groups)])
        self.waiting = list(zip(waiting, terms[len(self.groups) :]))
        self.send_last, self.what = send_last, what
        self.arrived, self.final = {}, {}

    def send(self, value, keys):
        bit = last_bit(*keys[0])
        targets = [(rel ^ (1 << bit), part) for rel, part in keys]
        onward = any(rel for rel, _ in targets)
        with jax.named_scope(f"scatter_{self.what}_block{keys[0][0]}_part{keys[0][1]}"):
            moved = (across if onward else self.send_last)(value, bit)
        first = 0
        for key, target in zip(keys, targets):
            if target[0]:
                self.arrived.setdefault(target, []).append((moved, first))
            else:
                self.final[key] = (moved, first)
            first += self.bounds[key[1]][1] - self.bounds[key[1]][0]

    def send_groups(self):
        for value, keys in zip(self.leaving, self.groups):
            self.send(value, keys)

    def send_sums(self, after=(), weight=1):
        sums = []
        height = self.bounds[0][1] - self.bounds[0][0]
        levels = {len(bits_of(keys[0][0])) for keys, _ in self.waiting}
        for level in sorted(levels, reverse=True):
            found = [pair for pair in self.waiting if len(bits_of(pair[0][0][0])) == level]
            totals = [
                (term, [self.arrived.get(key, []) for key in keys]) for keys, term in found
            ]
            results = sum_rows(totals, height, after, weight)
            sums += results
            for (keys, _), value in zip(found, results):
                self.send(value, keys)
        return sums


def call(kernel, out_shapes, operands, in_specs, scratch=(), flops=1, vmem=10, name=None):
    return pl.pallas_call(
        kernel,
        out_shape=out_shapes,
        in_specs=in_specs,
        out_specs=[pl.BlockSpec(memory_space=pltpu.VMEM)] * len(out_shapes),
        scratch_shapes=list(scratch),
        compiler_params=pltpu.CompilerParams(vmem_limit_bytes=vmem * MIB),
        cost_estimate=pl.CostEstimate(flops=int(flops), bytes_accessed=1, transcendentals=0),
        name=name,
    )(*operands)


ANY = pl.BlockSpec(memory_space=pl.ANY)
HBM = pl.BlockSpec(memory_space=pltpu.HBM)
VMEM = pl.BlockSpec(memory_space=pltpu.VMEM)


def normed_rows(inputs, gain, bounds, after=(), vmem=10):
    rows, width = inputs.shape

    def kernel(x_any, gain_any, *refs):
        *outs, inv_ref, x_ref, gain_ref, sems = refs[len(after) :]
        copies = [
            pltpu.make_async_copy(source, held, sems.at[i])
            for i, (source, held) in enumerate([(x_any, x_ref), (gain_any, gain_ref)])
        ]
        for copy in copies:
            copy.start()
        for copy in copies:
            copy.wait()
        for out_ref, (low, high) in zip(outs, bounds):
            x = x_ref[low:high, :]
            inv = lax.rsqrt(jnp.mean(x * x, -1, keepdims=True) + 1e-05)
            out_ref[...] = (x * inv * gain_ref[...]).astype(jnp.bfloat16)
            inv_ref[low:high, :] = inv

    *parts, inv = call(
        kernel,
        [jax.ShapeDtypeStruct((high - low, width), jnp.bfloat16) for low, high in bounds]
        + [jax.ShapeDtypeStruct((rows, 1), jnp.float32)],
        [inputs, gain, *after],
        [HBM] * 2 + [ANY] * len(after),
        [
            pltpu.VMEM(inputs.shape, jnp.float32),
            pltpu.VMEM(gain.shape, jnp.float32),
            pltpu.SemaphoreType.DMA((2,)),
        ],
        vmem=vmem,
        name="norm",
    )
    return parts, inv


def picked_rows(pieces, after=()):
    n = len(pieces)

    def kernel(*refs):
        outs, sems = refs[n + len(after) : -1], refs[-1]
        copies = [
            pltpu.make_async_copy(ref.at[pl.ds(low, high - low), :], out_ref, sems.at[i])
            for i, (ref, out_ref, (_, low, high)) in enumerate(zip(refs, outs, pieces))
        ]
        for copy in copies:
            copy.start()
        for copy in copies:
            copy.wait()

    return call(
        kernel,
        [
            jax.ShapeDtypeStruct((high - low, value.shape[1]), value.dtype)
            for value, low, high in pieces
        ],
        [value for value, _, _ in pieces] + list(after),
        [ANY] * (n + len(after)),
        [pltpu.SemaphoreType.DMA((n,))],
        name="pick",
    )


def cast_rows(inputs, after=()):
    def kernel(x_ref, *refs):
        refs[len(after)][...] = x_ref[...].astype(jnp.bfloat16)

    return call(
        kernel,
        [jax.ShapeDtypeStruct(inputs.shape, jnp.bfloat16)],
        (inputs, *after),
        [VMEM] + [ANY] * len(after),
        name="cast",
    )[0]


def sum_rows(totals, height, after=(), weight=1):
    pieces = [piece for _, parts in totals for moved in parts for piece in moved]
    n, m = len(totals), len(pieces)

    def kernel(*refs):
        arrivals, outs = list(refs[n : n + m]), refs[-n:]
        for (_, parts), term_ref, out_ref in zip(totals, refs, outs):
            for i, moved in enumerate(parts):
                here = slice(i * height, (i + 1) * height)
                total = term_ref[here, :]
                for _, first in moved:
                    ref = arrivals.pop(0)
                    total = total + ref[first : first + height, :].astype(jnp.float32)
                out_ref[here, :] = total.astype(jnp.bfloat16)

    return call(
        kernel,
        [jax.ShapeDtypeStruct(term.shape, jnp.bfloat16) for term, _ in totals],
        [term for term, _ in totals] + [value for value, _ in pieces] + list(after),
        [VMEM] * (n + m) + [ANY] * len(after),
        flops=weight,
        name="sum_rows",
    )


def block_copies(block_refs, keys, rows, all_rows, sems):
    return [
        pltpu.make_async_copy(
            ref, all_rows.at[pl.ds(rel * rows + low, ref.shape[0]), :], sems.at[i]
        )
        for i, (ref, (rel, low)) in enumerate(zip(block_refs, keys))
    ]


def turned(values, cosine, sine):
    return values * cosine + pltpu.roll(values, HD // 2, 1) * sine


def project_into(rows_ref, weight_ref, out_ref, cos_ref=None, sin_ref=None):
    features = out_ref.shape[1]
    for low in range(0, features, CHUNK):
        high = min(low + CHUNK, features)
        values = jnp.dot(
            rows_ref[...], weight_ref[:, low:high], preferred_element_type=jnp.float32
        )
        for head in range(0, high - low, HD):
            piece = values[:, head : head + HD]
            if cos_ref is not None:
                piece = turned(piece, cos_ref[...], sin_ref[...])
            out_ref[:, low + head : low + head + HD] = piece.astype(jnp.bfloat16)


def project(blocks, weights, cosine, sine, rows, weight=1):
    keys = sorted(blocks)
    length, width = cosine.shape[0], blocks[0, 0].shape[1]
    features = weights[0].shape[1]
    n = len(keys)

    def kernel(*refs):
        block_refs, weight_refs = refs[:n], refs[n : n + 3]
        cos_ref, sin_ref = refs[n + 3 : n + 5]
        outs = refs[n + 5 : n + 8]
        all_rows, sems = refs[n + 8 :]
        copies = block_copies(block_refs, keys, rows, all_rows, sems)
        for copy in copies:
            copy.start()
        for copy in copies:
            copy.wait()
        for i in range(3):
            tables = (cos_ref, sin_ref) if i < 2 else ()
            project_into(all_rows, weight_refs[i], outs[i], *tables)

    return call(
        kernel,
        [jax.ShapeDtypeStruct((length, features), jnp.bfloat16)] * 3,
        [blocks[key] for key in keys] + list(weights) + [cosine, sine],
        [ANY] * n + [VMEM] * 5,
        [pltpu.VMEM((length, width), jnp.bfloat16), pltpu.SemaphoreType.DMA((n,))],
        flops=weight,
        vmem=20,
        name="project",
    )


def term_outs(rows, width, count, joined):
    bounds = part_bounds(rows, count)
    groups, waiting = messages_of(rows, count, joined)

    def shape(keys, dtype):
        height = sum(bounds[part][1] - bounds[part][0] for _, part in keys)
        return jax.ShapeDtypeStruct((height, width), dtype)

    return [shape(keys, jnp.bfloat16) for keys in groups] + [
        shape(keys, jnp.float32) for keys in waiting
    ]


def store_terms(values, low, refs, rows, count, joined):
    bounds = part_bounds(rows, count)
    groups, waiting = messages_of(rows, count, joined)
    for ref, keys in zip(refs, groups + waiting):
        at = 0
        for rel, part in keys:
            first, last = bounds[part]
            piece = values[rel * rows + first : rel * rows + last]
            ref[at : at + last - first, low : low + values.shape[1]] = piece.astype(ref.dtype)
            at += last - first


def backward_heads(blocks, qkv, weight, cosine, sine, rows):
    in_keys = sorted(blocks)
    length, width = cosine.shape[0], blocks[0, 0].shape[1]
    features = qkv[0].shape[1]
    n = len(in_keys)
    step = min(length, 512)

    def kernel(*refs):
        block_refs, weight_ref = refs[:n], refs[n]
        q_ref, k_ref, v_ref, cos_ref, sin_ref = refs[n + 1 : n + 6]
        d_qkv = refs[n + 6 : n + 9]
        all_rows, d_attn, sems = refs[n + 9 :]
        copies = block_copies(block_refs, in_keys, rows, all_rows, sems)
        for copy in copies:
            copy.start()
        for copy in copies:
            copy.wait()
        project_into(all_rows, weight_ref, d_attn)

        for head in range(features // HD):
            cols = slice(head * HD, (head + 1) * HD)
            key, value = k_ref[:, cols], v_ref[:, cols]
            d_key, d_value = 0.0, 0.0
            for low in range(0, length, step):
                part = slice(low, low + step)
                query, grad = q_ref[part, cols], d_attn[part, cols]
                scores = lax.dot_general(key, query, NT, preferred_element_type=jnp.float32)
                top = jnp.max(scores, 0, keepdims=True)
                raised = jnp.exp2((scores - top) * EXP2_SCALE)
                probs = raised * (1.0 / jnp.sum(raised, 0, keepdims=True))
                d_value += jnp.dot(
                    probs.astype(jnp.bfloat16), grad, preferred_element_type=jnp.float32
                )
                d_probs = lax.dot_general(value, grad, NT, preferred_element_type=jnp.float32)
                delta = jnp.sum(probs * d_probs, 0, keepdims=True)
                d_scores = (probs * (d_probs - delta) * HD ** (-0.5)).astype(jnp.bfloat16)
                d_key += jnp.dot(d_scores, query, preferred_element_type=jnp.float32)
                d_query = lax.dot_general(
                    key, d_scores, TN, preferred_element_type=jnp.float32
                ).T
                d_qkv[0][part, cols] = turned(
                    d_query, cos_ref[part, :], -sin_ref[part, :]
                ).astype(jnp.bfloat16)
            d_qkv[1][:, cols] = turned(d_key, cos_ref[...], -sin_ref[...]).astype(jnp.bfloat16)
            d_qkv[2][:, cols] = d_value.astype(jnp.bfloat16)

    return call(
        kernel,
        [jax.ShapeDtypeStruct((length, features), jnp.bfloat16)] * 3,
        [blocks[key] for key in in_keys] + [weight] + list(qkv) + [cosine, sine],
        [ANY] * n + [VMEM] * 6,
        [
            pltpu.VMEM((length, width), jnp.bfloat16),
            pltpu.VMEM((length, features), jnp.bfloat16),
            pltpu.SemaphoreType.DMA((n,)),
        ],
        vmem=28,
        flops=HEADS_WEIGHT,
        name="backward_heads",
    )


def backward_terms(d_qkv, weights, rows, count, joined, after=()):
    length, features = d_qkv[0].shape
    width = weights[0].shape[0]
    shapes = term_outs(rows, width, count, joined)

    def kernel(*refs):
        grads, weight_refs = refs[:3], refs[3:6]
        own_ref, *outs = refs[6 + len(after) :]
        for low in range(0, width, CHUNK):
            total = 0.0
            for i in range(3):
                total += lax.dot_general(
                    grads[i][...],
                    weight_refs[i][low : low + CHUNK, :],
                    NT,
                    preferred_element_type=jnp.float32,
                )
            own_ref[:, low : low + CHUNK] = total[:rows]
            store_terms(total, low, outs, rows, count, joined)

    own, *terms = call(
        kernel,
        [jax.ShapeDtypeStruct((rows, width), jnp.float32)] + shapes,
        list(d_qkv) + list(weights) + list(after),
        [VMEM] * 6 + [ANY] * len(after),
        vmem=24,
        flops=TERMS_WEIGHT,
        name="backward_terms",
    )
    return own, terms


def forward_terms(qkv, act_in, weight, rows, count, joined, after=()):
    length, features = qkv[0].shape
    width = weight.shape[0]
    shapes = term_outs(rows, width, count, joined)
    step = min(length, 512)

    def kernel(*refs):
        q_ref, k_ref, v_ref, act_ref, weight_ref = refs[:5]
        own_ref, *outs = refs[5 + len(after) : -1]
        attn = refs[-1]
        for head in range(features // HD):
            cols = slice(head * HD, (head + 1) * HD)
            for low in range(0, length, step):
                part = slice(low, low + step)
                scores = lax.dot_general(
                    q_ref[part, cols], k_ref[:, cols], NT, preferred_element_type=jnp.float32
                )
                top = jnp.max(scores, 1, keepdims=True)
                raised = jnp.exp2((scores - top) * EXP2_SCALE)
                total = jnp.sum(raised, 1, keepdims=True)
                mixed = jnp.dot(
                    raised.astype(jnp.bfloat16), v_ref[:, cols], preferred_element_type=jnp.float32
                )
                attn[part, cols] = (mixed * (1.0 / total)).astype(jnp.bfloat16)

        for low in range(0, width, CHUNK):
            total = lax.dot_general(
                attn[...], weight_ref[low : low + CHUNK, :], NT, preferred_element_type=jnp.float32
            )
            own = total[:rows] + act_ref[:, low : low + CHUNK]
            own_ref[:, low : low + CHUNK] = own.astype(jnp.bfloat16)
            store_terms(total, low, outs, rows, count, joined)

    own, *terms = call(
        kernel,
        [jax.ShapeDtypeStruct((rows, width), jnp.bfloat16)] + shapes,
        list(qkv) + [act_in, weight, *after],
        [VMEM] * 5 + [ANY] * len(after),
        [pltpu.VMEM((length, features), jnp.bfloat16)],
        vmem=24,
        flops=FORWARD_WEIGHT,
        name="forward_terms",
    )
    return own, terms


def input_grad(own, pieces, saved, grad, inv, gain, bounds, after=()):
    keys = sorted(pieces)

    def kernel(own_ref, saved_ref, grad_ref, inv_ref, gain_ref, *refs):
        out_ref = refs[-1]
        for part, (low, high) in enumerate(bounds):
            total = own_ref[low:high, :]
            for ref, key in zip(refs, keys):
                if key[1] == part:
                    first = pieces[key][1]
                    total = total + ref[first : first + high - low, :].astype(jnp.float32)
            total = total * gain_ref[...]
            saved_rows = saved_ref[low:high, :]
            mean = jnp.mean(saved_rows * total, -1, keepdims=True)
            inv_rows = inv_ref[low:high, :]
            out_ref[low:high, :] = (
                grad_ref[low:high, :]
                + inv_rows * total
                - saved_rows * (inv_rows * inv_rows * inv_rows * mean)
            ).astype(jnp.bfloat16)

    return call(
        kernel,
        [jax.ShapeDtypeStruct(own.shape, jnp.bfloat16)],
        [own, saved, grad, inv, gain] + [pieces[key][0] for key in keys] + list(after),
        [VMEM] * (5 + len(keys)) + [ANY] * len(after),
        flops=INPUT_GRAD_WEIGHT,
        name="input_grad",
    )[0]


def added_pieces(total, pieces, refs, part, height):
    for ref, (key, (_, first)) in zip(refs, pieces.items()):
        if key[1] == part:
            total = total + ref[first : first + height, :].astype(jnp.float32)
    return total


def activation_sum(base, pieces, bounds):
    def kernel(base_ref, *refs):
        out_ref, mark_ref = refs[-2:]
        for part, (low, high) in enumerate(bounds):
            total = base_ref[low:high, :].astype(jnp.float32)
            out_ref[0, low:high, :] = added_pieces(total, pieces, refs, part, high - low)
        mark_ref[...] = jnp.zeros_like(mark_ref)

    return call(
        kernel,
        [
            jax.ShapeDtypeStruct((1, *base.shape), jnp.float32),
            jax.ShapeDtypeStruct((8, LANES), jnp.float32),
        ],
        [base] + [value for value, _ in pieces.values()],
        [VMEM] * (1 + len(pieces)),
        flops=LAST_SUM_WEIGHT,
        name="activation_sum",
    )


def widened(values, bounds, after=()):
    def kernel(in_any, *refs):
        out_ref, held, sems = refs[-3:]
        copies = [
            pltpu.make_async_copy(
                in_any.at[pl.ds(low, high - low), :],
                held.at[pl.ds(low, high - low), :],
                sems.at[i],
            )
            for i, (low, high) in enumerate(bounds)
        ]
        for copy in copies:
            copy.start()
        for copy, (low, high) in zip(copies, bounds):
            copy.wait()
            out_ref[0, low:high, :] = held[low:high, :].astype(jnp.float32)

    return call(
        kernel,
        [jax.ShapeDtypeStruct((1, *values.shape), jnp.float32)],
        [values, *after],
        [ANY] * (1 + len(after)),
        [
            pltpu.VMEM(values.shape, values.dtype),
            pltpu.SemaphoreType.DMA((len(bounds),)),
        ],
        name="widen",
    )[0]


def rope_tables(positions):
    half_dim = HD // 2
    inverse = 10000.0 ** (-(jnp.arange(half_dim).astype(jnp.float32) * 2.0 / HD))
    angles = positions.astype(jnp.float32)[:, None] * inverse[None, :]
    cosine, sine = jnp.cos(angles), jnp.sin(angles)
    return jnp.concatenate([cosine, cosine], 1), jnp.concatenate([-sine, sine], 1)


def shards(x_fwd, x_bwd, grad_in, gain, w_query, w_key, w_value, w_out):
    act_in, saved_in, grad = x_fwd[0], x_bwd[0], grad_in[0]
    rows = act_in.shape[0]
    count = lax.axis_size("seq")
    bounds = part_bounds(rows, count)
    own_query, own_key, own_value, own_out = w_query[0], w_key[0], w_value[0], w_out[0]

    block_of = lax.axis_index("seq") ^ jnp.arange(count)
    positions = (block_of[:, None] * rows + jnp.arange(rows)[None, :]).reshape(-1)
    cosine, sine = rope_tables(positions)

    whole = [(0, rows)]
    projections = (own_query, own_key, own_value)
    (normed_bwd,), inv_bwd = normed_rows(saved_in, gain, whole, vmem=62)
    grad_low = cast_rows(grad, [normed_bwd])
    all_bwd = gather_first(normed_bwd, "saved")
    all_grad = gather_first(grad_low, "grad")
    normed_fwd, _ = normed_rows(act_in, gain, bounds)
    picked = picked_rows(second_hops(all_bwd, bounds), [grad_low])
    all_bwd = gather_rest(all_bwd, picked, bounds, "saved")
    n = len(bounds)
    handed_on = [(value, 0, value.shape[0]) for value in normed_fwd]
    picked = picked_rows(handed_on + second_hops(all_grad, bounds), picked)
    all_fwd = gather_parts({}, picked[:n], bounds, True, "input")
    all_grad = gather_rest(all_grad, picked[n:], bounds, "grad")

    qkv = project(all_bwd, projections, cosine, sine, rows)
    all_fwd = gather_parts(all_fwd, picked_rows(handed_on, qkv[:1]), bounds, False, "input")
    d_qkv = backward_heads(all_grad, qkv, own_out, cosine, sine, rows)
    picked = picked_rows(second_hops(all_fwd, bounds), d_qkv[:1])
    all_fwd = gather_rest(all_fwd, picked, bounds, "input")
    d_own, d_terms = backward_terms(d_qkv, projections, rows, count, True, picked)
    qkv = project(all_fwd, projections, cosine, sine, rows, FORWARD_WEIGHT)
    own, terms = forward_terms(qkv, act_in, own_out, rows, count, False)

    back = Scatter(d_terms, rows, True, across, "grad")
    front = Scatter(
        terms, rows, False, lambda value, bit: across_and_on(value, 1 << bit), "branch"
    )
    back.send_groups()
    front.send_groups()
    d_sums = back.send_sums([terms[0]])
    own = across_and_on(own, 0)
    sums = front.send_sums(d_sums, SUMS_WEIGHT)
    d_input = input_grad(
        d_own, back.final, saved_in, grad, inv_bwd, gain, bounds, [own, *sums]
    )
    act_next, mark = activation_sum(own, front.final, bounds)
    return (act_next, widened(passed_along(d_input, "pipe", -1), bounds, [mark]))


def solution(mesh):
    placed = (
        P("pipe", "seq", None),
        P("pipe", "seq", None),
        P("pipe", "seq", None),
        P("pipe", None),
        P("pipe", None, "seq"),
        P("pipe", None, "seq"),
        P("pipe", None, "seq"),
        P("pipe", None, "seq"),
    )
    return jax.shard_map(
        shards,
        mesh=mesh,
        in_specs=placed,
        out_specs=(P("pipe", "seq", None), P("pipe", "seq", None)),
        check_vma=False,
    )
```

```python
import functools
import math

import jax
import jax.numpy as jnp
from jax import lax
from jax.experimental import pallas as pl
from jax.experimental.pallas import tpu as pltpu
from jax.sharding import PartitionSpec as P

HD = 128
LANES = 128
CHUNK = 256
EXP2_SCALE = HD ** (-0.5) * math.log2(math.e)
NT = (((1,), (1,)), ((), ()))
TN = (((0,), (0,)), ((), ()))
HEADS_WEIGHT = 8_000_000_000
TERMS_WEIGHT = 3_000_000_000
INPUT_GRAD_WEIGHT = 8_000_000_000
LAST_SUM_WEIGHT = 8_000_000_000
FORWARD_WEIGHT = 5_000_000_000
SUMS_WEIGHT = 6000000000
MIB = 1024 * 1024


def bits_of(number):
    return [bit for bit in range(number.bit_length()) if (number >> bit) & 1]


def by_distance(count):
    return sorted(range(1, count), key=lambda rel: (len(bits_of(rel)), rel))


def part_bounds(rows, count):
    parts = 2 if count > 2 else 1
    return [(rows * i // parts, rows * (i + 1) // parts) for i in range(parts)]


def last_bit(rel, part):
    bits = bits_of(rel)
    return bits[part % len(bits)]


def ways_to(rel, bounds):
    ways = {}
    for part, (low, high) in enumerate(bounds):
        bit = last_bit(rel, part)
        ways[bit] = (min(low, ways.get(bit, (low, high))[0]), high)
    return [(bit, low, high) for bit, (low, high) in ways.items()]


def across(value, bit):
    count = lax.axis_size("seq")
    return lax.ppermute(value, "seq", [(i, i ^ (1 << bit)) for i in range(count)])


def across_and_on(value, flip):
    count, sections = lax.axis_size("seq"), lax.axis_size("pipe")
    pairs = [
        (p * count + i, (p + 1) % sections * count + (i ^ flip))
        for p in range(sections)
        for i in range(count)
    ]
    return lax.ppermute(value, ("pipe", "seq"), pairs)


def passed_along(value, axis, steps):
    count = lax.axis_size(axis)
    pairs = [(source, (source + steps) % count) for source in range(count)]
    return lax.ppermute(value, axis, pairs)


def onward_rows(count, bounds):
    return [
        (rel ^ (1 << bit), bit, low, high)
        for rel in by_distance(count)
        for bit, low, high in ways_to(rel, bounds)
    ]


def goes_on(rel, low, count, bounds):
    return any(
        rel == at and first <= low < last for at, _, first, last in onward_rows(count, bounds)
    )


def gather_first(own, what):
    count = lax.axis_size("seq")
    blocks = {(0, 0): own}
    for rel in by_distance(count):
        if len(bits_of(rel)) == 1:
            with jax.named_scope(f"gather_{what}_block{rel}"):
                blocks[rel, 0] = across(own, bits_of(rel)[0])
    return blocks


def gather_parts(blocks, own_parts, bounds, early, what):
    count = lax.axis_size("seq")
    for rel in by_distance(count):
        for value, (low, _) in zip(own_parts, bounds):
            blocks.setdefault((0, low), value)
            if len(bits_of(rel)) == 1 and goes_on(rel, low, count, bounds) == early:
                with jax.named_scope(f"gather_{what}_block{rel}_first{low}"):
                    blocks[rel, low] = across(value, bits_of(rel)[0])
    return blocks


def second_hops(blocks, bounds):
    hops = []
    for rel, _, low, high in onward_rows(lax.axis_size("seq"), bounds):
        if len(bits_of(rel)) == 1:
            first = low if (rel, low) in blocks else 0
            hops.append((blocks[rel, first], low - first, high - first))
    return hops


def gather_rest(blocks, picked, bounds, what):
    count = lax.axis_size("seq")
    picked = list(picked)
    for rel, bit, low, high in onward_rows(count, bounds):
        if rel == 0:
            continue
        value = picked.pop(0) if len(bits_of(rel)) == 1 else blocks[rel, low]
        if value.shape[0] > high - low:
            value = value[: high - low]
        with jax.named_scope(f"gather_{what}_block{rel ^ (1 << bit)}_row{low}"):
            blocks[rel ^ (1 << bit), low] = across(value, bit)
    return blocks


def messages_of(rows, count, joined):
    parts = range(len(part_bounds(rows, count)))
    later = {
        (rel ^ (1 << last_bit(rel, part)), part)
        for rel in range(1, count)
        for part in parts
        if len(bits_of(rel)) > 1
    }
    groups, waiting = {}, {}
    for rel in reversed(by_distance(count)):
        for part in parts:
            key = (rel, part)
            if not joined and len(bits_of(rel)) == 1:
                waiting.setdefault(rel, []).append(key)
            elif key in later:
                waiting[key] = [key]
            else:
                groups.setdefault(last_bit(*key) if joined else key, []).append(key)
    return list(groups.values()), list(waiting.values())


class Scatter:

    def __init__(self, terms, rows, joined, send_last, what):
        count = lax.axis_size("seq")
        self.bounds = part_bounds(rows, count)
        self.groups, waiting = messages_of(rows, count, joined)
        self.leaving = list(terms[: len(self.groups)])
        self.waiting = list(zip(waiting, terms[len(self.groups) :]))
        self.send_last, self.what = send_last, what
        self.arrived, self.final = {}, {}

    def send(self, value, keys):
        bit = last_bit(*keys[0])
        targets = [(rel ^ (1 << bit), part) for rel, part in keys]
        onward = any(rel for rel, _ in targets)
        with jax.named_scope(f"scatter_{self.what}_block{keys[0][0]}_part{keys[0][1]}"):
            moved = (across if onward else self.send_last)(value, bit)
        first = 0
        for key, target in zip(keys, targets):
            if target[0]:
                self.arrived.setdefault(target, []).append((moved, first))
            else:
                self.final[key] = (moved, first)
            first += self.bounds[key[1]][1] - self.bounds[key[1]][0]

    def send_groups(self):
        for value, keys in zip(self.leaving, self.groups):
            self.send(value, keys)

    def send_sums(self, after=(), weight=1):
        sums = []
        height = self.bounds[0][1] - self.bounds[0][0]
        levels = {len(bits_of(keys[0][0])) for keys, _ in self.waiting}
        for level in sorted(levels, reverse=True):
            found = [pair for pair in self.waiting if len(bits_of(pair[0][0][0])) == level]
            totals = [
                (term, [self.arrived.get(key, []) for key in keys]) for keys, term in found
            ]
            results = sum_rows(totals, height, after, weight)
            sums += results
            for (keys, _), value in zip(found, results):
                self.send(value, keys)
        return sums


def call(kernel, out_shapes, operands, in_specs, scratch=(), flops=1, vmem=10, name=None):
    return pl.pallas_call(
        kernel,
        out_shape=out_shapes,
        in_specs=in_specs,
        out_specs=[pl.BlockSpec(memory_space=pltpu.VMEM)] * len(out_shapes),
        scratch_shapes=list(scratch),
        compiler_params=pltpu.CompilerParams(vmem_limit_bytes=vmem * MIB),
        cost_estimate=pl.CostEstimate(flops=int(flops), bytes_accessed=1, transcendentals=0),
        name=name,
    )(*operands)


ANY = pl.BlockSpec(memory_space=pl.ANY)
HBM = pl.BlockSpec(memory_space=pltpu.HBM)
VMEM = pl.BlockSpec(memory_space=pltpu.VMEM)


def normed_rows(inputs, gain, bounds, after=(), vmem=10):
    rows, width = inputs.shape

    def kernel(x_any, gain_any, *refs):
        *outs, inv_ref, x_ref, gain_ref, sems = refs[len(after) :]
        copies = [
            pltpu.make_async_copy(source, held, sems.at[i])
            for i, (source, held) in enumerate([(x_any, x_ref), (gain_any, gain_ref)])
        ]
        for copy in copies:
            copy.start()
        for copy in copies:
            copy.wait()
        for out_ref, (low, high) in zip(outs, bounds):
            x = x_ref[low:high, :]
            inv = lax.rsqrt(jnp.mean(x * x, -1, keepdims=True) + 1e-05)
            out_ref[...] = (x * inv * gain_ref[...]).astype(jnp.bfloat16)
            inv_ref[low:high, :] = inv

    *parts, inv = call(
        kernel,
        [jax.ShapeDtypeStruct((high - low, width), jnp.bfloat16) for low, high in bounds]
        + [jax.ShapeDtypeStruct((rows, 1), jnp.float32)],
        [inputs, gain, *after],
        [HBM] * 2 + [ANY] * len(after),
        [
            pltpu.VMEM(inputs.shape, jnp.float32),
            pltpu.VMEM(gain.shape, jnp.float32),
            pltpu.SemaphoreType.DMA((2,)),
        ],
        vmem=vmem,
        name="norm",
    )
    return parts, inv


def picked_rows(pieces, after=()):
    n = len(pieces)

    def kernel(*refs):
        outs, sems = refs[n + len(after) : -1], refs[-1]
        copies = [
            pltpu.make_async_copy(ref.at[pl.ds(low, high - low), :], out_ref, sems.at[i])
            for i, (ref, out_ref, (_, low, high)) in enumerate(zip(refs, outs, pieces))
        ]
        for copy in copies:
            copy.start()
        for copy in copies:
            copy.wait()

    return call(
        kernel,
        [
            jax.ShapeDtypeStruct((high - low, value.shape[1]), value.dtype)
            for value, low, high in pieces
        ],
        [value for value, _, _ in pieces] + list(after),
        [ANY] * (n + len(after)),
        [pltpu.SemaphoreType.DMA((n,))],
        name="pick",
    )


def cast_rows(inputs, after=()):
    def kernel(x_ref, *refs):
        refs[len(after)][...] = x_ref[...].astype(jnp.bfloat16)

    return call(
        kernel,
        [jax.ShapeDtypeStruct(inputs.shape, jnp.bfloat16)],
        (inputs, *after),
        [VMEM] + [ANY] * len(after),
        name="cast",
    )[0]


def sum_rows(totals, height, after=(), weight=1):
    pieces = [piece for _, parts in totals for moved in parts for piece in moved]
    n, m = len(totals), len(pieces)

    def kernel(*refs):
        arrivals, outs = list(refs[n : n + m]), refs[-n:]
        for (_, parts), term_ref, out_ref in zip(totals, refs, outs):
            for i, moved in enumerate(parts):
                here = slice(i * height, (i + 1) * height)
                total = term_ref[here, :]
                for _, first in moved:
                    ref = arrivals.pop(0)
                    total = total + ref[first : first + height, :].astype(jnp.float32)
                out_ref[here, :] = total.astype(jnp.bfloat16)

    return call(
        kernel,
        [jax.ShapeDtypeStruct(term.shape, jnp.bfloat16) for term, _ in totals],
        [term for term, _ in totals] + [value for value, _ in pieces] + list(after),
        [VMEM] * (n + m) + [ANY] * len(after),
        flops=weight,
        name="sum_rows",
    )


def block_copies(block_refs, keys, rows, all_rows, sems):
    return [
        pltpu.make_async_copy(
            ref, all_rows.at[pl.ds(rel * rows + low, ref.shape[0]), :], sems.at[i]
        )
        for i, (ref, (rel, low)) in enumerate(zip(block_refs, keys))
    ]


def turned(values, cosine, sine):
    return values * cosine + pltpu.roll(values, HD // 2, 1) * sine


def project_into(rows_ref, weight_ref, out_ref, cos_ref=None, sin_ref=None):
    features = out_ref.shape[1]
    for low in range(0, features, CHUNK):
        high = min(low + CHUNK, features)
        values = jnp.dot(
            rows_ref[...], weight_ref[:, low:high], preferred_element_type=jnp.float32
        )
        for head in range(0, high - low, HD):
            piece = values[:, head : head + HD]
            if cos_ref is not None:
                piece = turned(piece, cos_ref[...], sin_ref[...])
            out_ref[:, low + head : low + head + HD] = piece.astype(jnp.bfloat16)


def project(blocks, weights, cosine, sine, rows, weight=1):
    keys = sorted(blocks)
    length, width = cosine.shape[0], blocks[0, 0].shape[1]
    features = weights[0].shape[1]
    n = len(keys)

    def kernel(*refs):
        block_refs, weight_refs = refs[:n], refs[n : n + 3]
        cos_ref, sin_ref = refs[n + 3 : n + 5]
        outs = refs[n + 5 : n + 8]
        all_rows, sems = refs[n + 8 :]
        copies = block_copies(block_refs, keys, rows, all_rows, sems)
        for copy in copies:
            copy.start()
        for copy in copies:
            copy.wait()
        for i in range(3):
            tables = (cos_ref, sin_ref) if i < 2 else ()
            project_into(all_rows, weight_refs[i], outs[i], *tables)

    return call(
        kernel,
        [jax.ShapeDtypeStruct((length, features), jnp.bfloat16)] * 3,
        [blocks[key] for key in keys] + list(weights) + [cosine, sine],
        [ANY] * n + [VMEM] * 5,
        [pltpu.VMEM((length, width), jnp.bfloat16), pltpu.SemaphoreType.DMA((n,))],
        flops=weight,
        vmem=20,
        name="project",
    )


def term_outs(rows, width, count, joined):
    bounds = part_bounds(rows, count)
    groups, waiting = messages_of(rows, count, joined)

    def shape(keys, dtype):
        height = sum(bounds[part][1] - bounds[part][0] for _, part in keys)
        return jax.ShapeDtypeStruct((height, width), dtype)

    return [shape(keys, jnp.bfloat16) for keys in groups] + [
        shape(keys, jnp.float32) for keys in waiting
    ]


def store_terms(values, low, refs, rows, count, joined):
    bounds = part_bounds(rows, count)
    groups, waiting = messages_of(rows, count, joined)
    for ref, keys in zip(refs, groups + waiting):
        at = 0
        for rel, part in keys:
            first, last = bounds[part]
            piece = values[rel * rows + first : rel * rows + last]
            ref[at : at + last - first, low : low + values.shape[1]] = piece.astype(ref.dtype)
            at += last - first


def backward_heads(blocks, qkv, weight, cosine, sine, rows):
    in_keys = sorted(blocks)
    length, width = cosine.shape[0], blocks[0, 0].shape[1]
    features = qkv[0].shape[1]
    n = len(in_keys)
    step = min(length, 512)

    def kernel(*refs):
        block_refs, weight_ref = refs[:n], refs[n]
        q_ref, k_ref, v_ref, cos_ref, sin_ref = refs[n + 1 : n + 6]
        d_qkv = refs[n + 6 : n + 9]
        all_rows, d_attn, sems = refs[n + 9 :]
        copies = block_copies(block_refs, in_keys, rows, all_rows, sems)
        for copy in copies:
            copy.start()
        for copy in copies:
            copy.wait()
        project_into(all_rows, weight_ref, d_attn)

        for head in range(features // HD):
            cols = slice(head * HD, (head + 1) * HD)
            key, value = k_ref[:, cols], v_ref[:, cols]
            d_key, d_value = 0.0, 0.0
            for low in range(0, length, step):
                part = slice(low, low + step)
                query, grad = q_ref[part, cols], d_attn[part, cols]
                scores = lax.dot_general(key, query, NT, preferred_element_type=jnp.float32)
                top = jnp.max(scores, 0, keepdims=True)
                raised = jnp.exp2((scores - top) * EXP2_SCALE)
                probs = raised * (1.0 / jnp.sum(raised, 0, keepdims=True))
                d_value += jnp.dot(
                    probs.astype(jnp.bfloat16), grad, preferred_element_type=jnp.float32
                )
                d_probs = lax.dot_general(value, grad, NT, preferred_element_type=jnp.float32)
                delta = jnp.sum(probs * d_probs, 0, keepdims=True)
                d_scores = (probs * (d_probs - delta) * HD ** (-0.5)).astype(jnp.bfloat16)
                d_key += jnp.dot(d_scores, query, preferred_element_type=jnp.float32)
                d_query = lax.dot_general(
                    key, d_scores, TN, preferred_element_type=jnp.float32
                ).T
                d_qkv[0][part, cols] = turned(
                    d_query, cos_ref[part, :], -sin_ref[part, :]
                ).astype(jnp.bfloat16)
            d_qkv[1][:, cols] = turned(d_key, cos_ref[...], -sin_ref[...]).astype(jnp.bfloat16)
            d_qkv[2][:, cols] = d_value.astype(jnp.bfloat16)

    return call(
        kernel,
        [jax.ShapeDtypeStruct((length, features), jnp.bfloat16)] * 3,
        [blocks[key] for key in in_keys] + [weight] + list(qkv) + [cosine, sine],
        [ANY] * n + [VMEM] * 6,
        [
            pltpu.VMEM((length, width), jnp.bfloat16),
            pltpu.VMEM((length, features), jnp.bfloat16),
            pltpu.SemaphoreType.DMA((n,)),
        ],
        vmem=28,
        flops=HEADS_WEIGHT,
        name="backward_heads",
    )


def backward_terms(d_qkv, weights, rows, count, joined, after=()):
    length, features = d_qkv[0].shape
    width = weights[0].shape[0]
    shapes = term_outs(rows, width, count, joined)

    def kernel(*refs):
        grads, weight_refs = refs[:3], refs[3:6]
        own_ref, *outs = refs[6 + len(after) :]
        for low in range(0, width, CHUNK):
            total = 0.0
            for i in range(3):
                total += lax.dot_general(
                    grads[i][...],
                    weight_refs[i][low : low + CHUNK, :],
                    NT,
                    preferred_element_type=jnp.float32,
                )
            own_ref[:, low : low + CHUNK] = total[:rows]
            store_terms(total, low, outs, rows, count, joined)

    own, *terms = call(
        kernel,
        [jax.ShapeDtypeStruct((rows, width), jnp.float32)] + shapes,
        list(d_qkv) + list(weights) + list(after),
        [VMEM] * 6 + [ANY] * len(after),
        vmem=24,
        flops=TERMS_WEIGHT,
        name="backward_terms",
    )
    return own, terms


def forward_terms(qkv, act_in, weight, rows, count, joined, after=()):
    length, features = qkv[0].shape
    width = weight.shape[0]
    shapes = term_outs(rows, width, count, joined)
    step = min(length, 512)

    def kernel(*refs):
        q_ref, k_ref, v_ref, act_ref, weight_ref = refs[:5]
        own_ref, *outs = refs[5 + len(after) : -1]
        attn = refs[-1]
        for head in range(features // HD):
            cols = slice(head * HD, (head + 1) * HD)
            for low in range(0, length, step):
                part = slice(low, low + step)
                scores = lax.dot_general(
                    q_ref[part, cols], k_ref[:, cols], NT, preferred_element_type=jnp.float32
                )
                top = jnp.max(scores, 1, keepdims=True)
                raised = jnp.exp2((scores - top) * EXP2_SCALE)
                total = jnp.sum(raised, 1, keepdims=True)
                mixed = jnp.dot(
                    raised.astype(jnp.bfloat16), v_ref[:, cols], preferred_element_type=jnp.float32
                )
                attn[part, cols] = (mixed * (1.0 / total)).astype(jnp.bfloat16)

        for low in range(0, width, CHUNK):
            total = lax.dot_general(
                attn[...], weight_ref[low : low + CHUNK, :], NT, preferred_element_type=jnp.float32
            )
            own = total[:rows] + act_ref[:, low : low + CHUNK]
            own_ref[:, low : low + CHUNK] = own.astype(jnp.bfloat16)
            store_terms(total, low, outs, rows, count, joined)

    own, *terms = call(
        kernel,
        [jax.ShapeDtypeStruct((rows, width), jnp.bfloat16)] + shapes,
        list(qkv) + [act_in, weight, *after],
        [VMEM] * 5 + [ANY] * len(after),
        [pltpu.VMEM((length, features), jnp.bfloat16)],
        vmem=24,
        flops=FORWARD_WEIGHT,
        name="forward_terms",
    )
    return own, terms


def input_grad(own, pieces, saved, grad, inv, gain, bounds, after=()):
    keys = sorted(pieces)

    def kernel(own_ref, saved_ref, grad_ref, inv_ref, gain_ref, *refs):
        out_ref = refs[-1]
        for part, (low, high) in enumerate(bounds):
            total = own_ref[low:high, :]
            for ref, key in zip(refs, keys):
                if key[1] == part:
                    first = pieces[key][1]
                    total = total + ref[first : first + high - low, :].astype(jnp.float32)
            total = total * gain_ref[...]
            saved_rows = saved_ref[low:high, :]
            mean = jnp.mean(saved_rows * total, -1, keepdims=True)
            inv_rows = inv_ref[low:high, :]
            out_ref[low:high, :] = (
                grad_ref[low:high, :]
                + inv_rows * total
                - saved_rows * (inv_rows * inv_rows * inv_rows * mean)
            ).astype(jnp.bfloat16)

    return call(
        kernel,
        [jax.ShapeDtypeStruct(own.shape, jnp.bfloat16)],
        [own, saved, grad, inv, gain] + [pieces[key][0] for key in keys] + list(after),
        [VMEM] * (5 + len(keys)) + [ANY] * len(after),
        flops=INPUT_GRAD_WEIGHT,
        name="input_grad",
    )[0]


def added_pieces(total, pieces, refs, part, height):
    for ref, (key, (_, first)) in zip(refs, pieces.items()):
        if key[1] == part:
            total = total + ref[first : first + height, :].astype(jnp.float32)
    return total


def activation_sum(base, pieces, bounds):
    def kernel(base_ref, *refs):
        out_ref, mark_ref = refs[-2:]
        for part, (low, high) in enumerate(bounds):
            total = base_ref[low:high, :].astype(jnp.float32)
            out_ref[0, low:high, :] = added_pieces(total, pieces, refs, part, high - low)
        mark_ref[...] = jnp.zeros_like(mark_ref)

    return call(
        kernel,
        [
            jax.ShapeDtypeStruct((1, *base.shape), jnp.float32),
            jax.ShapeDtypeStruct((8, LANES), jnp.float32),
        ],
        [base] + [value for value, _ in pieces.values()],
        [VMEM] * (1 + len(pieces)),
        flops=LAST_SUM_WEIGHT,
        name="activation_sum",
    )


def widened(values, bounds, after=()):
    def kernel(in_any, *refs):
        out_ref, held, sems = refs[-3:]
        copies = [
            pltpu.make_async_copy(
                in_any.at[pl.ds(low, high - low), :],
                held.at[pl.ds(low, high - low), :],
                sems.at[i],
            )
            for i, (low, high) in enumerate(bounds)
        ]
        for copy in copies:
            copy.start()
        for copy, (low, high) in zip(copies, bounds):
            copy.wait()
            out_ref[0, low:high, :] = held[low:high, :].astype(jnp.float32)

    return call(
        kernel,
        [jax.ShapeDtypeStruct((1, *values.shape), jnp.float32)],
        [values, *after],
        [ANY] * (1 + len(after)),
        [
            pltpu.VMEM(values.shape, values.dtype),
            pltpu.SemaphoreType.DMA((len(bounds),)),
        ],
        name="widen",
    )[0]


def rope_tables(positions):
    half_dim = HD // 2
    inverse = 10000.0 ** (-(jnp.arange(half_dim).astype(jnp.float32) * 2.0 / HD))
    angles = positions.astype(jnp.float32)[:, None] * inverse[None, :]
    cosine, sine = jnp.cos(angles), jnp.sin(angles)
    return jnp.concatenate([cosine, cosine], 1), jnp.concatenate([-sine, sine], 1)


def shards(x_fwd, x_bwd, grad_in, gain, w_query, w_key, w_value, w_out):
    act_in, saved_in, grad = x_fwd[0], x_bwd[0], grad_in[0]
    rows = act_in.shape[0]
    count = lax.axis_size("seq")
    bounds = part_bounds(rows, count)
    own_query, own_key, own_value, own_out = w_query[0], w_key[0], w_value[0], w_out[0]

    block_of = lax.axis_index("seq") ^ jnp.arange(count)
    positions = (block_of[:, None] * rows + jnp.arange(rows)[None, :]).reshape(-1)
    cosine, sine = rope_tables(positions)

    whole = [(0, rows)]
    projections = (own_query, own_key, own_value)
    (normed_bwd,), inv_bwd = normed_rows(saved_in, gain, whole, vmem=62)
    grad_low = cast_rows(grad, [normed_bwd, cosine, sine])
    all_bwd = gather_first(normed_bwd, "saved")
    all_grad = gather_first(grad_low, "grad")
    normed_fwd, _ = normed_rows(act_in, gain, bounds)
    picked = picked_rows(second_hops(all_bwd, bounds), [grad_low])
    all_bwd = gather_rest(all_bwd, picked, bounds, "saved")
    n = len(bounds)
    handed_on = [(value, 0, value.shape[0]) for value in normed_fwd]
    picked = picked_rows(handed_on + second_hops(all_grad, bounds), picked)
    all_fwd = gather_parts({}, picked[:n], bounds, True, "input")
    all_grad = gather_rest(all_grad, picked[n:], bounds, "grad")

    qkv = project(all_bwd, projections, cosine, sine, rows)
    all_fwd = gather_parts(all_fwd, picked_rows(handed_on, qkv[:1]), bounds, False, "input")
    d_qkv = backward_heads(all_grad, qkv, own_out, cosine, sine, rows)
    picked = picked_rows(second_hops(all_fwd, bounds), d_qkv[:1])
    all_fwd = gather_rest(all_fwd, picked, bounds, "input")
    d_own, d_terms = backward_terms(d_qkv, projections, rows, count, True, picked)
    qkv = project(all_fwd, projections, cosine, sine, rows, FORWARD_WEIGHT)
    own, terms = forward_terms(qkv, act_in, own_out, rows, count, False)

    back = Scatter(d_terms, rows, True, across, "grad")
    front = Scatter(
        terms, rows, False, lambda value, bit: across_and_on(value, 1 << bit), "branch"
    )
    back.send_groups()
    front.send_groups()
    d_sums = back.send_sums([terms[0]])
    own = across_and_on(own, 0)
    sums = front.send_sums(d_sums, SUMS_WEIGHT)
    d_input = input_grad(
        d_own, back.final, saved_in, grad, inv_bwd, gain, bounds, [own, *sums]
    )
    act_next, mark = activation_sum(own, front.final, bounds)
    return (act_next, widened(passed_along(d_input, "pipe", -1), bounds, [mark]))


def solution(mesh):
    placed = (
        P("pipe", "seq", None),
        P("pipe", "seq", None),
        P("pipe", "seq", None),
        P("pipe", None),
        P("pipe", None, "seq"),
        P("pipe", None, "seq"),
        P("pipe", None, "seq"),
        P("pipe", None, "seq"),
    )
    return jax.shard_map(
        shards,
        mesh=mesh,
        in_specs=placed,
        out_specs=(P("pipe", "seq", None), P("pipe", "seq", None)),
        check_vma=False,
    )
```

```python
import functools
import math

import jax
import jax.numpy as jnp
from jax import lax
from jax.experimental import pallas as pl
from jax.experimental.pallas import tpu as pltpu
from jax.sharding import PartitionSpec as P

HD = 128
LANES = 128
CHUNK = 256
EXP2_SCALE = HD ** (-0.5) * math.log2(math.e)
NT = (((1,), (1,)), ((), ()))
TN = (((0,), (0,)), ((), ()))
HEADS_WEIGHT = 8_000_000_000
TERMS_WEIGHT = 3_000_000_000
INPUT_GRAD_WEIGHT = 8_000_000_000
LAST_SUM_WEIGHT = 8_000_000_000
FORWARD_WEIGHT = 5_000_000_000
SUMS_WEIGHT = 1_000_000_000
MIB = 1024 * 1024


def bits_of(number):
    return [bit for bit in range(number.bit_length()) if (number >> bit) & 1]


def by_distance(count):
    return sorted(range(1, count), key=lambda rel: (len(bits_of(rel)), rel))


def part_bounds(rows, count):
    parts = 2 if count > 2 else 1
    return [(rows * i // parts, rows * (i + 1) // parts) for i in range(parts)]


def last_bit(rel, part):
    bits = bits_of(rel)
    return bits[part % len(bits)]


def ways_to(rel, bounds):
    ways = {}
    for part, (low, high) in enumerate(bounds):
        bit = last_bit(rel, part)
        ways[bit] = (min(low, ways.get(bit, (low, high))[0]), high)
    return [(bit, low, high) for bit, (low, high) in ways.items()]


def across(value, bit):
    count = lax.axis_size("seq")
    return lax.ppermute(value, "seq", [(i, i ^ (1 << bit)) for i in range(count)])


def across_and_on(value, flip):
    count, sections = lax.axis_size("seq"), lax.axis_size("pipe")
    pairs = [
        (p * count + i, (p + 1) % sections * count + (i ^ flip))
        for p in range(sections)
        for i in range(count)
    ]
    return lax.ppermute(value, ("pipe", "seq"), pairs)


def passed_along(value, axis, steps):
    count = lax.axis_size(axis)
    pairs = [(source, (source + steps) % count) for source in range(count)]
    return lax.ppermute(value, axis, pairs)


def onward_rows(count, bounds):
    return [
        (rel ^ (1 << bit), bit, low, high)
        for rel in by_distance(count)
        for bit, low, high in ways_to(rel, bounds)
    ]


def goes_on(rel, low, count, bounds):
    return any(
        rel == at and first <= low < last for at, _, first, last in onward_rows(count, bounds)
    )


def gather_first(own, what):
    count = lax.axis_size("seq")
    blocks = {(0, 0): own}
    for rel in by_distance(count):
        if len(bits_of(rel)) == 1:
            with jax.named_scope(f"gather_{what}_block{rel}"):
                blocks[rel, 0] = across(own, bits_of(rel)[0])
    return blocks


def gather_parts(blocks, own_parts, bounds, early, what):
    count = lax.axis_size("seq")
    for rel in by_distance(count):
        for value, (low, _) in zip(own_parts, bounds):
            blocks.setdefault((0, low), value)
            if len(bits_of(rel)) == 1 and goes_on(rel, low, count, bounds) == early:
                with jax.named_scope(f"gather_{what}_block{rel}_first{low}"):
                    blocks[rel, low] = across(value, bits_of(rel)[0])
    return blocks


def second_hops(blocks, bounds):
    hops = []
    for rel, _, low, high in onward_rows(lax.axis_size("seq"), bounds):
        if len(bits_of(rel)) == 1:
            first = low if (rel, low) in blocks else 0
            hops.append((blocks[rel, first], low - first, high - first))
    return hops


def gather_rest(blocks, picked, bounds, what):
    count = lax.axis_size("seq")
    picked = list(picked)
    for rel, bit, low, high in onward_rows(count, bounds):
        if rel == 0:
            continue
        value = picked.pop(0) if len(bits_of(rel)) == 1 else blocks[rel, low]
        if value.shape[0] > high - low:
            value = value[: high - low]
        with jax.named_scope(f"gather_{what}_block{rel ^ (1 << bit)}_row{low}"):
            blocks[rel ^ (1 << bit), low] = across(value, bit)
    return blocks


def messages_of(rows, count, joined):
    parts = range(len(part_bounds(rows, count)))
    later = {
        (rel ^ (1 << last_bit(rel, part)), part)
        for rel in range(1, count)
        for part in parts
        if len(bits_of(rel)) > 1
    }
    groups, waiting = {}, {}
    for rel in reversed(by_distance(count)):
        for part in parts:
            key = (rel, part)
            if not joined and len(bits_of(rel)) == 1:
                waiting.setdefault(rel, []).append(key)
            elif key in later:
                waiting[key] = [key]
            else:
                groups.setdefault(last_bit(*key) if joined else key, []).append(key)
    return list(groups.values()), list(waiting.values())


class Scatter:

    def __init__(self, terms, rows, joined, send_last, what):
        count = lax.axis_size("seq")
        self.bounds = part_bounds(rows, count)
        self.groups, waiting = messages_of(rows, count, joined)
        self.leaving = list(terms[: len(self.groups)])
        self.waiting = list(zip(waiting, terms[len(self.groups) :]))
        self.send_last, self.what = send_last, what
        self.arrived, self.final = {}, {}

    def send(self, value, keys):
        bit = last_bit(*keys[0])
        targets = [(rel ^ (1 << bit), part) for rel, part in keys]
        onward = any(rel for rel, _ in targets)
        with jax.named_scope(f"scatter_{self.what}_block{keys[0][0]}_part{keys[0][1]}"):
            moved = (across if onward else self.send_last)(value, bit)
        first = 0
        for key, target in zip(keys, targets):
            if target[0]:
                self.arrived.setdefault(target, []).append((moved, first))
            else:
                self.final[key] = (moved, first)
            first += self.bounds[key[1]][1] - self.bounds[key[1]][0]

    def send_groups(self):
        for value, keys in zip(self.leaving, self.groups):
            self.send(value, keys)

    def send_sums(self, after=(), weight=1):
        sums = []
        height = self.bounds[0][1] - self.bounds[0][0]
        levels = {len(bits_of(keys[0][0])) for keys, _ in self.waiting}
        for level in sorted(levels, reverse=True):
            found = [pair for pair in self.waiting if len(bits_of(pair[0][0][0])) == level]
            totals = [
                (term, [self.arrived.get(key, []) for key in keys]) for keys, term in found
            ]
            results = sum_rows(totals, height, after, weight)
            sums += results
            for (keys, _), value in zip(found, results):
                self.send(value, keys)
        return sums


def call(kernel, out_shapes, operands, in_specs, scratch=(), flops=1, vmem=10, name=None):
    return pl.pallas_call(
        kernel,
        out_shape=out_shapes,
        in_specs=in_specs,
        out_specs=[pl.BlockSpec(memory_space=pltpu.VMEM)] * len(out_shapes),
        scratch_shapes=list(scratch),
        compiler_params=pltpu.CompilerParams(vmem_limit_bytes=vmem * MIB),
        cost_estimate=pl.CostEstimate(flops=int(flops), bytes_accessed=1, transcendentals=0),
        name=name,
    )(*operands)


ANY = pl.BlockSpec(memory_space=pl.ANY)
HBM = pl.BlockSpec(memory_space=pltpu.HBM)
VMEM = pl.BlockSpec(memory_space=pltpu.VMEM)


def normed_rows(inputs, gain, bounds, after=(), vmem=10):
    rows, width = inputs.shape

    def kernel(x_any, gain_any, *refs):
        *outs, inv_ref, x_ref, gain_ref, sems = refs[len(after) :]
        copies = [
            pltpu.make_async_copy(source, held, sems.at[i])
            for i, (source, held) in enumerate([(x_any, x_ref), (gain_any, gain_ref)])
        ]
        for copy in copies:
            copy.start()
        for copy in copies:
            copy.wait()
        for out_ref, (low, high) in zip(outs, bounds):
            x = x_ref[low:high, :]
            inv = lax.rsqrt(jnp.mean(x * x, -1, keepdims=True) + 1e-05)
            out_ref[...] = (x * inv * gain_ref[...]).astype(jnp.bfloat16)
            inv_ref[low:high, :] = inv

    *parts, inv = call(
        kernel,
        [jax.ShapeDtypeStruct((high - low, width), jnp.bfloat16) for low, high in bounds]
        + [jax.ShapeDtypeStruct((rows, 1), jnp.float32)],
        [inputs, gain, *after],
        [HBM] * 2 + [ANY] * len(after),
        [
            pltpu.VMEM(inputs.shape, jnp.float32),
            pltpu.VMEM(gain.shape, jnp.float32),
            pltpu.SemaphoreType.DMA((2,)),
        ],
        vmem=vmem,
        name="norm",
    )
    return parts, inv


def picked_rows(pieces, after=()):
    n = len(pieces)

    def kernel(*refs):
        outs, sems = refs[n + len(after) : -1], refs[-1]
        copies = [
            pltpu.make_async_copy(ref.at[pl.ds(low, high - low), :], out_ref, sems.at[i])
            for i, (ref, out_ref, (_, low, high)) in enumerate(zip(refs, outs, pieces))
        ]
        for copy in copies:
            copy.start()
        for copy in copies:
            copy.wait()

    return call(
        kernel,
        [
            jax.ShapeDtypeStruct((high - low, value.shape[1]), value.dtype)
            for value, low, high in pieces
        ],
        [value for value, _, _ in pieces] + list(after),
        [ANY] * (n + len(after)),
        [pltpu.SemaphoreType.DMA((n,))],
        name="pick",
    )


def cast_rows(inputs, after=()):
    def kernel(x_ref, *refs):
        refs[len(after)][...] = x_ref[...].astype(jnp.bfloat16)

    return call(
        kernel,
        [jax.ShapeDtypeStruct(inputs.shape, jnp.bfloat16)],
        (inputs, *after),
        [VMEM] + [ANY] * len(after),
        name="cast",
    )[0]


def sum_rows(totals, height, after=(), weight=1):
    pieces = [piece for _, parts in totals for moved in parts for piece in moved]
    n, m = len(totals), len(pieces)

    def kernel(*refs):
        arrivals, outs = list(refs[n : n + m]), refs[-n:]
        for (_, parts), term_ref, out_ref in zip(totals, refs, outs):
            for i, moved in enumerate(parts):
                here = slice(i * height, (i + 1) * height)
                total = term_ref[here, :]
                for _, first in moved:
                    ref = arrivals.pop(0)
                    total = total + ref[first : first + height, :].astype(jnp.float32)
                out_ref[here, :] = total.astype(jnp.bfloat16)

    return call(
        kernel,
        [jax.ShapeDtypeStruct(term.shape, jnp.bfloat16) for term, _ in totals],
        [term for term, _ in totals] + [value for value, _ in pieces] + list(after),
        [VMEM] * (n + m) + [ANY] * len(after),
        flops=weight,
        name="sum_rows",
    )


def block_copies(block_refs, keys, rows, all_rows, sems):
    return [
        pltpu.make_async_copy(
            ref, all_rows.at[pl.ds(rel * rows + low, ref.shape[0]), :], sems.at[i]
        )
        for i, (ref, (rel, low)) in enumerate(zip(block_refs, keys))
    ]


def turned(values, cosine, sine):
    return values * cosine + pltpu.roll(values, HD // 2, 1) * sine


def project_into(rows_ref, weight_ref, out_ref, cos_ref=None, sin_ref=None):
    features = out_ref.shape[1]
    for low in range(0, features, CHUNK):
        high = min(low + CHUNK, features)
        values = jnp.dot(
            rows_ref[...], weight_ref[:, low:high], preferred_element_type=jnp.float32
        )
        for head in range(0, high - low, HD):
            piece = values[:, head : head + HD]
            if cos_ref is not None:
                piece = turned(piece, cos_ref[...], sin_ref[...])
            out_ref[:, low + head : low + head + HD] = piece.astype(jnp.bfloat16)


def project(blocks, weights, cosine, sine, rows, weight=1):
    keys = sorted(blocks)
    length, width = cosine.shape[0], blocks[0, 0].shape[1]
    features = weights[0].shape[1]
    n = len(keys)

    def kernel(*refs):
        block_refs, weight_refs = refs[:n], refs[n : n + 3]
        cos_ref, sin_ref = refs[n + 3 : n + 5]
        outs = refs[n + 5 : n + 8]
        all_rows, sems = refs[n + 8 :]
        copies = block_copies(block_refs, keys, rows, all_rows, sems)
        for copy in copies:
            copy.start()
        for copy in copies:
            copy.wait()
        for i in range(3):
            tables = (cos_ref, sin_ref) if i < 2 else ()
            project_into(all_rows, weight_refs[i], outs[i], *tables)

    return call(
        kernel,
        [jax.ShapeDtypeStruct((length, features), jnp.bfloat16)] * 3,
        [blocks[key] for key in keys] + list(weights) + [cosine, sine],
        [ANY] * n + [VMEM] * 5,
        [pltpu.VMEM((length, width), jnp.bfloat16), pltpu.SemaphoreType.DMA((n,))],
        flops=weight,
        vmem=20,
        name="project",
    )


def term_outs(rows, width, count, joined):
    bounds = part_bounds(rows, count)
    groups, waiting = messages_of(rows, count, joined)

    def shape(keys, dtype):
        height = sum(bounds[part][1] - bounds[part][0] for _, part in keys)
        return jax.ShapeDtypeStruct((height, width), dtype)

    return [shape(keys, jnp.bfloat16) for keys in groups] + [
        shape(keys, jnp.float32) for keys in waiting
    ]


def store_terms(values, low, refs, rows, count, joined):
    bounds = part_bounds(rows, count)
    groups, waiting = messages_of(rows, count, joined)
    for ref, keys in zip(refs, groups + waiting):
        at = 0
        for rel, part in keys:
            first, last = bounds[part]
            piece = values[rel * rows + first : rel * rows + last]
            ref[at : at + last - first, low : low + values.shape[1]] = piece.astype(ref.dtype)
            at += last - first


def backward_heads(blocks, qkv, weight, cosine, sine, rows):
    in_keys = sorted(blocks)
    length, width = cosine.shape[0], blocks[0, 0].shape[1]
    features = qkv[0].shape[1]
    n = len(in_keys)
    step = min(length, 512)

    def kernel(*refs):
        block_refs, weight_ref = refs[:n], refs[n]
        q_ref, k_ref, v_ref, cos_ref, sin_ref = refs[n + 1 : n + 6]
        d_qkv = refs[n + 6 : n + 9]
        all_rows, d_attn, sems = refs[n + 9 :]
        copies = block_copies(block_refs, in_keys, rows, all_rows, sems)
        for copy in copies:
            copy.start()
        for copy in copies:
            copy.wait()
        project_into(all_rows, weight_ref, d_attn)

        for head in range(features // HD):
            cols = slice(head * HD, (head + 1) * HD)
            key, value = k_ref[:, cols], v_ref[:, cols]
            d_key, d_value = 0.0, 0.0
            for low in range(0, length, step):
                part = slice(low, low + step)
                query, grad = q_ref[part, cols], d_attn[part, cols]
                scores = lax.dot_general(key, query, NT, preferred_element_type=jnp.float32)
                top = jnp.max(scores, 0, keepdims=True)
                raised = jnp.exp2((scores - top) * EXP2_SCALE)
                probs = raised * (1.0 / jnp.sum(raised, 0, keepdims=True))
                d_value += jnp.dot(
                    probs.astype(jnp.bfloat16), grad, preferred_element_type=jnp.float32
                )
                d_probs = lax.dot_general(value, grad, NT, preferred_element_type=jnp.float32)
                delta = jnp.sum(probs * d_probs, 0, keepdims=True)
                d_scores = (probs * (d_probs - delta) * HD ** (-0.5)).astype(jnp.bfloat16)
                d_key += jnp.dot(d_scores, query, preferred_element_type=jnp.float32)
                d_query = lax.dot_general(
                    key, d_scores, TN, preferred_element_type=jnp.float32
                ).T
                d_qkv[0][part, cols] = turned(
                    d_query, cos_ref[part, :], -sin_ref[part, :]
                ).astype(jnp.bfloat16)
            d_qkv[1][:, cols] = turned(d_key, cos_ref[...], -sin_ref[...]).astype(jnp.bfloat16)
            d_qkv[2][:, cols] = d_value.astype(jnp.bfloat16)

    return call(
        kernel,
        [jax.ShapeDtypeStruct((length, features), jnp.bfloat16)] * 3,
        [blocks[key] for key in in_keys] + [weight] + list(qkv) + [cosine, sine],
        [ANY] * n + [VMEM] * 6,
        [
            pltpu.VMEM((length, width), jnp.bfloat16),
            pltpu.VMEM((length, features), jnp.bfloat16),
            pltpu.SemaphoreType.DMA((n,)),
        ],
        vmem=28,
        flops=HEADS_WEIGHT,
        name="backward_heads",
    )


def backward_terms(d_qkv, weights, rows, count, joined, after=()):
    length, features = d_qkv[0].shape
    width = weights[0].shape[0]
    shapes = term_outs(rows, width, count, joined)

    def kernel(*refs):
        grads, weight_refs = refs[:3], refs[3:6]
        own_ref, *outs = refs[6 + len(after) :]
        for low in range(0, width, CHUNK):
            total = 0.0
            for i in range(3):
                total += lax.dot_general(
                    grads[i][...],
                    weight_refs[i][low : low + CHUNK, :],
                    NT,
                    preferred_element_type=jnp.float32,
                )
            own_ref[:, low : low + CHUNK] = total[:rows]
            store_terms(total, low, outs, rows, count, joined)

    own, *terms = call(
        kernel,
        [jax.ShapeDtypeStruct((rows, width), jnp.float32)] + shapes,
        list(d_qkv) + list(weights) + list(after),
        [VMEM] * 6 + [ANY] * len(after),
        vmem=24,
        flops=TERMS_WEIGHT,
        name="backward_terms",
    )
    return own, terms


def forward_terms(qkv, act_in, weight, rows, count, joined, after=()):
    length, features = qkv[0].shape
    width = weight.shape[0]
    shapes = term_outs(rows, width, count, joined)
    step = min(length, 512)

    def kernel(*refs):
        q_ref, k_ref, v_ref, act_ref, weight_ref = refs[:5]
        own_ref, *outs = refs[5 + len(after) : -1]
        attn = refs[-1]
        for head in range(features // HD):
            cols = slice(head * HD, (head + 1) * HD)
            for low in range(0, length, step):
                part = slice(low, low + step)
                scores = lax.dot_general(
                    q_ref[part, cols], k_ref[:, cols], NT, preferred_element_type=jnp.float32
                )
                top = jnp.max(scores, 1, keepdims=True)
                raised = jnp.exp2((scores - top) * EXP2_SCALE)
                total = jnp.sum(raised, 1, keepdims=True)
                mixed = jnp.dot(
                    raised.astype(jnp.bfloat16), v_ref[:, cols], preferred_element_type=jnp.float32
                )
                attn[part, cols] = (mixed * (1.0 / total)).astype(jnp.bfloat16)

        for low in range(0, width, CHUNK):
            total = lax.dot_general(
                attn[...], weight_ref[low : low + CHUNK, :], NT, preferred_element_type=jnp.float32
            )
            own = total[:rows] + act_ref[:, low : low + CHUNK]
            own_ref[:, low : low + CHUNK] = own.astype(jnp.bfloat16)
            store_terms(total, low, outs, rows, count, joined)

    own, *terms = call(
        kernel,
        [jax.ShapeDtypeStruct((rows, width), jnp.bfloat16)] + shapes,
        list(qkv) + [act_in, weight, *after],
        [VMEM] * 5 + [ANY] * len(after),
        [pltpu.VMEM((length, features), jnp.bfloat16)],
        vmem=24,
        flops=FORWARD_WEIGHT,
        name="forward_terms",
    )
    return own, terms


def input_grad(own, pieces, saved, grad, inv, gain, bounds, after=()):
    keys = sorted(pieces)

    def kernel(own_ref, saved_ref, grad_ref, inv_ref, gain_ref, *refs):
        out_ref = refs[-1]
        for part, (low, high) in enumerate(bounds):
            total = own_ref[low:high, :]
            for ref, key in zip(refs, keys):
                if key[1] == part:
                    first = pieces[key][1]
                    total = total + ref[first : first + high - low, :].astype(jnp.float32)
            total = total * gain_ref[...]
            saved_rows = saved_ref[low:high, :]
            mean = jnp.mean(saved_rows * total, -1, keepdims=True)
            inv_rows = inv_ref[low:high, :]
            out_ref[low:high, :] = (
                grad_ref[low:high, :]
                + inv_rows * total
                - saved_rows * (inv_rows * inv_rows * inv_rows * mean)
            ).astype(jnp.bfloat16)

    return call(
        kernel,
        [jax.ShapeDtypeStruct(own.shape, jnp.bfloat16)],
        [own, saved, grad, inv, gain] + [pieces[key][0] for key in keys] + list(after),
        [VMEM] * (5 + len(keys)) + [ANY] * len(after),
        flops=INPUT_GRAD_WEIGHT,
        name="input_grad",
    )[0]


def added_pieces(total, pieces, refs, part, height):
    for ref, (key, (_, first)) in zip(refs, pieces.items()):
        if key[1] == part:
            total = total + ref[first : first + height, :].astype(jnp.float32)
    return total


def activation_sum(base, pieces, bounds):
    def kernel(base_ref, *refs):
        out_ref, mark_ref = refs[-2:]
        for part, (low, high) in enumerate(bounds):
            total = base_ref[low:high, :].astype(jnp.float32)
            out_ref[0, low:high, :] = added_pieces(total, pieces, refs, part, high - low)
        mark_ref[...] = jnp.zeros_like(mark_ref)

    return call(
        kernel,
        [
            jax.ShapeDtypeStruct((1, *base.shape), jnp.float32),
            jax.ShapeDtypeStruct((8, LANES), jnp.float32),
        ],
        [base] + [value for value, _ in pieces.values()],
        [VMEM] * (1 + len(pieces)),
        flops=LAST_SUM_WEIGHT,
        name="activation_sum",
    )


def widened(values, bounds, after=()):
    def kernel(in_any, *refs):
        out_ref, held, sems = refs[-3:]
        copies = [
            pltpu.make_async_copy(
                in_any.at[pl.ds(low, high - low), :],
                held.at[pl.ds(low, high - low), :],
                sems.at[i],
            )
            for i, (low, high) in enumerate(bounds)
        ]
        for copy in copies:
            copy.start()
        for copy, (low, high) in zip(copies, bounds):
            copy.wait()
            out_ref[0, low:high, :] = held[low:high, :].astype(jnp.float32)

    return call(
        kernel,
        [jax.ShapeDtypeStruct((1, *values.shape), jnp.float32)],
        [values, *after],
        [ANY] * (1 + len(after)),
        [
            pltpu.VMEM(values.shape, values.dtype),
            pltpu.SemaphoreType.DMA((len(bounds),)),
        ],
        name="widen",
    )[0]


def rope_tables(positions):
    half_dim = HD // 2
    inverse = 10000.0 ** (-(jnp.arange(half_dim).astype(jnp.float32) * 2.0 / HD))
    angles = positions.astype(jnp.float32)[:, None] * inverse[None, :]
    cosine, sine = jnp.cos(angles), jnp.sin(angles)
    return jnp.concatenate([cosine, cosine], 1), jnp.concatenate([-sine, sine], 1)


def shards(x_fwd, x_bwd, grad_in, gain, w_query, w_key, w_value, w_out):
    act_in, saved_in, grad = x_fwd[0], x_bwd[0], grad_in[0]
    rows = act_in.shape[0]
    count = lax.axis_size("seq")
    bounds = part_bounds(rows, count)
    own_query, own_key, own_value, own_out = w_query[0], w_key[0], w_value[0], w_out[0]

    block_of = lax.axis_index("seq") ^ jnp.arange(count)
    positions = (block_of[:, None] * rows + jnp.arange(rows)[None, :]).reshape(-1)
    cosine, sine = rope_tables(positions)

    whole = [(0, rows)]
    projections = (own_query, own_key, own_value)
    (normed_bwd,), inv_bwd = normed_rows(saved_in, gain, whole, vmem=62)
    grad_low = cast_rows(grad, [normed_bwd, cosine, sine])
    all_bwd = gather_first(normed_bwd, "saved")
    all_grad = gather_first(grad_low, "grad")
    normed_fwd, _ = normed_rows(act_in, gain, bounds)
    picked = picked_rows(second_hops(all_bwd, bounds), [grad_low])
    all_bwd = gather_rest(all_bwd, picked, bounds, "saved")
    n = len(bounds)
    handed_on = [(value, 0, value.shape[0]) for value in normed_fwd]
    picked = picked_rows(handed_on + second_hops(all_grad, bounds), picked)
    all_fwd = gather_parts({}, picked[:n], bounds, True, "input")
    all_grad = gather_rest(all_grad, picked[n:], bounds, "grad")

    qkv = project(all_bwd, projections, cosine, sine, rows)
    all_fwd = gather_parts(all_fwd, picked_rows(handed_on, qkv[:1]), bounds, False, "input")
    d_qkv = backward_heads(all_grad, qkv, own_out, cosine, sine, rows)
    picked = picked_rows(second_hops(all_fwd, bounds), d_qkv[:1])
    all_fwd = gather_rest(all_fwd, picked, bounds, "input")
    d_own, d_terms = backward_terms(d_qkv, projections, rows, count, True, picked)
    qkv = project(all_fwd, projections, cosine, sine, rows, FORWARD_WEIGHT)
    own, terms = forward_terms(qkv, act_in, own_out, rows, count, False)

    back = Scatter(d_terms, rows, True, across, "grad")
    front = Scatter(
        terms, rows, False, lambda value, bit: across_and_on(value, 1 << bit), "branch"
    )
    back.send_groups()
    front.send_groups()
    d_sums = back.send_sums([terms[0]])
    own = across_and_on(own, 0)
    sums = front.send_sums(d_sums, SUMS_WEIGHT)
    d_input = input_grad(
        d_own, back.final, saved_in, grad, inv_bwd, gain, bounds, [own, *sums]
    )
    act_next, mark = activation_sum(own, front.final, bounds)
    return (act_next, widened(passed_along(d_input, "pipe", -1), bounds, [mark]))


def solution(mesh):
    placed = (
        P("pipe", "seq", None),
        P("pipe", "seq", None),
        P("pipe", "seq", None),
        P("pipe", None),
        P("pipe", None, "seq"),
        P("pipe", None, "seq"),
        P("pipe", None, "seq"),
        P("pipe", None, "seq"),
    )
    return jax.shard_map(
        shards,
        mesh=mesh,
        in_specs=placed,
        out_specs=(P("pipe", "seq", None), P("pipe", "seq", None)),
        check_vma=False,
    )
```

```python
import functools
import math

import jax
import jax.numpy as jnp
from jax import lax
from jax.experimental import pallas as pl
from jax.experimental.pallas import tpu as pltpu
from jax.sharding import PartitionSpec as P

HD = 128
LANES = 128
CHUNK = 512
EXP2_SCALE = HD ** (-0.5) * math.log2(math.e)
NT = (((1,), (1,)), ((), ()))
TN = (((0,), (0,)), ((), ()))
HEADS_WEIGHT = 8_000_000_000
TERMS_WEIGHT = 3_000_000_000
INPUT_GRAD_WEIGHT = 8_000_000_000
LAST_SUM_WEIGHT = 8_000_000_000
FORWARD_WEIGHT = 5_000_000_000
SUMS_WEIGHT = 1_000_000_000
MIB = 1024 * 1024


def bits_of(number):
    return [bit for bit in range(number.bit_length()) if (number >> bit) & 1]


def by_distance(count):
    return sorted(range(1, count), key=lambda rel: (len(bits_of(rel)), rel))


def part_bounds(rows, count):
    parts = 2 if count > 2 else 1
    return [(rows * i // parts, rows * (i + 1) // parts) for i in range(parts)]


def last_bit(rel, part):
    bits = bits_of(rel)
    return bits[part % len(bits)]


def ways_to(rel, bounds):
    ways = {}
    for part, (low, high) in enumerate(bounds):
        bit = last_bit(rel, part)
        ways[bit] = (min(low, ways.get(bit, (low, high))[0]), high)
    return [(bit, low, high) for bit, (low, high) in ways.items()]


def across(value, bit):
    count = lax.axis_size("seq")
    return lax.ppermute(value, "seq", [(i, i ^ (1 << bit)) for i in range(count)])


def across_and_on(value, flip):
    count, sections = lax.axis_size("seq"), lax.axis_size("pipe")
    pairs = [
        (p * count + i, (p + 1) % sections * count + (i ^ flip))
        for p in range(sections)
        for i in range(count)
    ]
    return lax.ppermute(value, ("pipe", "seq"), pairs)


def passed_along(value, axis, steps):
    count = lax.axis_size(axis)
    pairs = [(source, (source + steps) % count) for source in range(count)]
    return lax.ppermute(value, axis, pairs)


def onward_rows(count, bounds):
    return [
        (rel ^ (1 << bit), bit, low, high)
        for rel in by_distance(count)
        for bit, low, high in ways_to(rel, bounds)
    ]


def goes_on(rel, low, count, bounds):
    return any(
        rel == at and first <= low < last for at, _, first, last in onward_rows(count, bounds)
    )


def gather_first(own, what):
    count = lax.axis_size("seq")
    blocks = {(0, 0): own}
    for rel in by_distance(count):
        if len(bits_of(rel)) == 1:
            with jax.named_scope(f"gather_{what}_block{rel}"):
                blocks[rel, 0] = across(own, bits_of(rel)[0])
    return blocks


def gather_parts(blocks, own_parts, bounds, early, what):
    count = lax.axis_size("seq")
    for rel in by_distance(count):
        for value, (low, _) in zip(own_parts, bounds):
            blocks.setdefault((0, low), value)
            if len(bits_of(rel)) == 1 and goes_on(rel, low, count, bounds) == early:
                with jax.named_scope(f"gather_{what}_block{rel}_first{low}"):
                    blocks[rel, low] = across(value, bits_of(rel)[0])
    return blocks


def second_hops(blocks, bounds):
    hops = []
    for rel, _, low, high in onward_rows(lax.axis_size("seq"), bounds):
        if len(bits_of(rel)) == 1:
            first = low if (rel, low) in blocks else 0
            hops.append((blocks[rel, first], low - first, high - first))
    return hops


def gather_rest(blocks, picked, bounds, what):
    count = lax.axis_size("seq")
    picked = list(picked)
    for rel, bit, low, high in onward_rows(count, bounds):
        if rel == 0:
            continue
        value = picked.pop(0) if len(bits_of(rel)) == 1 else blocks[rel, low]
        if value.shape[0] > high - low:
            value = value[: high - low]
        with jax.named_scope(f"gather_{what}_block{rel ^ (1 << bit)}_row{low}"):
            blocks[rel ^ (1 << bit), low] = across(value, bit)
    return blocks


def messages_of(rows, count, joined):
    parts = range(len(part_bounds(rows, count)))
    later = {
        (rel ^ (1 << last_bit(rel, part)), part)
        for rel in range(1, count)
        for part in parts
        if len(bits_of(rel)) > 1
    }
    groups, waiting = {}, {}
    for rel in reversed(by_distance(count)):
        for part in parts:
            key = (rel, part)
            if not joined and len(bits_of(rel)) == 1:
                waiting.setdefault(rel, []).append(key)
            elif key in later:
                waiting[key] = [key]
            else:
                groups.setdefault(last_bit(*key) if joined else key, []).append(key)
    return list(groups.values()), list(waiting.values())


class Scatter:

    def __init__(self, terms, rows, joined, send_last, what):
        count = lax.axis_size("seq")
        self.bounds = part_bounds(rows, count)
        self.groups, waiting = messages_of(rows, count, joined)
        self.leaving = list(terms[: len(self.groups)])
        self.waiting = list(zip(waiting, terms[len(self.groups) :]))
        self.send_last, self.what = send_last, what
        self.arrived, self.final = {}, {}

    def send(self, value, keys):
        bit = last_bit(*keys[0])
        targets = [(rel ^ (1 << bit), part) for rel, part in keys]
        onward = any(rel for rel, _ in targets)
        with jax.named_scope(f"scatter_{self.what}_block{keys[0][0]}_part{keys[0][1]}"):
            moved = (across if onward else self.send_last)(value, bit)
        first = 0
        for key, target in zip(keys, targets):
            if target[0]:
                self.arrived.setdefault(target, []).append((moved, first))
            else:
                self.final[key] = (moved, first)
            first += self.bounds[key[1]][1] - self.bounds[key[1]][0]

    def send_groups(self):
        for value, keys in zip(self.leaving, self.groups):
            self.send(value, keys)

    def send_sums(self, after=(), weight=1):
        sums = []
        height = self.bounds[0][1] - self.bounds[0][0]
        levels = {len(bits_of(keys[0][0])) for keys, _ in self.waiting}
        for level in sorted(levels, reverse=True):
            found = [pair for pair in self.waiting if len(bits_of(pair[0][0][0])) == level]
            totals = [
                (term, [self.arrived.get(key, []) for key in keys]) for keys, term in found
            ]
            results = sum_rows(totals, height, after, weight)
            sums += results
            for (keys, _), value in zip(found, results):
                self.send(value, keys)
        return sums


def call(kernel, out_shapes, operands, in_specs, scratch=(), flops=1, vmem=10, name=None):
    return pl.pallas_call(
        kernel,
        out_shape=out_shapes,
        in_specs=in_specs,
        out_specs=[pl.BlockSpec(memory_space=pltpu.VMEM)] * len(out_shapes),
        scratch_shapes=list(scratch),
        compiler_params=pltpu.CompilerParams(vmem_limit_bytes=vmem * MIB),
        cost_estimate=pl.CostEstimate(flops=int(flops), bytes_accessed=1, transcendentals=0),
        name=name,
    )(*operands)


ANY = pl.BlockSpec(memory_space=pl.ANY)
HBM = pl.BlockSpec(memory_space=pltpu.HBM)
VMEM = pl.BlockSpec(memory_space=pltpu.VMEM)


def normed_rows(inputs, gain, bounds, after=(), vmem=10):
    rows, width = inputs.shape

    def kernel(x_any, gain_any, *refs):
        *outs, inv_ref, x_ref, gain_ref, sems = refs[len(after) :]
        copies = [
            pltpu.make_async_copy(source, held, sems.at[i])
            for i, (source, held) in enumerate([(x_any, x_ref), (gain_any, gain_ref)])
        ]
        for copy in copies:
            copy.start()
        for copy in copies:
            copy.wait()
        for out_ref, (low, high) in zip(outs, bounds):
            x = x_ref[low:high, :]
            inv = lax.rsqrt(jnp.mean(x * x, -1, keepdims=True) + 1e-05)
            out_ref[...] = (x * inv * gain_ref[...]).astype(jnp.bfloat16)
            inv_ref[low:high, :] = inv

    *parts, inv = call(
        kernel,
        [jax.ShapeDtypeStruct((high - low, width), jnp.bfloat16) for low, high in bounds]
        + [jax.ShapeDtypeStruct((rows, 1), jnp.float32)],
        [inputs, gain, *after],
        [HBM] * 2 + [ANY] * len(after),
        [
            pltpu.VMEM(inputs.shape, jnp.float32),
            pltpu.VMEM(gain.shape, jnp.float32),
            pltpu.SemaphoreType.DMA((2,)),
        ],
        vmem=vmem,
        name="norm",
    )
    return parts, inv


def picked_rows(pieces, after=()):
    n = len(pieces)

    def kernel(*refs):
        outs, sems = refs[n + len(after) : -1], refs[-1]
        copies = [
            pltpu.make_async_copy(ref.at[pl.ds(low, high - low), :], out_ref, sems.at[i])
            for i, (ref, out_ref, (_, low, high)) in enumerate(zip(refs, outs, pieces))
        ]
        for copy in copies:
            copy.start()
        for copy in copies:
            copy.wait()

    return call(
        kernel,
        [
            jax.ShapeDtypeStruct((high - low, value.shape[1]), value.dtype)
            for value, low, high in pieces
        ],
        [value for value, _, _ in pieces] + list(after),
        [ANY] * (n + len(after)),
        [pltpu.SemaphoreType.DMA((n,))],
        name="pick",
    )


def cast_rows(inputs, after=()):
    def kernel(x_ref, *refs):
        refs[len(after)][...] = x_ref[...].astype(jnp.bfloat16)

    return call(
        kernel,
        [jax.ShapeDtypeStruct(inputs.shape, jnp.bfloat16)],
        (inputs, *after),
        [VMEM] + [ANY] * len(after),
        name="cast",
    )[0]


def sum_rows(totals, height, after=(), weight=1):
    pieces = [piece for _, parts in totals for moved in parts for piece in moved]
    n, m = len(totals), len(pieces)

    def kernel(*refs):
        arrivals, outs = list(refs[n : n + m]), refs[-n:]
        for (_, parts), term_ref, out_ref in zip(totals, refs, outs):
            for i, moved in enumerate(parts):
                here = slice(i * height, (i + 1) * height)
                total = term_ref[here, :]
                for _, first in moved:
                    ref = arrivals.pop(0)
                    total = total + ref[first : first + height, :].astype(jnp.float32)
                out_ref[here, :] = total.astype(jnp.bfloat16)

    return call(
        kernel,
        [jax.ShapeDtypeStruct(term.shape, jnp.bfloat16) for term, _ in totals],
        [term for term, _ in totals] + [value for value, _ in pieces] + list(after),
        [VMEM] * (n + m) + [ANY] * len(after),
        flops=weight,
        name="sum_rows",
    )


def block_copies(block_refs, keys, rows, all_rows, sems):
    return [
        pltpu.make_async_copy(
            ref, all_rows.at[pl.ds(rel * rows + low, ref.shape[0]), :], sems.at[i]
        )
        for i, (ref, (rel, low)) in enumerate(zip(block_refs, keys))
    ]


def turned(values, cosine, sine):
    return values * cosine + pltpu.roll(values, HD // 2, 1) * sine


def project_into(rows_ref, weight_ref, out_ref, cos_ref=None, sin_ref=None):
    features = out_ref.shape[1]
    for low in range(0, features, CHUNK):
        high = min(low + CHUNK, features)
        values = jnp.dot(
            rows_ref[...], weight_ref[:, low:high], preferred_element_type=jnp.float32
        )
        for head in range(0, high - low, HD):
            piece = values[:, head : head + HD]
            if cos_ref is not None:
                piece = turned(piece, cos_ref[...], sin_ref[...])
            out_ref[:, low + head : low + head + HD] = piece.astype(jnp.bfloat16)


def project(blocks, weights, cosine, sine, rows, weight=1):
    keys = sorted(blocks)
    length, width = cosine.shape[0], blocks[0, 0].shape[1]
    features = weights[0].shape[1]
    n = len(keys)

    def kernel(*refs):
        block_refs, weight_refs = refs[:n], refs[n : n + 3]
        cos_ref, sin_ref = refs[n + 3 : n + 5]
        outs = refs[n + 5 : n + 8]
        all_rows, sems = refs[n + 8 :]
        copies = block_copies(block_refs, keys, rows, all_rows, sems)
        for copy in copies:
            copy.start()
        for copy in copies:
            copy.wait()
        for i in range(3):
            tables = (cos_ref, sin_ref) if i < 2 else ()
            project_into(all_rows, weight_refs[i], outs[i], *tables)

    return call(
        kernel,
        [jax.ShapeDtypeStruct((length, features), jnp.bfloat16)] * 3,
        [blocks[key] for key in keys] + list(weights) + [cosine, sine],
        [ANY] * n + [VMEM] * 5,
        [pltpu.VMEM((length, width), jnp.bfloat16), pltpu.SemaphoreType.DMA((n,))],
        flops=weight,
        vmem=20,
        name="project",
    )


def term_outs(rows, width, count, joined):
    bounds = part_bounds(rows, count)
    groups, waiting = messages_of(rows, count, joined)

    def shape(keys, dtype):
        height = sum(bounds[part][1] - bounds[part][0] for _, part in keys)
        return jax.ShapeDtypeStruct((height, width), dtype)

    return [shape(keys, jnp.bfloat16) for keys in groups] + [
        shape(keys, jnp.float32) for keys in waiting
    ]


def store_terms(values, low, refs, rows, count, joined):
    bounds = part_bounds(rows, count)
    groups, waiting = messages_of(rows, count, joined)
    for ref, keys in zip(refs, groups + waiting):
        at = 0
        for rel, part in keys:
            first, last = bounds[part]
            piece = values[rel * rows + first : rel * rows + last]
            ref[at : at + last - first, low : low + values.shape[1]] = piece.astype(ref.dtype)
            at += last - first


def backward_heads(blocks, qkv, weight, cosine, sine, rows):
    in_keys = sorted(blocks)
    length, width = cosine.shape[0], blocks[0, 0].shape[1]
    features = qkv[0].shape[1]
    n = len(in_keys)
    step = min(length, 512)

    def kernel(*refs):
        block_refs, weight_ref = refs[:n], refs[n]
        q_ref, k_ref, v_ref, cos_ref, sin_ref = refs[n + 1 : n + 6]
        d_qkv = refs[n + 6 : n + 9]
        all_rows, d_attn, sems = refs[n + 9 :]
        copies = block_copies(block_refs, in_keys, rows, all_rows, sems)
        for copy in copies:
            copy.start()
        for copy in copies:
            copy.wait()
        project_into(all_rows, weight_ref, d_attn)

        for head in range(features // HD):
            cols = slice(head * HD, (head + 1) * HD)
            key, value = k_ref[:, cols], v_ref[:, cols]
            d_key, d_value = 0.0, 0.0
            for low in range(0, length, step):
                part = slice(low, low + step)
                query, grad = q_ref[part, cols], d_attn[part, cols]
                scores = lax.dot_general(key, query, NT, preferred_element_type=jnp.float32)
                top = jnp.max(scores, 0, keepdims=True)
                raised = jnp.exp2((scores - top) * EXP2_SCALE)
                probs = raised * (1.0 / jnp.sum(raised, 0, keepdims=True))
                d_value += jnp.dot(
                    probs.astype(jnp.bfloat16), grad, preferred_element_type=jnp.float32
                )
                d_probs = lax.dot_general(value, grad, NT, preferred_element_type=jnp.float32)
                delta = jnp.sum(probs * d_probs, 0, keepdims=True)
                d_scores = (probs * (d_probs - delta) * HD ** (-0.5)).astype(jnp.bfloat16)
                d_key += jnp.dot(d_scores, query, preferred_element_type=jnp.float32)
                d_query = lax.dot_general(
                    key, d_scores, TN, preferred_element_type=jnp.float32
                ).T
                d_qkv[0][part, cols] = turned(
                    d_query, cos_ref[part, :], -sin_ref[part, :]
                ).astype(jnp.bfloat16)
            d_qkv[1][:, cols] = turned(d_key, cos_ref[...], -sin_ref[...]).astype(jnp.bfloat16)
            d_qkv[2][:, cols] = d_value.astype(jnp.bfloat16)

    return call(
        kernel,
        [jax.ShapeDtypeStruct((length, features), jnp.bfloat16)] * 3,
        [blocks[key] for key in in_keys] + [weight] + list(qkv) + [cosine, sine],
        [ANY] * n + [VMEM] * 6,
        [
            pltpu.VMEM((length, width), jnp.bfloat16),
            pltpu.VMEM((length, features), jnp.bfloat16),
            pltpu.SemaphoreType.DMA((n,)),
        ],
        vmem=28,
        flops=HEADS_WEIGHT,
        name="backward_heads",
    )


def backward_terms(d_qkv, weights, rows, count, joined, after=()):
    length, features = d_qkv[0].shape
    width = weights[0].shape[0]
    shapes = term_outs(rows, width, count, joined)

    def kernel(*refs):
        grads, weight_refs = refs[:3], refs[3:6]
        own_ref, *outs = refs[6 + len(after) :]
        for low in range(0, width, CHUNK):
            total = 0.0
            for i in range(3):
                total += lax.dot_general(
                    grads[i][...],
                    weight_refs[i][low : low + CHUNK, :],
                    NT,
                    preferred_element_type=jnp.float32,
                )
            own_ref[:, low : low + CHUNK] = total[:rows]
            store_terms(total, low, outs, rows, count, joined)

    own, *terms = call(
        kernel,
        [jax.ShapeDtypeStruct((rows, width), jnp.float32)] + shapes,
        list(d_qkv) + list(weights) + list(after),
        [VMEM] * 6 + [ANY] * len(after),
        vmem=24,
        flops=TERMS_WEIGHT,
        name="backward_terms",
    )
    return own, terms


def forward_terms(qkv, act_in, weight, rows, count, joined, after=()):
    length, features = qkv[0].shape
    width = weight.shape[0]
    shapes = term_outs(rows, width, count, joined)
    step = min(length, 512)

    def kernel(*refs):
        q_ref, k_ref, v_ref, act_ref, weight_ref = refs[:5]
        own_ref, *outs = refs[5 + len(after) : -1]
        attn = refs[-1]
        for head in range(features // HD):
            cols = slice(head * HD, (head + 1) * HD)
            for low in range(0, length, step):
                part = slice(low, low + step)
                scores = lax.dot_general(
                    q_ref[part, cols], k_ref[:, cols], NT, preferred_element_type=jnp.float32
                )
                top = jnp.max(scores, 1, keepdims=True)
                raised = jnp.exp2((scores - top) * EXP2_SCALE)
                total = jnp.sum(raised, 1, keepdims=True)
                mixed = jnp.dot(
                    raised.astype(jnp.bfloat16), v_ref[:, cols], preferred_element_type=jnp.float32
                )
                attn[part, cols] = (mixed * (1.0 / total)).astype(jnp.bfloat16)

        for low in range(0, width, CHUNK):
            total = lax.dot_general(
                attn[...], weight_ref[low : low + CHUNK, :], NT, preferred_element_type=jnp.float32
            )
            own = total[:rows] + act_ref[:, low : low + CHUNK]
            own_ref[:, low : low + CHUNK] = own.astype(jnp.bfloat16)
            store_terms(total, low, outs, rows, count, joined)

    own, *terms = call(
        kernel,
        [jax.ShapeDtypeStruct((rows, width), jnp.bfloat16)] + shapes,
        list(qkv) + [act_in, weight, *after],
        [VMEM] * 5 + [ANY] * len(after),
        [pltpu.VMEM((length, features), jnp.bfloat16)],
        vmem=24,
        flops=FORWARD_WEIGHT,
        name="forward_terms",
    )
    return own, terms


def input_grad(own, pieces, saved, grad, inv, gain, bounds, after=()):
    keys = sorted(pieces)

    def kernel(own_ref, saved_ref, grad_ref, inv_ref, gain_ref, *refs):
        out_ref = refs[-1]
        for part, (low, high) in enumerate(bounds):
            total = own_ref[low:high, :]
            for ref, key in zip(refs, keys):
                if key[1] == part:
                    first = pieces[key][1]
                    total = total + ref[first : first + high - low, :].astype(jnp.float32)
            total = total * gain_ref[...]
            saved_rows = saved_ref[low:high, :]
            mean = jnp.mean(saved_rows * total, -1, keepdims=True)
            inv_rows = inv_ref[low:high, :]
            out_ref[low:high, :] = (
                grad_ref[low:high, :]
                + inv_rows * total
                - saved_rows * (inv_rows * inv_rows * inv_rows * mean)
            ).astype(jnp.bfloat16)

    return call(
        kernel,
        [jax.ShapeDtypeStruct(own.shape, jnp.bfloat16)],
        [own, saved, grad, inv, gain] + [pieces[key][0] for key in keys] + list(after),
        [VMEM] * (5 + len(keys)) + [ANY] * len(after),
        flops=INPUT_GRAD_WEIGHT,
        name="input_grad",
    )[0]


def added_pieces(total, pieces, refs, part, height):
    for ref, (key, (_, first)) in zip(refs, pieces.items()):
        if key[1] == part:
            total = total + ref[first : first + height, :].astype(jnp.float32)
    return total


def activation_sum(base, pieces, bounds):
    def kernel(base_ref, *refs):
        out_ref, mark_ref = refs[-2:]
        for part, (low, high) in enumerate(bounds):
            total = base_ref[low:high, :].astype(jnp.float32)
            out_ref[0, low:high, :] = added_pieces(total, pieces, refs, part, high - low)
        mark_ref[...] = jnp.zeros_like(mark_ref)

    return call(
        kernel,
        [
            jax.ShapeDtypeStruct((1, *base.shape), jnp.float32),
            jax.ShapeDtypeStruct((8, LANES), jnp.float32),
        ],
        [base] + [value for value, _ in pieces.values()],
        [VMEM] * (1 + len(pieces)),
        flops=LAST_SUM_WEIGHT,
        name="activation_sum",
    )


def widened(values, bounds, after=()):
    def kernel(in_any, *refs):
        out_ref, held, sems = refs[-3:]
        copies = [
            pltpu.make_async_copy(
                in_any.at[pl.ds(low, high - low), :],
                held.at[pl.ds(low, high - low), :],
                sems.at[i],
            )
            for i, (low, high) in enumerate(bounds)
        ]
        for copy in copies:
            copy.start()
        for copy, (low, high) in zip(copies, bounds):
            copy.wait()
            out_ref[0, low:high, :] = held[low:high, :].astype(jnp.float32)

    return call(
        kernel,
        [jax.ShapeDtypeStruct((1, *values.shape), jnp.float32)],
        [values, *after],
        [ANY] * (1 + len(after)),
        [
            pltpu.VMEM(values.shape, values.dtype),
            pltpu.SemaphoreType.DMA((len(bounds),)),
        ],
        name="widen",
    )[0]


def rope_tables(positions):
    half_dim = HD // 2
    inverse = 10000.0 ** (-(jnp.arange(half_dim).astype(jnp.float32) * 2.0 / HD))
    angles = positions.astype(jnp.float32)[:, None] * inverse[None, :]
    cosine, sine = jnp.cos(angles), jnp.sin(angles)
    return jnp.concatenate([cosine, cosine], 1), jnp.concatenate([-sine, sine], 1)


def shards(x_fwd, x_bwd, grad_in, gain, w_query, w_key, w_value, w_out):
    act_in, saved_in, grad = x_fwd[0], x_bwd[0], grad_in[0]
    rows = act_in.shape[0]
    count = lax.axis_size("seq")
    bounds = part_bounds(rows, count)
    own_query, own_key, own_value, own_out = w_query[0], w_key[0], w_value[0], w_out[0]

    block_of = lax.axis_index("seq") ^ jnp.arange(count)
    positions = (block_of[:, None] * rows + jnp.arange(rows)[None, :]).reshape(-1)
    cosine, sine = rope_tables(positions)

    whole = [(0, rows)]
    projections = (own_query, own_key, own_value)
    (normed_bwd,), inv_bwd = normed_rows(saved_in, gain, whole, vmem=62)
    grad_low = cast_rows(grad, [normed_bwd, cosine, sine])
    all_bwd = gather_first(normed_bwd, "saved")
    all_grad = gather_first(grad_low, "grad")
    normed_fwd, _ = normed_rows(act_in, gain, bounds)
    picked = picked_rows(second_hops(all_bwd, bounds), [grad_low])
    all_bwd = gather_rest(all_bwd, picked, bounds, "saved")
    n = len(bounds)
    handed_on = [(value, 0, value.shape[0]) for value in normed_fwd]
    picked = picked_rows(handed_on + second_hops(all_grad, bounds), picked)
    all_fwd = gather_parts({}, picked[:n], bounds, True, "input")
    all_grad = gather_rest(all_grad, picked[n:], bounds, "grad")

    qkv = project(all_bwd, projections, cosine, sine, rows)
    all_fwd = gather_parts(all_fwd, picked_rows(handed_on, qkv[:1]), bounds, False, "input")
    d_qkv = backward_heads(all_grad, qkv, own_out, cosine, sine, rows)
    picked = picked_rows(second_hops(all_fwd, bounds), d_qkv[:1])
    all_fwd = gather_rest(all_fwd, picked, bounds, "input")
    d_own, d_terms = backward_terms(d_qkv, projections, rows, count, True, picked)
    qkv = project(all_fwd, projections, cosine, sine, rows, FORWARD_WEIGHT)
    own, terms = forward_terms(qkv, act_in, own_out, rows, count, False)

    back = Scatter(d_terms, rows, True, across, "grad")
    front = Scatter(
        terms, rows, False, lambda value, bit: across_and_on(value, 1 << bit), "branch"
    )
    back.send_groups()
    front.send_groups()
    d_sums = back.send_sums([terms[0]])
    own = across_and_on(own, 0)
    sums = front.send_sums(d_sums, SUMS_WEIGHT)
    d_input = input_grad(
        d_own, back.final, saved_in, grad, inv_bwd, gain, bounds, [own, *sums]
    )
    act_next, mark = activation_sum(own, front.final, bounds)
    return (act_next, widened(passed_along(d_input, "pipe", -1), bounds, [mark]))


def solution(mesh):
    placed = (
        P("pipe", "seq", None),
        P("pipe", "seq", None),
        P("pipe", "seq", None),
        P("pipe", None),
        P("pipe", None, "seq"),
        P("pipe", None, "seq"),
        P("pipe", None, "seq"),
        P("pipe", None, "seq"),
    )
    return jax.shard_map(
        shards,
        mesh=mesh,
        in_specs=placed,
        out_specs=(P("pipe", "seq", None), P("pipe", "seq", None)),
        check_vma=False,
    )
```
